32 devices in a mesh: dp: 8 (over z, y), tensor: 4 (over x, core).
Axes of the slice: x: 2, y: 2, z: 4, core: 2. Of those that a mesh axis runs over, the one named last changes fastest.
Arguments:
- text_input: bfloat16 [16, 512, 768], P('dp', 'tensor'), may hold values from -6 to 6
- visual_input: bfloat16 [16, 512, 768], P('dp', 'tensor'), may hold values from -6 to 6
- text_boxes: int32 [16, 2, 512], P('dp'), may hold values from 0 to 999
- text_count: int32 [16], P('dp'), may hold values from 20 to 512, as said below
- text_prenorm: bfloat16 [768], replicated, may hold values from 0.5 to 1.5
- text_query: bfloat16 [768, 768], P(None, 'tensor'), may hold values from -0.21875 to 0.21875
- text_key: bfloat16 [768, 768], P(None, 'tensor'), may hold values from -0.21875 to 0.21875
- text_value: bfloat16 [768, 768], P(None, 'tensor'), may hold values from -0.21875 to 0.21875
- text_output: bfloat16 [768, 768], P('tensor'), may hold values from -0.625 to 0.625
- text_midnorm: bfloat16 [768], replicated, may hold values from 0.5 to 1.5
- text_expand: bfloat16 [768, 3072], P(None, 'tensor'), may hold values from -0.21875 to 0.21875
- text_shrink: bfloat16 [3072, 768], P('tensor'), may hold values from -0.21875 to 0.21875
- visual_prenorm: bfloat16 [768], replicated, may hold values from 0.5 to 1.5
- visual_query: bfloat16 [768, 768], P(None, 'tensor'), may hold values from -0.21875 to 0.21875
- visual_key: bfloat16 [768, 768], P(None, 'tensor'), may hold values from -0.21875 to 0.21875
- visual_value: bfloat16 [768, 768], P(None, 'tensor'), may hold values from -0.21875 to 0.21875
- visual_output: bfloat16 [768, 768], P('tensor'), may hold values from -0.625 to 0.625
- visual_midnorm: bfloat16 [768], replicated, may hold values from 0.5 to 1.5
- visual_expand: bfloat16 [768, 3072], P(None, 'tensor'), may hold values from -0.21875 to 0.21875
- visual_shrink: bfloat16 [3072, 768], P('tensor'), may hold values from -0.21875 to 0.21875
- slopes: float32 [12], P('tensor'), may hold values from 0.5 to 6
- text_cotangent: bfloat16 [16, 512, 768], P('dp', 'tensor'), may hold values from -6 to 6
- visual_cotangent: bfloat16 [16, 512, 768], P('dp', 'tensor'), may hold values from -6 to 6
Outputs:
- text_result: bfloat16 [16, 512, 768], P('dp', 'tensor')
- visual_result: bfloat16 [16, 512, 768], P('dp', 'tensor')
- text_input_grad: bfloat16 [16, 512, 768], P('dp', 'tensor')
- visual_input_grad: bfloat16 [16, 512, 768], P('dp', 'tensor')
- text_prenorm_grad: float32 [768], replicated
- text_query_grad: float32 [768, 768], P(None, 'tensor')
- text_key_grad: float32 [768, 768], P(None, 'tensor')
- text_value_grad: float32 [768, 768], P(None, 'tensor')
- text_output_grad: float32 [768, 768], P('tensor')
- text_midnorm_grad: float32 [768], replicated
- text_expand_grad: float32 [768, 3072], P(None, 'tensor')
- text_shrink_grad: float32 [3072, 768], P('tensor')
- visual_prenorm_grad: float32 [768], replicated
- visual_query_grad: float32 [768, 768], P(None, 'tensor')
- visual_key_grad: float32 [768, 768], P(None, 'tensor')
- visual_value_grad: float32 [768, 768], P(None, 'tensor')
- visual_output_grad: float32 [768, 768], P('tensor')
- visual_midnorm_grad: float32 [768], replicated
- visual_expand_grad: float32 [768, 3072], P(None, 'tensor')
- visual_shrink_grad: float32 [3072, 768], P('tensor')
- slopes_grad: float32 [12], P('tensor')
The draws below stay inside these ranges and needn't reach their ends.
Inputs may be any that keep to these rules, and one draw needn't show every extreme that they name: `text_count`: each aligned group of 2 pages holds one page with more than 384 text tokens, and one page of all holds exactly 512.
All inputs are finite; a program needn't handle non-finite values.
Results may differ from the reference program's by a relative error of at most 0.023.
Values may be sent and summed in bfloat16 or wider, within the bound.
No kernel may reach another device: no remote copies, remote signals or barrier semaphores. Data moves between devices by JAX's collectives and lax.ppermute only.
A program may use at most 128 MiB of HBM per device.

```python
import math
from functools import partial
import jax
import jax.numpy as jnp
from jax import lax

D = 768
HEADS = 12
HEAD_DIM = 64
FF = 3072
TEXT_LEN = 512
VIS_LEN = 512
GRID_W = 32
NBIN = 1000
MIN_TEXT = 20
PAGES_DEV = 2
PAGES = 16
TEXT_SHARD = 128


def draw_text_count(key, part):
    key = jax.random.fold_in(key, 11)
    first_key, second_key, third_key, fourth_key = jax.random.split(key, 4)
    counts = jax.random.randint(first_key, (PAGES,), MIN_TEXT, TEXT_LEN + 1)
    spanning = jax.random.randint(third_key, (PAGES,), TEXT_LEN - TEXT_SHARD + 1, TEXT_LEN + 1)
    chosen = jax.random.randint(second_key, (PAGES // PAGES_DEV,), 0, PAGES_DEV)
    position = jnp.arange(PAGES, dtype=jnp.int32) % PAGES_DEV
    group_pick = jnp.repeat(chosen, PAGES_DEV)
    result = jnp.where(position == group_pick, spanning, counts)
    fullest = jax.random.randint(fourth_key, (), 0, PAGES)
    result = jnp.where(jnp.arange(PAGES, dtype=jnp.int32) == fullest, TEXT_LEN, result)
    return result.astype(jnp.int32)


def set_ends(values, key, least, high):
    place = [jax.random.randint(jax.random.fold_in(key, axis), (), 0, length) for axis, length in enumerate(values.shape)]
    main_axis = values.shape.index(max(values.shape))
    next_to = place[:main_axis] + [(place[main_axis] + 1) % values.shape[main_axis]] + place[main_axis + 1:]
    return values.at[tuple(place)].set(least).at[tuple(next_to)].set(high)


def block_scale(stream_key, dims, cuts, least, high):
    loudness = 1.0
    for dim, blocks in cuts:
        steps = jax.random.uniform(jax.random.fold_in(jax.random.fold_in(stream_key, 6), dim), (blocks,), jnp.float32, least / len(cuts), high / len(cuts))
        loudness = loudness * jnp.repeat(jnp.exp(steps), dims[dim] // blocks).reshape((-1,) + (1,) * (len(dims) - 1 - dim))
    return loudness


def centred(own_key, dims, width, reach, cuts=(), held_as=jnp.bfloat16):
    factor_of = block_scale(own_key, dims, cuts, -0.22, 0.18) if cuts else 1.0
    entries = jax.random.normal(own_key, dims, jnp.float32) * width * factor_of
    return jnp.minimum(jnp.maximum(entries, -reach), reach).astype(held_as)


def setup_inputs(seed: int = 0) -> dict:
    key_list = jax.random.split(jax.random.key(seed), 24)
    text_input = centred(key_list[0], (PAGES, TEXT_LEN, D), 1.0, 6.0, ((0, 8), (1, 4)))
    visual_input = centred(key_list[1], (PAGES, VIS_LEN, D), 1.0, 6.0, ((0, 8), (1, 4)))
    text_boxes = set_ends(jax.random.randint(key_list[2], (PAGES, 2, TEXT_LEN), 0, NBIN), jax.random.fold_in(key_list[2], 1), 0, NBIN - 1).astype(jnp.int32)
    text_count = draw_text_count(jax.random.fold_in(key_list[23], 71), 0)
    text_prenorm = jnp.clip(1.0 + 0.1 * jax.random.normal(key_list[4], (D,), jnp.float32), 0.5, 1.5).astype(jnp.bfloat16)
    text_query = centred(key_list[5], (D, D), D ** -0.5, 0.21875, ((1, 4),))
    text_key = centred(key_list[6], (D, D), D ** -0.5, 0.21875, ((1, 4),))
    text_value = centred(key_list[7], (D, D), D ** -0.5, 0.21875, ((1, 4),))
    text_output = centred(key_list[8], (D, D), (D // 8) ** -0.5, 0.625, ((0, 4),))
    text_midnorm = jnp.clip(1.0 + 0.1 * jax.random.normal(key_list[9], (D,), jnp.float32), 0.5, 1.5).astype(jnp.bfloat16)
    text_expand = centred(key_list[10], (D, FF), D ** -0.5, 0.21875, ((1, 4),))
    text_shrink = centred(key_list[11], (FF, D), (FF // 4) ** -0.5, 0.21875, ((0, 4),))
    visual_prenorm = jnp.clip(1.0 + 0.1 * jax.random.normal(key_list[12], (D,), jnp.float32), 0.5, 1.5).astype(jnp.bfloat16)
    visual_query = centred(key_list[13], (D, D), D ** -0.5, 0.21875, ((1, 4),))
    visual_key = centred(key_list[14], (D, D), D ** -0.5, 0.21875, ((1, 4),))
    visual_value = centred(key_list[15], (D, D), D ** -0.5, 0.21875, ((1, 4),))
    visual_output = centred(key_list[16], (D, D), (D // 8) ** -0.5, 0.625, ((0, 4),))
    visual_midnorm = jnp.clip(1.0 + 0.1 * jax.random.normal(key_list[17], (D,), jnp.float32), 0.5, 1.5).astype(jnp.bfloat16)
    visual_expand = centred(key_list[18], (D, FF), D ** -0.5, 0.21875, ((1, 4),))
    visual_shrink = centred(key_list[19], (FF, D), (FF // 4) ** -0.5, 0.21875, ((0, 4),))
    slopes = jnp.clip(jnp.exp(math.log(6.0) - 2.4849066 * jax.random.uniform(key_list[20], (HEADS,), jnp.float32) ** block_scale(key_list[20], (HEADS,), ((0, 4),), -0.2, 0.2)), 0.5, 6.0)
    text_cotangent = centred(key_list[21], (PAGES, TEXT_LEN, D), 1.0, 6.0, ((0, 8), (1, 4)))
    visual_cotangent = centred(key_list[22], (PAGES, VIS_LEN, D), 1.0, 6.0, ((0, 8), (1, 4)))
    return {"text_input": text_input, "visual_input": visual_input, "text_boxes": text_boxes, "text_count": text_count, "text_prenorm": text_prenorm, "text_query": text_query, "text_key": text_key, "text_value": text_value, "text_output": text_output, "text_midnorm": text_midnorm, "text_expand": text_expand, "text_shrink": text_shrink, "visual_prenorm": visual_prenorm, "visual_query": visual_query, "visual_key": visual_key, "visual_value": visual_value, "visual_output": visual_output, "visual_midnorm": visual_midnorm, "visual_expand": visual_expand, "visual_shrink": visual_shrink, "slopes": slopes, "text_cotangent": text_cotangent, "visual_cotangent": visual_cotangent}


EPSILON = 1e-05
PRECISE = lax.Precision.HIGHEST

@jax.custom_vjp
def low(v):
    return lax.optimization_barrier(v.astype(jnp.bfloat16)).astype(jnp.float32)

@jax.custom_vjp
def low_back(v):
    return v

def low_keep(v):
    return (low(v), None)

def low_pass(kept, grad):
    return (grad,)

def back_keep(v):
    return (v, None)

def back_low(kept, grad):
    return (low(grad),)
low.defvjp(low_keep, low_pass)
low_back.defvjp(back_keep, back_low)

def layer_norm(values, gain_vector):
    center = values - lax.optimization_barrier(jnp.mean(values, axis=-1, keepdims=True))
    spread = lax.optimization_barrier(jnp.mean(center * center, axis=-1, keepdims=True))
    return center * lax.rsqrt(spread + EPSILON) * gain_vector

def gelu_tanh(values):
    return 0.5 * values * (1.0 + jnp.tanh(0.7978845608028654 * (values + 0.044715 * values * values * values)))

def pair_distance(coord_x, coord_y):
    delta_x = coord_x[..., :, None] - coord_x[..., None, :]
    delta_y = coord_y[..., :, None] - coord_y[..., None, :]
    return jnp.sqrt(delta_x * delta_x + delta_y * delta_y)

def grid_distance(token_count):
    places = jnp.arange(token_count, dtype=jnp.int32)
    coord_x = ((places % GRID_W).astype(jnp.float32) + 0.5) / GRID_W
    coord_y = ((places // GRID_W).astype(jnp.float32) + 0.5) / (token_count // GRID_W)
    return pair_distance(coord_x, coord_y)

def page_attention(page_items, slopes):
    queries, keys_all, values_all, distance, key_valid = page_items
    scores = jnp.einsum('qhd,khd->hqk', queries, keys_all, precision=PRECISE) * HEAD_DIM ** (-0.5)
    scores = low_back(scores - slopes[:, None, None] * distance[None])
    scores = jnp.where(key_valid[None, None, :], scores, -1e+30)
    highest = lax.optimization_barrier(jnp.max(scores, axis=-1, keepdims=True))
    exponent = jnp.exp(scores - highest)
    soft_weights = low(exponent / lax.optimization_barrier(jnp.sum(exponent, axis=-1, keepdims=True)))
    return jnp.einsum('hqk,khd->qhd', soft_weights, values_all, precision=PRECISE)

def stream_forward(inputs, weights, distance, key_valid, slopes):
    first_gain, query_weight, key_weight, value_weight, output_weight, second_gain, expand_weight, shrink_weight = weights
    page_total, token_total, model_width = inputs.shape
    first_normed = low(layer_norm(inputs, first_gain))

    def project(matrix):
        product = jnp.dot(first_normed, matrix, precision=PRECISE)
        return low(low_back(product)).reshape(page_total, token_total, HEADS, HEAD_DIM)
    page_step = jax.checkpoint(partial(page_attention, slopes=slopes))
    attended = lax.map(page_step, (project(query_weight), project(key_weight), project(value_weight), distance, key_valid))
    attended = low(low_back(attended.reshape(page_total, token_total, model_width)))
    middle = inputs + low_back(jnp.dot(attended, output_weight, precision=PRECISE))
    second_normed = low(layer_norm(middle, second_gain))
    hidden = low_back(jnp.dot(second_normed, expand_weight, precision=PRECISE))
    active = low(gelu_tanh(hidden))
    return middle + jnp.dot(active, shrink_weight, precision=PRECISE)

def reference(text_input, visual_input, text_boxes, text_count, text_prenorm, text_query, text_key, text_value, text_output, text_midnorm, text_expand, text_shrink, visual_prenorm, visual_query, visual_key, visual_value, visual_output, visual_midnorm, visual_expand, visual_shrink, slopes, text_cotangent, visual_cotangent):
    text_distance = pair_distance(text_boxes[:, 0].astype(jnp.float32) / NBIN, text_boxes[:, 1].astype(jnp.float32) / NBIN)
    text_valid = jnp.arange(TEXT_LEN, dtype=jnp.int32)[None, :] < text_count[:, None]
    visual_distance = jnp.broadcast_to(grid_distance(VIS_LEN)[None], (PAGES, VIS_LEN, VIS_LEN))
    visual_valid = jnp.full((PAGES, VIS_LEN), True)
    text_weights = tuple((matrix.astype(jnp.float32) for matrix in (text_prenorm, text_query, text_key, text_value, text_output, text_midnorm, text_expand, text_shrink)))
    visual_weights = tuple((matrix.astype(jnp.float32) for matrix in (visual_prenorm, visual_query, visual_key, visual_value, visual_output, visual_midnorm, visual_expand, visual_shrink)))

    def forward(text_stream, visual_stream, text_params, visual_params, slope_values):
        text_side = stream_forward(text_stream, text_params, text_distance, text_valid, slope_values)
        visual_side = stream_forward(visual_stream, visual_params, visual_distance, visual_valid, slope_values)
        return (text_side, visual_side)
    outputs, pullback = jax.vjp(forward, text_input.astype(jnp.float32), visual_input.astype(jnp.float32), text_weights, visual_weights, slopes)
    text_grad, visual_grad, text_wgrads, visual_wgrads, slope_grads = pullback((text_cotangent.astype(jnp.float32), visual_cotangent.astype(jnp.float32)))
    return (outputs[0].astype(jnp.bfloat16), outputs[1].astype(jnp.bfloat16), text_grad.astype(jnp.bfloat16), visual_grad.astype(jnp.bfloat16), text_wgrads[0], text_wgrads[1], text_wgrads[2], text_wgrads[3], text_wgrads[4], text_wgrads[5], text_wgrads[6], text_wgrads[7], visual_wgrads[0], visual_wgrads[1], visual_wgrads[2], visual_wgrads[3], visual_wgrads[4], visual_wgrads[5], visual_wgrads[6], visual_wgrads[7], slope_grads)
```

```python
import jax
import jax.numpy as jnp
from jax import lax
from jax.sharding import PartitionSpec as P

HEAD_DIM = 64
GRID_W = 32
NBIN = 1000
EPSILON = 1e-05
AXES = ("dp", "tensor")
ROWS = (((0,), (0,)), ((), ()))
COLS = (((1,), (1,)), ((), ()))
F32 = jnp.float32
BF16 = jnp.bfloat16


def layer_norm(values, gain):
    center = values - jnp.mean(values, axis=-1, keepdims=True)
    spread = jnp.mean(center * center, axis=-1, keepdims=True)
    return center * lax.rsqrt(spread + EPSILON) * gain


def gelu_tanh(values):
    return (
        0.5
        * values
        * (1.0 + jnp.tanh(0.7978845608028654 * (values + 0.044715 * values * values * values)))
    )


def matmul(a, b, dims=None):
    if dims is None:
        return jnp.dot(a, b, preferred_element_type=F32)
    return lax.dot_general(a, b, dims, preferred_element_type=F32)


class Links:
    def __init__(self, pairs):
        self.pairs = pairs
        self.high = pairs // 2
        self.ring_size = 4

    def table(self, move):
        out = []
        for dp in range(self.pairs):
            for tensor in range(4):
                hi, lo, x, c = move(dp // 2, dp % 2, tensor // 2, tensor % 2)
                out.append((dp * 4 + tensor, (hi * 2 + lo) * 4 + x * 2 + c))
        return out

    def send(self, value, move):
        return lax.ppermute(value, AXES, self.table(move))

    def core(self, value):
        return self.send(value, lambda hi, lo, x, c: (hi, lo, x, 1 - c))

    def across(self, value):
        return self.send(value, lambda hi, lo, x, c: (hi, lo, 1 - x, c))

    def stream(self, value):
        return self.send(value, lambda hi, lo, x, c: (hi, 1 - lo, x, c))

    def level(self, value, bit):
        return self.send(value, lambda hi, lo, x, c: (hi ^ bit, lo, x, c))

    def ring(self, value):
        n = self.ring_size
        return self.send(
            value, lambda hi, lo, x, c: (hi // n * n + (hi % n + 1) % n, lo, x, c)
        )

    def out_to_page(self, value, k):
        return self.send(value, lambda hi, lo, x, c: (hi, c ^ (k & 1), x ^ (k >> 1), lo))

    def back_to_rows(self, value, k):
        return self.send(value, lambda hi, lo, x, c: (hi, c, x ^ (k >> 1), lo ^ (k & 1)))


def add_low(a, b):
    return (a.astype(F32) + b.astype(F32)).astype(BF16)


def pick(flag, one, other):
    return jnp.where(flag, one, other)


def shards(
    text_input,
    visual_input,
    text_boxes,
    text_count,
    text_prenorm,
    text_query,
    text_key,
    text_value,
    text_output,
    text_midnorm,
    text_expand,
    text_shrink,
    visual_prenorm,
    visual_query,
    visual_key,
    visual_value,
    visual_output,
    visual_midnorm,
    visual_expand,
    visual_shrink,
    slopes,
    text_cotangent,
    visual_cotangent,
):
    dp_index = lax.axis_index("dp")
    tensor_index = lax.axis_index("tensor")
    hi, lo = dp_index // 2, dp_index % 2
    x, c = tensor_index // 2, tensor_index % 2
    links = Links(lax.axis_size("dp"))
    block = text_input.shape[1]
    tokens = text_boxes.shape[2]
    width = text_input.shape[2]
    heads_slot = slopes.shape[0]
    is_text = lo == 0
    place = 2 * x + lo

    def to_page(text_rows, visual_rows):
        both = jnp.stack([text_rows, visual_rows])
        parts = []
        for k in range(4):
            part = lax.dynamic_slice(
                both, (c ^ (k & 1), x ^ (k >> 1), 0, 0), (1, 1, block, width)
            ).reshape(block, width)
            parts.append(links.out_to_page(part, k))
        return jnp.concatenate(parts, axis=0)

    def to_rows(page):
        parts = [
            links.back_to_rows(page[k * block : (k + 1) * block], k) for k in range(4)
        ]
        even = [pick(c == 0, parts[2 * k2], parts[2 * k2 + 1]) for k2 in range(2)]
        odd = [pick(c == 0, parts[2 * k2 + 1], parts[2 * k2]) for k2 in range(2)]
        text = jnp.stack([pick(x == 0, even[0], even[1]), pick(x == 0, even[1], even[0])])
        visual = jnp.stack([pick(x == 0, odd[0], odd[1]), pick(x == 0, odd[1], odd[0])])
        return text, visual

    source = to_page(text_input, visual_input)
    info = jnp.concatenate(
        [
            lax.dynamic_slice(text_boxes, (x, 0, 0), (1, 2, tokens)).reshape(2, tokens),
            jnp.full((1, tokens), lax.dynamic_slice(text_count, (x,), (1,))[0], jnp.int32),
        ]
    )
    info = pick(c == lo, info, links.stream(info))
    count = pick(is_text, info[2, 0], tokens)
    order = jnp.arange(tokens, dtype=jnp.int32)
    absolute = (place ^ (order // block)) * block + order % block
    boxes = info[:2].reshape(2, 4, block)
    boxes = pick(place // 2 == 1, boxes[:, jnp.array([2, 3, 0, 1])], boxes)
    boxes = pick(place % 2 == 1, boxes[:, jnp.array([1, 0, 3, 2])], boxes)
    boxes = boxes.reshape(2, tokens).astype(F32) / NBIN
    coord_x = pick(is_text, boxes[0], ((absolute % GRID_W).astype(F32) + 0.5) / GRID_W)
    coord_y = pick(
        is_text, boxes[1], ((absolute // GRID_W).astype(F32) + 0.5) / (tokens // GRID_W)
    )
    delta_x = coord_x[:, None] - coord_x[None, :]
    delta_y = coord_y[:, None] - coord_y[None, :]
    distance = jnp.sqrt(delta_x * delta_x + delta_y * delta_y)
    valid = absolute < count

    half = hi % 2

    def slots(shard):
        rows = shard.shape[0] // 2
        mine = lax.dynamic_slice(shard, (half * rows, 0), (rows, shard.shape[1]))
        first = links.across(mine)
        second = links.level(first, 1)
        other = pick(
            half == 0,
            jnp.concatenate([first, second]),
            jnp.concatenate([second, first]),
        )
        return [shard, links.core(shard), other, links.core(other)]

    qkv_weights = slots(
        pick(
            is_text,
            jnp.concatenate([text_query, text_key, text_value], axis=1),
            jnp.concatenate([visual_query, visual_key, visual_value], axis=1),
        )
    )
    slopes_other = links.across(slopes)
    slope_slots = [slopes, links.core(slopes), slopes_other, links.core(slopes_other)]
    cotangent = to_page(text_cotangent, visual_cotangent)
    output_weights = slots(pick(is_text, text_output, visual_output))
    expand_weights = slots(pick(is_text, text_expand, visual_expand))
    shrink_weights = slots(pick(is_text, text_shrink, visual_shrink))
    gain_first = pick(is_text, text_prenorm, visual_prenorm).astype(F32)
    gain_second = pick(is_text, text_midnorm, visual_midnorm).astype(F32)

    def split(packed):
        parts = jnp.split(packed, 3, axis=1)
        return [part.reshape(tokens, heads_slot, HEAD_DIM) for part in parts]

    def scores_of(queries, keys_all, slope):
        scores = jnp.einsum("qhd,khd->hqk", queries, keys_all, preferred_element_type=F32)
        scores = scores * HEAD_DIM ** (-0.5) - slope[:, None, None] * distance[None]
        return jnp.where(valid[None, None, :], scores, -1e30)

    stream = source.astype(F32)
    first_normed = layer_norm(stream, gain_first).astype(BF16)
    heads = []
    attended = []
    branch = None
    for j in range(4):
        packed = matmul(first_normed, qkv_weights[j]).astype(BF16)
        queries, keys_all, values_all = split(packed)
        scores = scores_of(queries, keys_all, slope_slots[j])
        highest = jnp.max(scores, axis=-1, keepdims=True)
        exponent = jnp.exp(scores - highest)
        totals = jnp.sum(exponent, axis=-1, keepdims=True)
        soft_weights = (exponent / totals).astype(BF16)
        mixed = jnp.einsum("hqk,khd->qhd", soft_weights, values_all, preferred_element_type=F32)
        mixed = mixed.astype(BF16).reshape(tokens, -1)
        heads.append((queries, keys_all, values_all, highest + jnp.log(totals)))
        attended.append(mixed)
        part = matmul(mixed, output_weights[j])
        branch = part if branch is None else branch + part
    middle = stream + branch
    second_normed = layer_norm(middle, gain_second).astype(BF16)
    hidden = [matmul(second_normed, expand_weights[j]) for j in range(4)]
    active = [gelu_tanh(h).astype(BF16) for h in hidden]

    def reduced(parts):
        own = add_low(parts[0], links.core(parts[1]))
        far = add_low(parts[2], links.core(parts[3]))
        own = add_low(own, links.across(far))
        n = links.ring_size
        place_ring = hi % n
        rows = own.shape[0] // n

        def piece(index):
            return lax.dynamic_slice(own, (index % n * rows, 0), (rows, own.shape[1]))

        moving = piece(place_ring + n - 1)
        for k in range(n - 1):
            moving = add_low(links.ring(moving), piece(place_ring + n - 2 - k + n))
        groups = links.high // n
        if groups > 1:
            group_table = [
                [(g * n + r) * 2 + l for g in range(groups)] for r in range(n) for l in range(2)
            ]
            moving = lax.psum(moving, "dp", axis_index_groups=group_table)
        chunks = [moving]
        for k in range(n - 1):
            chunks.append(links.ring(chunks[-1]))
        theirs = [links.stream(chunk) for chunk in chunks]

        def laid(flag):
            cycle = [pick(flag, a, b) for a, b in zip(chunks, theirs, strict=True)][::-1]
            both = jnp.concatenate(cycle + cycle)
            start = (n - 1 - place_ring) * rows
            return lax.dynamic_slice(both, (start, 0), own.shape).astype(F32)

        return laid(is_text), laid(jnp.logical_not(is_text))

    shrink_grads = reduced([matmul(a, cotangent, ROWS).astype(BF16) for a in active])
    added = None
    hidden_grad = []
    second_grad = None
    for j in range(4):
        part = matmul(active[j], shrink_weights[j])
        added = part if added is None else added + part
        active_grad = matmul(cotangent, shrink_weights[j], COLS)
        back = jax.vjp(gelu_tanh, hidden[j])[1](active_grad)[0].astype(BF16)
        hidden_grad.append(back)
        part = matmul(back, expand_weights[j], COLS)
        second_grad = part if second_grad is None else second_grad + part
    result = (middle + added).astype(BF16)
    text_result, visual_result = to_rows(result)
    expand_grads = reduced([matmul(second_normed, h, ROWS).astype(BF16) for h in hidden_grad])
    middle_part, midnorm_grad = jax.vjp(layer_norm, middle, gain_second)[1](second_grad)
    middle_grad = cotangent.astype(F32) + middle_part
    branch_grad = middle_grad.astype(BF16)

    output_grads = reduced([matmul(a, branch_grad, ROWS).astype(BF16) for a in attended])
    qkv_grads = []
    slope_grads = []
    first_grad = None
    for j in range(4):
        queries, keys_all, values_all, log_total = heads[j]
        attended_grad = matmul(branch_grad, output_weights[j], COLS).astype(BF16)
        attended_grad = attended_grad.reshape(tokens, heads_slot, HEAD_DIM)
        probs = jnp.exp(scores_of(queries, keys_all, slope_slots[j]) - log_total)
        values_grad = jnp.einsum(
            "hqk,qhd->khd", probs.astype(BF16), attended_grad, preferred_element_type=F32
        )
        probs_grad = jnp.einsum(
            "qhd,khd->hqk", attended_grad, values_all, preferred_element_type=F32
        )
        scores_grad = probs * (probs_grad - jnp.sum(probs * probs_grad, axis=-1, keepdims=True))
        scores_grad = scores_grad.astype(BF16)
        slope_grads.append(-jnp.sum(scores_grad.astype(F32) * distance[None], axis=(1, 2)))
        queries_grad = jnp.einsum(
            "hqk,khd->qhd", scores_grad, keys_all, preferred_element_type=F32
        ) * HEAD_DIM ** (-0.5)
        keys_grad = jnp.einsum(
            "hqk,qhd->khd", scores_grad, queries, preferred_element_type=F32
        ) * HEAD_DIM ** (-0.5)
        packed = jnp.concatenate(
            [g.astype(BF16).reshape(tokens, -1) for g in (queries_grad, keys_grad, values_grad)],
            axis=1,
        )
        qkv_grads.append(matmul(first_normed, packed, ROWS).astype(BF16))
        part = matmul(packed, qkv_weights[j], COLS)
        first_grad = part if first_grad is None else first_grad + part
    qkv_text, qkv_visual = reduced(qkv_grads)
    stream_part, prenorm_grad = jax.vjp(layer_norm, stream, gain_first)[1](first_grad)
    text_input_grad, visual_input_grad = to_rows((middle_grad + stream_part).astype(BF16))

    slope_rel = jnp.stack(slope_grads)
    slope_rel = pick(c == 0, slope_rel, slope_rel[jnp.array([1, 0, 3, 2])])
    slope_abs = pick(x == 0, slope_rel, slope_rel[jnp.array([2, 3, 0, 1])]).reshape(-1)
    slope_row = jnp.zeros((width,), F32).at[: slope_abs.shape[0]].set(slope_abs)
    small = jnp.stack([prenorm_grad, midnorm_grad, slope_row])
    small = small + links.core(small)
    small = small + links.across(small)
    bit = 1
    while bit < links.high:
        small = small + links.level(small, bit)
        bit *= 2
    small_other = links.stream(small)
    text_small = pick(is_text, small, small_other)
    visual_small = pick(is_text, small_other, small)
    slope_sum = lax.dynamic_slice(
        (text_small + visual_small)[2], (tensor_index * heads_slot,), (heads_slot,)
    )
    text_qkv = jnp.split(qkv_text, 3, axis=1)
    visual_qkv = jnp.split(qkv_visual, 3, axis=1)
    return (
        text_result,
        visual_result,
        text_input_grad,
        visual_input_grad,
        text_small[0],
        *text_qkv,
        output_grads[0],
        text_small[1],
        expand_grads[0],
        shrink_grads[0],
        visual_small[0],
        *visual_qkv,
        output_grads[1],
        visual_small[1],
        expand_grads[1],
        shrink_grads[1],
        slope_sum,
    )


def solution(mesh):
    rows = P("dp", "tensor", None)
    split_out = P(None, "tensor")
    split_in = P("tensor", None)
    weights = (P(), split_out, split_out, split_out, split_in, P(), split_out, split_in)
    return jax.shard_map(
        shards,
        mesh=mesh,
        in_specs=(
            rows,
            rows,
            P("dp", None, None),
            P("dp"),
            *weights,
            *weights,
            P("tensor"),
            rows,
            rows,
        ),
        out_specs=(rows, rows, rows, rows, *weights, *weights, P("tensor")),
        check_vma=False,
    )
```

```python
import functools

import jax
import jax.numpy as jnp
from jax import lax
from jax.experimental import pallas as pl
from jax.experimental.pallas import tpu as pltpu
from jax.sharding import PartitionSpec as P

HEAD_DIM = 64
GRID_W = 32
NBIN = 1000
EPSILON = 1e-05
AXES = ("dp", "tensor")
ROWS = (((0,), (0,)), ((), ()))
COLS = (((1,), (1,)), ((), ()))
F32 = jnp.float32
BF16 = jnp.bfloat16
FAR = 1e30
GELU_A = 0.7978845608028654
GELU_B = 0.044715
SCALE = HEAD_DIM ** (-0.5)
FLAG_LO, FLAG_X, FLAG_C, FLAG_HALF, FLAG_RING, FLAG_PLACE, FLAG_TENSOR = range(7)
VMEM_LIMIT = 48 * 1024 * 1024
IN_VMEM = pl.BlockSpec(memory_space=pltpu.VMEM)
IN_SMEM = pl.BlockSpec(memory_space=pltpu.SMEM)
IN_ANY = pl.BlockSpec(memory_space=pl.ANY)


def dot(a, b, dims=None):
    if dims is None:
        return jnp.dot(a, b, preferred_element_type=F32)
    return lax.dot_general(a, b, dims, preferred_element_type=F32)


def kernel_call(body, outs, ins, scalars=0, scratch=(), after=(), far_ins=0, far_outs=0):
    count = len(ins)

    def whole(*refs):
        body(*refs[:count], *refs[count + len(after) :])

    near = [IN_SMEM] * scalars + [IN_VMEM] * (count - scalars - far_ins) + [IN_ANY] * far_ins
    return pl.pallas_call(
        whole,
        out_shape=outs,
        in_specs=near + [IN_ANY] * len(after),
        out_specs=[IN_VMEM] * (len(outs) - far_outs) + [IN_ANY] * far_outs,
        scratch_shapes=list(scratch),
        compiler_params=pltpu.CompilerParams(vmem_limit_bytes=VMEM_LIMIT),
        cost_estimate=pl.CostEstimate(flops=1000, bytes_accessed=1000, transcendentals=0),
    )(*ins, *after)


def shape(rows, cols, dtype):
    return jax.ShapeDtypeStruct((rows, cols), dtype)


def norm_parts(values):
    center = values - jnp.mean(values, axis=-1, keepdims=True)
    spread = jnp.mean(center * center, axis=-1, keepdims=True)
    scale = lax.rsqrt(spread + EPSILON)
    return center * scale, scale


def norm_back(normed, scale, gain, grad):
    inner = grad * gain
    mean_inner = jnp.mean(inner, axis=-1, keepdims=True)
    mean_both = jnp.mean(inner * normed, axis=-1, keepdims=True)
    return scale * (inner - mean_inner - normed * mean_both)


def first_norm_body(gains_ref, *refs):
    blocks, (source_ref, out_ref) = refs[:-2], refs[-2:]
    rows = blocks[0].shape[0]
    for k, block in enumerate(blocks):
        at = slice(k * rows, (k + 1) * rows)
        values = block[...]
        source_ref[at, :] = values
        normed, unused = norm_parts(values.astype(F32))
        out_ref[at, :] = (normed * gains_ref[0:1, :]).astype(BF16)


def first_norm(gains, blocks, after):
    rows, cols = blocks[0].shape
    outs = [shape(rows * len(blocks), cols, BF16)] * 2
    return kernel_call(first_norm_body, outs, [gains, *blocks], after=after)


def second_norm_body(source_ref, branch_ref, gains_ref, middle_ref, out_ref):
    middle = source_ref[...].astype(F32) + branch_ref[...]
    middle_ref[...] = middle
    normed, unused = norm_parts(middle)
    out_ref[...] = (normed * gains_ref[1:2, :]).astype(BF16)


def second_norm(source, branch, gains):
    outs = [shape(*source.shape, F32), shape(*source.shape, BF16)]
    return kernel_call(second_norm_body, outs, [source, branch, gains])


def second_back_body(
    middle_ref, gains_ref, grad_ref, cot_ref, added_ref, mid_ref, branch_ref, gain_out, result_ref
):
    middle = middle_ref[...]
    normed, scale = norm_parts(middle)
    grad = grad_ref[...]
    total = cot_ref[...].astype(F32) + norm_back(normed, scale, gains_ref[1:2, :], grad)
    mid_ref[...] = total
    branch_ref[...] = total.astype(BF16)
    gain_out[...] = jnp.sum(grad * normed, axis=0, keepdims=True)
    result_ref[...] = (middle + added_ref[...]).astype(BF16)


def second_back(middle, gains, grad, cotangent, added):
    rows, cols = middle.shape
    outs = [shape(rows, cols, F32), shape(rows, cols, BF16), shape(1, cols, F32)]
    outs.append(shape(rows, cols, BF16))
    return kernel_call(second_back_body, outs, [middle, gains, grad, cotangent, added])


def first_back_body(
    heads, flags, source_ref, gains_ref, grad_ref, mid_ref, midnorm_ref, result_ref, *refs
):
    slopes, blocks, small_ref = refs[:4], refs[4:8], refs[8]
    normed, scale = norm_parts(source_ref[...].astype(F32))
    grad = grad_ref[...]
    out = (mid_ref[...] + norm_back(normed, scale, gains_ref[0:1, :], grad)).astype(BF16)
    rows = result_ref.shape[0] // 4
    for k in range(4):
        blocks[k][:rows, :] = result_ref[k * rows : (k + 1) * rows, :]
        blocks[k][rows:, :] = out[k * rows : (k + 1) * rows, :]
    small_ref[...] = jnp.zeros_like(small_ref)
    small_ref[0:1, :] = jnp.sum(grad * normed, axis=0, keepdims=True)
    small_ref[1:2, :] = midnorm_ref[...]
    lane = lax.broadcasted_iota(jnp.int32, midnorm_ref.shape, 1)
    row = jnp.zeros(midnorm_ref.shape, F32)
    for j in range(4):
        sums = -jnp.sum(slopes[j][...], axis=1, keepdims=True)
        for h in range(heads):
            spot = (flags[FLAG_TENSOR] ^ j) * heads + h
            row = row + jnp.where(lane == spot, sums[h : h + 1, :], 0.0)
    small_ref[2:3, :] = row


def first_back(heads, flags, source, gains, grad, middle_grad, midnorm_grad, result, slope_rows):
    rows, cols = source.shape
    outs = [shape(rows // 2, cols, BF16)] * 4 + [shape(8, cols, F32)]
    ins = [flags, source, gains, grad, middle_grad, midnorm_grad, result, *slope_rows]
    out = kernel_call(functools.partial(first_back_body, heads), outs, ins, 1)
    return out[:4], out[4]


def each(flag, one, other):
    pl.when(flag == 0)(one)
    pl.when(flag != 0)(other)


def info_body(flags, counts, boxes_ref, info_ref):
    info_ref[...] = jnp.zeros_like(info_ref)
    info_ref[0:2, :] = boxes_ref[flags[FLAG_X]]
    info_ref[2:3, :] = jnp.full((1, info_ref.shape[1]), counts[flags[FLAG_X]], jnp.int32)


def page_info(flags, counts, boxes):
    outs = [shape(8, boxes.shape[2], jnp.int32)]
    return kernel_call(info_body, outs, [flags, counts, boxes], 2)[0]


def distance_body(flags, own_ref, theirs_ref, far_ref, info):
    tokens = far_ref.shape[0]
    block = tokens // 4
    mine = 1 - (flags[FLAG_LO] ^ flags[FLAG_C])
    text = 1 - flags[FLAG_LO]
    share = text.astype(F32)
    for k in range(4):
        at = slice(k * block, (k + 1) * block)
        shard = flags[FLAG_PLACE] ^ k
        there = pl.ds(pl.multiple_of(shard * block, block), block)
        boxes = own_ref[:, there] * mine + theirs_ref[:, there] * (1 - mine)
        index = lax.broadcasted_iota(jnp.int32, (1, block), 1) + shard * block
        column = (index & (GRID_W - 1)).astype(F32)
        line = (index >> (GRID_W.bit_length() - 1)).astype(F32)
        text_place = boxes[0:2, :].astype(F32) / NBIN
        coord_x = text_place[0:1, :] * share + (column + 0.5) / GRID_W * (1.0 - share)
        coord_y = text_place[1:2, :] * share + (line + 0.5) / (tokens // GRID_W) * (1.0 - share)
        count = boxes[2:3, :] * text + tokens * (1 - text)
        info[...] = jnp.zeros_like(info) if k == 0 else info[...]
        info[0:1, at] = coord_x
        info[1:2, at] = coord_y
        info[2:3, at] = jnp.where(index < count, 0.0, 1.0)
    turned = info[...].T
    delta_x = turned[:, 0:1] - info[0:1, :]
    delta_y = turned[:, 1:2] - info[1:2, :]
    distance = jnp.sqrt(delta_x * delta_x + delta_y * delta_y)
    far_ref[...] = jnp.where(turned[:, 2:3] > 0.5, FAR, distance)


def distances(flags, own, theirs):
    tokens = own.shape[1]
    scratch = [pltpu.VMEM((8, tokens), F32)]
    return kernel_call(
        distance_body, [shape(tokens, tokens, F32)], [flags, own, theirs], 1, scratch
    )[0]


def lay_body(groups, flags, *refs):
    size = len(groups)
    mine, theirs = refs[:4], refs[4:8]
    outs = (refs[8 : 8 + size], refs[8 + size : 8 + 2 * size])
    held, sems = refs[8 + 2 * size :][:size], refs[-1]
    rows = mine[0].shape[0]
    waits = []
    for r in range(4):
        spot = (flags[FLAG_RING] + 4 - r) & 3
        for side, chunk in enumerate((mine[r], theirs[r])):
            stream = flags[FLAG_LO] ^ side
            for g, (low, high, left, right) in enumerate(groups):
                slot = held[g].at[2 * r + side]
                sem = sems.at[g, 2 * r + side]
                slot[...] = chunk[:, left:right].astype(F32)
                for p in range(4):
                    first, last = max(p * rows, low), min((p + 1) * rows, high)
                    if first >= last:
                        continue
                    piece = slot.at[pl.ds(first - p * rows, last - first)]
                    place = pl.ds(first - low, last - first)

                    def move(out, piece=piece, place=place, sem=sem):
                        pltpu.make_async_copy(piece, out.at[place], sem).start()

                    for s in range(2):
                        pl.when((spot == p) & (stream == s))(
                            functools.partial(move, outs[s][g])
                        )
                    waits.append((spot == p, piece, outs[0][g].at[place], sem))
    for flag, piece, place, sem in waits:
        pl.when(flag)(pltpu.make_async_copy(piece, place, sem).wait)


def lay(flags, chunks, theirs, groups):
    rows = chunks[0].shape[0]
    outs = [shape(high - low, right - left, F32) for low, high, left, right in groups] * 2
    scratch = [pltpu.VMEM((8, rows, right - left), F32) for low, high, left, right in groups]
    scratch.append(pltpu.SemaphoreType.DMA((len(groups), 8)))
    out = kernel_call(
        functools.partial(lay_body, groups),
        outs,
        [flags, *chunks, *theirs],
        1,
        scratch,
        far_outs=len(outs),
    )
    return out[: len(groups)], out[len(groups) :]


def sort_body(flags, *refs):
    parts, outs, sems = refs[:4], refs[4:8], refs[8]
    rows = outs[0].shape[1]
    copies = []
    for k in range(4):
        stream = flags[FLAG_C] ^ (k & 1)
        page = flags[FLAG_X] ^ (k >> 1)
        for n in range(2):
            piece = parts[k].at[pl.ds(n * rows, rows)]
            sem = sems.at[2 * k + n]

            def move(out, piece=piece, page=page, sem=sem):
                pltpu.make_async_copy(piece, out.at[page], sem).start()

            each(
                stream,
                functools.partial(move, outs[2 * n]),
                functools.partial(move, outs[2 * n + 1]),
            )
            copies.append(pltpu.make_async_copy(piece, outs[0].at[0], sem))
    for copy in copies:
        copy.wait()


def sort_rows(flags, parts):
    rows, cols = parts[0].shape
    outs = [jax.ShapeDtypeStruct((2, rows // 2, cols), BF16)] * 4
    scratch = [pltpu.SemaphoreType.DMA((8,))]
    return kernel_call(sort_body, outs, [flags, *parts], 1, scratch, far_ins=4, far_outs=4)


def attention_ahead_body(heads, block, first, slope_ref, normed_ref, w_ref, far_ref, *refs):
    branch_ref = None if first else refs[0]
    qkv_ref, attended_ref, log_ref, out_ref = refs if first else refs[1:]
    tokens = normed_ref.shape[0]
    wide = heads * HEAD_DIM
    qkv_ref[...] = dot(normed_ref[...], w_ref[: 3 * wide, :], COLS).astype(BF16)
    for h in range(heads):
        col = slice(h * HEAD_DIM, (h + 1) * HEAD_DIM)
        keys = qkv_ref[:, wide + col.start : wide + col.stop]
        values_t = qkv_ref[:, 2 * wide + col.start : 2 * wide + col.stop].T
        slope = slope_ref[h]
        for b in range(tokens // block):
            rows = slice(b * block, (b + 1) * block)
            scores = dot(keys, qkv_ref[rows, col], COLS) * SCALE - slope * far_ref[:, rows]
            highest = jnp.max(scores, axis=0, keepdims=True)
            exponent = jnp.exp(scores - highest)
            totals = jnp.sum(exponent, axis=0, keepdims=True)
            soft_weights = (exponent * (1.0 / totals)).astype(BF16)
            log_ref[h : h + 1, rows] = highest + jnp.log(totals)
            attended_ref[rows, col] = dot(values_t, soft_weights).T.astype(BF16)
    part = dot(attended_ref[...], w_ref[3 * wide :, :])
    out_ref[...] = part if first else branch_ref[...] + part


def attention_ahead(slope, normed, w, far, branch, after=()):
    rows, cols = normed.shape
    heads = slope.shape[0]
    wide = heads * HEAD_DIM
    ins = [slope, normed, w, far] + ([] if branch is None else [branch])
    outs = [shape(rows, 3 * wide, BF16), shape(rows, wide, BF16), shape(8, rows, F32)]
    outs.append(shape(rows, cols, F32))
    body = functools.partial(attention_ahead_body, heads, min(256, rows), branch is None)
    return kernel_call(body, outs, ins, 1, after=after)


def attention_behind_body(
    heads, block, first, slope_ref, branch_ref, normed_ref, w_ref, qkv_ref, attended_ref, log_ref, far_ref, *refs
):
    grad_ref = None if first else refs[0]
    weight_grad, out_slope, out_ref, out_qkv, attended_grad, keys_sum, values_sum = (
        refs if first else refs[1:]
    )
    tokens = branch_ref.shape[0]
    wide = heads * HEAD_DIM
    attended_grad[...] = dot(branch_ref[...], w_ref[3 * wide :, :], COLS).astype(BF16)
    for h in range(heads):
        col = slice(h * HEAD_DIM, (h + 1) * HEAD_DIM)
        key_col = slice(wide + col.start, wide + col.stop)
        value_col = slice(2 * wide + col.start, 2 * wide + col.stop)
        keys = qkv_ref[:, key_col]
        values = qkv_ref[:, value_col]
        keys_t = keys.T
        slope = slope_ref[h]
        for b in range(tokens // block):
            rows = slice(b * block, (b + 1) * block)
            queries = qkv_ref[rows, col]
            grad = attended_grad[rows, col]
            far = far_ref[:, rows]
            scores = dot(keys, queries, COLS) * SCALE - slope * far
            probs = jnp.exp(scores - log_ref[h : h + 1, rows])
            values_part = dot(probs.astype(BF16), grad)
            probs_grad = dot(values, grad, COLS)
            mean = jnp.sum(probs * probs_grad, axis=0, keepdims=True)
            scores_grad = probs * (probs_grad - mean)
            out_slope[h : h + 1, rows] = jnp.sum(scores_grad * far, axis=0, keepdims=True)
            scores_grad = scores_grad.astype(BF16)
            keys_part = dot(scores_grad, queries)
            if b == 0:
                keys_sum[...] = keys_part
                values_sum[...] = values_part
            else:
                keys_sum[...] += keys_part
                values_sum[...] += values_part
            queries_grad = dot(keys_t, scores_grad) * SCALE
            out_qkv[rows, col] = queries_grad.T.astype(BF16)
        out_qkv[:, key_col] = (keys_sum[...] * SCALE).astype(BF16)
        out_qkv[:, value_col] = values_sum[...].astype(BF16)
    part = dot(out_qkv[...], w_ref[: 3 * wide, :])
    weight_grad[: 3 * wide, :] = dot(out_qkv[...], normed_ref[...], ROWS).astype(BF16)
    weight_grad[3 * wide :, :] = dot(attended_ref[...], branch_ref[...], ROWS).astype(BF16)
    out_ref[...] = part if first else grad_ref[...] + part


def attention_behind(slope, branch_grad, normed, w, kept, far, grad, after=()):
    rows, cols = branch_grad.shape
    heads = slope.shape[0]
    wide = heads * HEAD_DIM
    ins = [slope, branch_grad, normed, w, *kept, far] + ([] if grad is None else [grad])
    outs = [shape(4 * wide, cols, BF16), shape(8, rows, F32), shape(rows, cols, F32)]
    scratch = [pltpu.VMEM((rows, 3 * wide), BF16), pltpu.VMEM((rows, wide), BF16)] + [pltpu.VMEM((rows, HEAD_DIM), F32)] * 2
    body = functools.partial(attention_behind_body, heads, min(256, rows), grad is None)
    return kernel_call(body, outs, ins, 1, scratch, after)


def gelu_both(values):
    square = values * values
    bend = jnp.tanh(GELU_A * values * (1.0 + GELU_B * square))
    half = 0.5 * (1.0 + bend)
    slope = half + 0.5 * values * (1.0 - bend * bend) * (
        GELU_A + (3.0 * GELU_A * GELU_B) * square
    )
    return values * half, slope


def hidden_ahead_body(count, blocks, normed_ref, *refs):
    weights, refs = refs[:count], refs[count:]
    parts, outs, held = refs[:blocks], refs[blocks:-1], refs[-1]
    tokens, cols = normed_ref.shape
    for k in range(blocks):
        rows = parts[k].shape[0]
        outs[2 * count][k * rows : (k + 1) * rows, :] = parts[k][...]
    step = 32
    for j in range(count):
        held[...] = dot(normed_ref[...], weights[j][...])
        for b in range(tokens // step):
            rows = slice(b * step, (b + 1) * step)
            active, back = gelu_both(held[rows, :])
            outs[2 * j][rows, :] = active.astype(BF16)
            outs[2 * j + 1][rows, :] = back.astype(BF16)


def hidden_ahead(normed, weights, parts=(), after=()):
    rows, cols = normed.shape
    count, wide = len(weights), weights[0].shape[1]
    outs = [shape(rows, wide, BF16)] * (2 * count)
    if parts:
        outs.append(shape(rows, cols, BF16))
    body = functools.partial(hidden_ahead_body, count, len(parts))
    scratch = [pltpu.VMEM((rows, wide), F32)]
    out = kernel_call(body, outs, [normed, *weights, *parts], 0, scratch, after)
    return out[0 : 2 * count : 2], out[1 : 2 * count : 2], out[-1]


def hidden_behind_body(count, first, cot_ref, *refs):
    active, back, shrink, expand = (refs[count * i : count * (i + 1)] for i in range(4))
    refs = refs[4 * count :]
    before, refs = ((), refs) if first else (refs[:2], refs[2:])
    grads, (added_ref, out_ref) = refs[:count], refs[count:]
    cols = cot_ref.shape[1]
    for j in range(count):
        part = dot(active[j][...], shrink[j][...])
        if j == 0:
            added_ref[...] = part if first else before[0][...] + part
        else:
            added_ref[...] += part
        active_grad = dot(cot_ref[...], shrink[j][...], COLS)
        grads[j][...] = (active_grad * back[j][...].astype(F32)).astype(BF16)
        part = dot(grads[j][...], expand[j][...], COLS)
        if j == 0:
            out_ref[...] = part if first else before[1][...] + part
        else:
            out_ref[...] += part


def hidden_behind(cotangent, active, back, shrink, expand, before=(), after=()):
    rows, cols = cotangent.shape
    count, wide = len(active), active[0].shape[1]
    outs = [shape(rows, wide, BF16)] * count + [shape(rows, cols, F32)] * 2
    body = functools.partial(hidden_behind_body, count, not before)
    ins = [cotangent, *active, *back, *shrink, *expand, *before]
    out = kernel_call(body, outs, ins, after=after)
    return out[:count], out[count:]


class Links:
    def __init__(self, pairs):
        self.pairs = pairs
        self.high = pairs // 2
        self.ring_size = 4

    def send(self, value, move):
        table = []
        for dp in range(self.pairs):
            for tensor in range(4):
                hi, lo, x, c = move(dp // 2, dp % 2, tensor // 2, tensor % 2)
                table.append((dp * 4 + tensor, (hi * 2 + lo) * 4 + x * 2 + c))
        return lax.ppermute(value, AXES, table)

    def core(self, value):
        return self.send(value, lambda hi, lo, x, c: (hi, lo, x, 1 - c))

    def across(self, value):
        return self.send(value, lambda hi, lo, x, c: (hi, lo, 1 - x, c))

    def stream(self, value):
        return self.send(value, lambda hi, lo, x, c: (hi, 1 - lo, x, c))

    def level(self, value, bit):
        return self.send(value, lambda hi, lo, x, c: (hi ^ bit, lo, x, c))

    def ring(self, value):
        n = self.ring_size
        return self.send(
            value, lambda hi, lo, x, c: (hi // n * n + (hi % n + 1) % n, lo, x, c)
        )

    def out_to_page(self, value, k):
        return self.send(value, lambda hi, lo, x, c: (hi, c ^ (k & 1), x ^ (k >> 1), lo))

    def back_to_rows(self, value, k):
        return self.send(value, lambda hi, lo, x, c: (hi, c, x ^ (k >> 1), lo ^ (k & 1)))


def add_low(a, b):
    return (a.astype(F32) + b.astype(F32)).astype(BF16)


tie = lax.optimization_barrier


def shards(
    text_input,
    visual_input,
    text_boxes,
    text_count,
    text_prenorm,
    text_query,
    text_key,
    text_value,
    text_output,
    text_midnorm,
    text_expand,
    text_shrink,
    visual_prenorm,
    visual_query,
    visual_key,
    visual_value,
    visual_output,
    visual_midnorm,
    visual_expand,
    visual_shrink,
    slopes,
    text_cotangent,
    visual_cotangent,
):
    dp_index = lax.axis_index("dp")
    tensor_index = lax.axis_index("tensor")
    hi, lo = dp_index // 2, dp_index % 2
    x, c = tensor_index // 2, tensor_index % 2
    links = Links(lax.axis_size("dp"))
    heads_slot = slopes.shape[0]
    half = hi % 2
    n = links.ring_size
    flags = jnp.stack([lo, x, c, half, hi % n, 2 * x + lo, tensor_index]).astype(jnp.int32)
    gains = jnp.where(
        lo == 0,
        jnp.stack([text_prenorm, text_midnorm]),
        jnp.stack([visual_prenorm, visual_midnorm]),
    ).astype(F32)

    def joined(first, second):
        return jnp.concatenate(
            [jnp.where(half == 0, first, second), jnp.where(half == 0, second, first)]
        )

    def own_half(shard):
        rows = shard.shape[0] // 2
        return lax.dynamic_slice(shard, (half * rows, 0), (rows, shard.shape[1]))

    def page_blocks(text_rows, visual_rows):
        blocks = []
        for k in range(4):
            parts = [
                lax.dynamic_index_in_dim(rows, x ^ (k >> 1), 0, False)
                for rows in (text_rows, visual_rows)
            ]
            blocks.append(jnp.where((c ^ (k & 1)) == 0, *parts))
        return blocks

    def to_page(blocks):
        return [links.out_to_page(blocks[k], k) for k in (3, 2, 1, 0)][::-1]

    attn_own = jnp.where(
        lo == 0,
        jnp.concatenate([text_query.T, text_key.T, text_value.T, text_output]),
        jnp.concatenate([visual_query.T, visual_key.T, visual_value.T, visual_output]),
    )
    attn_first = links.across(own_half(attn_own))
    in_blocks = to_page(page_blocks(text_input, visual_input))
    info = page_info(flags, text_count, text_boxes)
    info_theirs = links.stream(info)
    slopes_other = links.across(slopes)
    slope_slots = [slopes, links.core(slopes), slopes_other, links.core(slopes_other)]
    attn_core = links.core(attn_own)
    expand_own = jnp.where(lo == 0, text_expand, visual_expand)
    shrink_own = jnp.where(lo == 0, text_shrink, visual_shrink)
    expand_half, shrink_half = own_half(expand_own), own_half(shrink_own)
    cot_blocks = page_blocks(text_cotangent, visual_cotangent)
    far = distances(flags, info, info_theirs)
    expand_half, attn_first = tie((expand_half, attn_first))
    expand_first = links.across(expand_half)
    attn_second = links.level(attn_first, 1)
    source, first_normed = first_norm(gains, in_blocks, [attn_first, far])

    saved = [None] * 4

    def ahead(j, weights, branch, after=()):
        qkv, attended, log_total, branch = attention_ahead(
            slope_slots[j], first_normed, weights, far, branch, after
        )
        saved[j] = (qkv, attended, log_total)
        return branch

    branch = ahead(0, attn_own, None)
    branch = ahead(1, attn_core, branch)
    attn_other = joined(attn_first, attn_second)
    attn_slots = [attn_own, attn_core, attn_other, links.core(attn_other)]
    expand_first, branch = tie((expand_first, branch))
    expand_second = links.level(expand_first, 1)
    *cot_blocks, expand_first = tie((*cot_blocks, expand_first))
    cot_blocks = to_page(cot_blocks)
    branch = ahead(2, attn_slots[2], branch, [expand_first])
    branch = ahead(3, attn_slots[3], branch)
    shrink_half, cot_blocks[3] = tie((shrink_half, cot_blocks[3]))
    shrink_first = links.across(shrink_half)
    middle, second_normed = second_norm(source, branch, gains)
    expand_slots = [expand_own, links.core(expand_own)]
    active, back, cotangent = hidden_ahead(second_normed, expand_slots, cot_blocks)
    expand_other = joined(expand_first, expand_second)
    expand_slots += [expand_other, links.core(expand_other)]
    active_far, back_far, unused = hidden_ahead(
        second_normed, expand_slots[2:], after=[active[0]]
    )
    active, back = [*active, *active_far], [*back, *back_far]

    def low(value):
        return value.astype(BF16)

    def add_low(a, b):
        return low(a.astype(F32) + b.astype(F32))

    def near_sum(parts):
        return add_low(parts[2], links.core(parts[0])), add_low(parts[3], links.core(parts[1]))

    order = (1, 3, 0, 2)

    def piece(own, index):
        rows = own.shape[0] // n
        return lax.dynamic_slice(own, (index % n * rows, 0), (rows, own.shape[1]))

    def ring_first(own):
        return links.ring(piece(own, hi % n + n - 1))

    def ring_next(own, moved, k):
        moving = add_low(moved, piece(own, hi % n + 2 * n - 2 - k))
        if k < n - 2:
            return links.ring(moving)
        groups = links.high // n
        if groups > 1:
            table = [
                [(g * n + r) * 2 + l for g in range(groups)] for r in range(n) for l in range(2)
            ]
            moving = lax.psum(moving, "dp", axis_index_groups=table)
        return moving

    def ring_sum(own):
        moved = ring_first(own)
        for k in range(n - 1):
            moved = ring_next(own, moved, k)
        return moved

    def spread(moving):
        chunks = [moving]
        for k in range(n - 1):
            chunks.append(links.ring(chunks[-1]))
        return chunks, [links.stream(chunk) for chunk in chunks]

    sh_near, sh_far = near_sum([low(dot(active[j], cotangent, ROWS)) for j in order])
    sh_theirs = links.across(sh_far)
    shrink_slots = [shrink_own, links.core(shrink_own)]
    grads, sums = hidden_behind(
        cotangent,
        active[:2],
        back[:2],
        shrink_slots,
        expand_slots[:2],
        after=[sh_far, shrink_first],
    )
    shrink_other = joined(shrink_first, links.level(shrink_first, 1))
    shrink_slots += [shrink_other, links.core(shrink_other)]
    grads_far, (added, second_grad) = hidden_behind(
        cotangent, active[2:], back[2:], shrink_slots[2:], expand_slots[2:], sums
    )
    hidden_grad = [*grads, *grads_far]
    middle_grad, branch_grad, midnorm_grad, result = second_back(
        middle, gains, second_grad, cotangent, added
    )
    ex_near, ex_far = near_sum([low(dot(second_normed, hidden_grad[j], ROWS)) for j in order])
    ex_theirs = links.across(ex_far)
    sh_sum_in = add_low(sh_near, sh_theirs)
    moved = ring_first(sh_sum_in)

    attn_parts = []
    slope_rows = [None] * 4
    first_grad = None
    for step, j in enumerate(order):
        part, slope_rows[j], first_grad = attention_behind(
            slope_slots[j],
            branch_grad,
            first_normed,
            attn_slots[j],
            saved[j],
            far,
            first_grad,
            [ex_far] if step == 0 else [moved],
        )
        attn_parts.append(part)
        if step < n - 1:
            moved, first_grad = tie((moved, first_grad))
            moved = ring_next(sh_sum_in, moved, step)
    sh_sum = moved
    at_near, at_far = near_sum(attn_parts)
    rows_out, small = first_back(
        heads_slot, flags, source, gains, first_grad, middle_grad, midnorm_grad, result, slope_rows
    )
    sh_chunks = spread(sh_sum)
    at_far, ex_theirs = tie((at_far, ex_theirs))
    at_theirs = links.across(at_far)
    ex_sum = ring_sum(add_low(ex_near, ex_theirs))
    small = small + links.core(small)
    small = small + links.across(small)
    bit = 1
    while bit < links.high:
        small = small + links.level(small, bit)
        bit *= 2
    small_other = links.stream(small)

    ex_chunks = spread(ex_sum)
    *rows_out, at_theirs = tie((*rows_out, at_theirs))
    rows_back = [links.back_to_rows(rows_out[k], k) for k in range(4)]
    at_sum = ring_sum(add_low(at_near, at_theirs))
    at_chunks = spread(at_sum)

    wide, width = text_output.shape
    whole = [(0, text_shrink.shape[0], 0, width)]
    quarters = [(i * wide, (i + 1) * wide, 0, width) for i in range(4)]
    (text_sh,), (visual_sh,) = lay(flags, *sh_chunks, whole)
    (text_ex,), (visual_ex,) = lay(flags, *ex_chunks, whole)
    text_at, visual_at = lay(flags, *at_chunks, quarters)
    text_result, visual_result, text_input_grad, visual_input_grad = sort_rows(flags, rows_back)

    text_small = jnp.where(lo == 0, small, small_other)
    visual_small = jnp.where(lo == 0, small_other, small)
    slope_sum = lax.dynamic_slice(
        (text_small + visual_small)[2], (tensor_index * heads_slot,), (heads_slot,)
    )
    return (
        text_result,
        visual_result,
        text_input_grad,
        visual_input_grad,
        text_small[0],
        *(grad.T for grad in text_at[:3]),
        text_at[3],
        text_small[1],
        text_ex,
        text_sh,
        visual_small[0],
        *(grad.T for grad in visual_at[:3]),
        visual_at[3],
        visual_small[1],
        visual_ex,
        visual_sh,
        slope_sum,
    )


def solution(mesh):
    rows = P("dp", "tensor", None)
    split_out = P(None, "tensor")
    split_in = P("tensor", None)
    weights = (P(), split_out, split_out, split_out, split_in, P(), split_out, split_in)
    return jax.shard_map(
        shards,
        mesh=mesh,
        in_specs=(
            rows,
            rows,
            P("dp", None, None),
            P("dp"),
            *weights,
            *weights,
            P("tensor"),
            rows,
            rows,
        ),
        out_specs=(rows, rows, rows, rows, *weights, *weights, P("tensor")),
        check_vma=False,
    )
```

```python
import functools

import jax
import jax.numpy as jnp
from jax import lax
from jax.experimental import pallas as pl
from jax.experimental.pallas import tpu as pltpu
from jax.sharding import PartitionSpec as P

HEAD_DIM = 64
GRID_W = 32
NBIN = 1000
EPSILON = 1e-05
AXES = ("dp", "tensor")
ROWS = (((0,), (0,)), ((), ()))
COLS = (((1,), (1,)), ((), ()))
F32 = jnp.float32
BF16 = jnp.bfloat16
FAR = 1e30
GELU_A = 0.7978845608028654
GELU_B = 0.044715
SCALE = HEAD_DIM ** (-0.5)
FLAG_LO, FLAG_X, FLAG_C, FLAG_HALF, FLAG_RING, FLAG_PLACE, FLAG_TENSOR = range(7)
VMEM_LIMIT = 16 * 1024 * 1024
IN_VMEM = pl.BlockSpec(memory_space=pltpu.VMEM)
IN_SMEM = pl.BlockSpec(memory_space=pltpu.SMEM)
IN_ANY = pl.BlockSpec(memory_space=pl.ANY)


def dot(a, b, dims=None):
    if dims is None:
        return jnp.dot(a, b, preferred_element_type=F32)
    return lax.dot_general(a, b, dims, preferred_element_type=F32)


def kernel_call(body, outs, ins, scalars=0, scratch=(), after=(), far_ins=0, far_outs=0):
    count = len(ins)

    def whole(*refs):
        body(*refs[:count], *refs[count + len(after) :])

    near = [IN_SMEM] * scalars + [IN_VMEM] * (count - scalars - far_ins) + [IN_ANY] * far_ins
    return pl.pallas_call(
        whole,
        out_shape=outs,
        in_specs=near + [IN_ANY] * len(after),
        out_specs=[IN_VMEM] * (len(outs) - far_outs) + [IN_ANY] * far_outs,
        scratch_shapes=list(scratch),
        compiler_params=pltpu.CompilerParams(vmem_limit_bytes=VMEM_LIMIT),
        cost_estimate=pl.CostEstimate(flops=10_000_000_000, bytes_accessed=1_000_000, transcendentals=0),
    )(*ins, *after)


def shape(rows, cols, dtype):
    return jax.ShapeDtypeStruct((rows, cols), dtype)


def norm_parts(values):
    center = values - jnp.mean(values, axis=-1, keepdims=True)
    spread = jnp.mean(center * center, axis=-1, keepdims=True)
    scale = lax.rsqrt(spread + EPSILON)
    return center * scale, scale


def norm_back(normed, scale, gain, grad):
    inner = grad * gain
    mean_inner = jnp.mean(inner, axis=-1, keepdims=True)
    mean_both = jnp.mean(inner * normed, axis=-1, keepdims=True)
    return scale * (inner - mean_inner - normed * mean_both)


def first_norm_body(gains_ref, *refs):
    blocks, (source_ref, out_ref) = refs[:-2], refs[-2:]
    rows = blocks[0].shape[0]
    for k, block in enumerate(blocks):
        at = slice(k * rows, (k + 1) * rows)
        values = block[...]
        source_ref[at, :] = values
        normed, unused = norm_parts(values.astype(F32))
        out_ref[at, :] = (normed * gains_ref[0:1, :]).astype(BF16)


def first_norm(gains, blocks, after):
    rows, cols = blocks[0].shape
    outs = [shape(rows * len(blocks), cols, BF16)] * 2
    return kernel_call(first_norm_body, outs, [gains, *blocks], after=after)


def second_norm_body(source_ref, branch_ref, gains_ref, middle_ref, out_ref):
    middle = source_ref[...].astype(F32) + branch_ref[...]
    middle_ref[...] = middle
    normed, unused = norm_parts(middle)
    out_ref[...] = (normed * gains_ref[1:2, :]).astype(BF16)


def second_norm(source, branch, gains, after):
    outs = [shape(*source.shape, F32), shape(*source.shape, BF16)]
    return kernel_call(second_norm_body, outs, [source, branch, gains], after=after)


def second_back_body(
    middle_ref, gains_ref, grad_ref, cot_ref, added_ref, mid_ref, branch_ref, gain_out, result_ref
):
    middle = middle_ref[...]
    normed, scale = norm_parts(middle)
    grad = grad_ref[...]
    total = cot_ref[...].astype(F32) + norm_back(normed, scale, gains_ref[1:2, :], grad)
    mid_ref[...] = total
    branch_ref[...] = total.astype(BF16)
    gain_out[...] = jnp.sum(grad * normed, axis=0, keepdims=True)
    result_ref[...] = (middle + added_ref[...]).astype(BF16)


def second_back(middle, gains, grad, cotangent, added, after):
    rows, cols = middle.shape
    outs = [shape(rows, cols, F32), shape(rows, cols, BF16), shape(1, cols, F32)]
    outs.append(shape(rows, cols, BF16))
    return kernel_call(second_back_body, outs, [middle, gains, grad, cotangent, added], after=after)


def first_back_body(
    heads, flags, source_ref, gains_ref, grad_ref, mid_ref, midnorm_ref, result_ref, *refs
):
    slopes, blocks, small_ref = refs[:4], refs[4:8], refs[8]
    normed, scale = norm_parts(source_ref[...].astype(F32))
    grad = grad_ref[...]
    out = (mid_ref[...] + norm_back(normed, scale, gains_ref[0:1, :], grad)).astype(BF16)
    rows = result_ref.shape[0] // 4
    for k in range(4):
        blocks[k][:rows, :] = result_ref[k * rows : (k + 1) * rows, :]
        blocks[k][rows:, :] = out[k * rows : (k + 1) * rows, :]
    small_ref[...] = jnp.zeros_like(small_ref)
    small_ref[0:1, :] = jnp.sum(grad * normed, axis=0, keepdims=True)
    small_ref[1:2, :] = midnorm_ref[...]
    lane = lax.broadcasted_iota(jnp.int32, midnorm_ref.shape, 1)
    row = jnp.zeros(midnorm_ref.shape, F32)
    for j in range(4):
        sums = -jnp.sum(slopes[j][...], axis=1, keepdims=True)
        for h in range(heads):
            spot = (flags[FLAG_TENSOR] ^ j) * heads + h
            row = row + jnp.where(lane == spot, sums[h : h + 1, :], 0.0)
    small_ref[2:3, :] = row


def first_back(heads, flags, source, gains, grad, middle_grad, midnorm_grad, result, slope_rows, after):
    rows, cols = source.shape
    outs = [shape(rows // 2, cols, BF16)] * 4 + [shape(8, cols, F32)]
    ins = [flags, source, gains, grad, middle_grad, midnorm_grad, result, *slope_rows]
    out = kernel_call(functools.partial(first_back_body, heads), outs, ins, 1, after=after)
    return out[:4], out[4]


def each(flag, one, other):
    pl.when(flag == 0)(one)
    pl.when(flag != 0)(other)


def info_body(flags, counts, boxes_ref, info_ref):
    info_ref[...] = jnp.zeros_like(info_ref)
    info_ref[0:2, :] = boxes_ref[flags[FLAG_X]]
    info_ref[2:3, :] = jnp.full((1, info_ref.shape[1]), counts[flags[FLAG_X]], jnp.int32)


def page_info(flags, counts, boxes):
    outs = [shape(8, boxes.shape[2], jnp.int32)]
    return kernel_call(info_body, outs, [flags, counts, boxes], 2)[0]


def distance_body(flags, own_ref, theirs_ref, far_ref, info):
    tokens = far_ref.shape[0]
    block = tokens // 4
    mine = 1 - (flags[FLAG_LO] ^ flags[FLAG_C])
    text = 1 - flags[FLAG_LO]
    share = text.astype(F32)
    for k in range(4):
        at = slice(k * block, (k + 1) * block)
        shard = flags[FLAG_PLACE] ^ k
        there = pl.ds(pl.multiple_of(shard * block, block), block)
        boxes = own_ref[:, there] * mine + theirs_ref[:, there] * (1 - mine)
        index = lax.broadcasted_iota(jnp.int32, (1, block), 1) + shard * block
        column = (index & (GRID_W - 1)).astype(F32)
        line = (index >> (GRID_W.bit_length() - 1)).astype(F32)
        text_place = boxes[0:2, :].astype(F32) / NBIN
        coord_x = text_place[0:1, :] * share + (column + 0.5) / GRID_W * (1.0 - share)
        coord_y = text_place[1:2, :] * share + (line + 0.5) / (tokens // GRID_W) * (1.0 - share)
        count = boxes[2:3, :] * text + tokens * (1 - text)
        info[...] = jnp.zeros_like(info) if k == 0 else info[...]
        info[0:1, at] = coord_x
        info[1:2, at] = coord_y
        info[2:3, at] = jnp.where(index < count, 0.0, 1.0)
    turned = info[...].T
    delta_x = turned[:, 0:1] - info[0:1, :]
    delta_y = turned[:, 1:2] - info[1:2, :]
    distance = jnp.sqrt(delta_x * delta_x + delta_y * delta_y)
    far_ref[...] = jnp.where(turned[:, 2:3] > 0.5, FAR, distance)


def distances(flags, own, theirs, after=()):
    tokens = own.shape[1]
    scratch = [pltpu.VMEM((8, tokens), F32)]
    return kernel_call(
        distance_body, [shape(tokens, tokens, F32)], [flags, own, theirs], 1, scratch, after
    )[0]


def near_body(flags, own_ref, own_core, far_ref, far_core, near_ref, *pieces):
    near_ref[...] = (own_ref[...].astype(F32) + own_core[...].astype(F32)).astype(BF16)
    rows = pieces[0].shape[0]
    for i, out_ref in enumerate(pieces):
        at = pl.ds(pl.multiple_of(((flags[FLAG_RING] + 3 - i) & 3) * rows, rows), rows)
        out_ref[...] = (far_ref[at, :].astype(F32) + far_core[at, :].astype(F32)).astype(BF16)


def near_sums(flags, parts, after):
    rows, cols = parts[0].shape
    outs = [shape(rows, cols, BF16)] + [shape(rows // 4, cols, BF16)] * 4
    out = kernel_call(near_body, outs, [flags, *parts], 1, after=after)
    return out[0], out[1:]


def piece_body(step, flags, near_ref, *refs):
    received, out_ref = refs[:-1], refs[-1]
    rows = out_ref.shape[0]
    at = pl.ds(pl.multiple_of(((flags[FLAG_RING] + 3 - step) & 3) * rows, rows), rows)
    total = near_ref[at, :].astype(F32)
    for value in received:
        total = total + value[...].astype(F32)
    out_ref[...] = total.astype(BF16)


def piece_sum(step, flags, near, received, after):
    rows, cols = received[0].shape
    body = functools.partial(piece_body, step)
    return kernel_call(body, [shape(rows, cols, BF16)], [flags, near, *received], 1, after=after)[0]


def lay_body(groups, flags, *refs):
    size = len(groups)
    chunks = (refs[:4], refs[4:8])
    outs = (refs[8 : 8 + size], refs[8 + size : 8 + 2 * size])
    held, sems = refs[8 + 2 * size :]
    rows = held.shape[1]
    waits = []
    for r in range(4):
        spot = (flags[FLAG_RING] + 4 - r) & 3
        for side in range(2):
            slot, sem = held.at[2 * r + side], sems.at[2 * r + side]
            slot[...] = chunks[side][r][...].astype(F32)
            stream = flags[FLAG_LO] ^ side
            for p in range(4):
                for g, (low, high) in enumerate(groups):
                    if not low <= p * rows < high:
                        continue
                    place = pl.ds(p * rows - low, rows)
                    for s in range(2):
                        copy = pltpu.make_async_copy(slot, outs[s][g].at[place], sem)
                        pl.when((spot == p) & (stream == s))(copy.start)
            waits.append(pltpu.make_async_copy(slot, outs[0][0].at[pl.ds(0, rows)], sem))
    for copy in waits:
        copy.wait()


def lay(flags, chunks, theirs, groups, after=()):
    rows, cols = chunks[0].shape
    outs = [shape(high - low, cols, F32) for low, high in groups] * 2
    scratch = [pltpu.VMEM((8, rows, cols), F32), pltpu.SemaphoreType.DMA((8,))]
    out = kernel_call(
        functools.partial(lay_body, groups),
        outs,
        [flags, *chunks, *theirs],
        1,
        scratch,
        after,
        far_outs=len(outs),
    )
    return out[: len(groups)], out[len(groups) :]


def sort_body(flags, *refs):
    parts, outs, sems = refs[:4], refs[4:8], refs[8]
    rows = outs[0].shape[1]
    copies = []
    for k in range(4):
        stream = flags[FLAG_C] ^ (k & 1)
        page = flags[FLAG_X] ^ (k >> 1)
        for n in range(2):
            piece = parts[k].at[pl.ds(n * rows, rows)]
            sem = sems.at[2 * k + n]

            def move(out, piece=piece, page=page, sem=sem):
                pltpu.make_async_copy(piece, out.at[page], sem).start()

            each(
                stream,
                functools.partial(move, outs[2 * n]),
                functools.partial(move, outs[2 * n + 1]),
            )
            copies.append(pltpu.make_async_copy(piece, outs[0].at[0], sem))
    for copy in copies:
        copy.wait()


def sort_rows(flags, parts, after=()):
    rows, cols = parts[0].shape
    outs = [jax.ShapeDtypeStruct((2, rows // 2, cols), BF16)] * 4
    scratch = [pltpu.SemaphoreType.DMA((8,))]
    return kernel_call(sort_body, outs, [flags, *parts], 1, scratch, after, far_ins=4, far_outs=4)


def attention_ahead_body(heads, block, first, slope_ref, normed_ref, w_ref, far_ref, *refs):
    branch_ref = None if first else refs[0]
    qkv_ref, attended_ref, log_ref, out_ref = refs if first else refs[1:]
    tokens = normed_ref.shape[0]
    wide = heads * HEAD_DIM
    qkv_ref[...] = dot(normed_ref[...], w_ref[: 3 * wide, :], COLS).astype(BF16)
    for h in range(heads):
        col = slice(h * HEAD_DIM, (h + 1) * HEAD_DIM)
        keys = qkv_ref[:, wide + col.start : wide + col.stop]
        values_t = qkv_ref[:, 2 * wide + col.start : 2 * wide + col.stop].T
        slope = slope_ref[h]
        for b in range(tokens // block):
            rows = slice(b * block, (b + 1) * block)
            scores = dot(keys, qkv_ref[rows, col], COLS) * SCALE - slope * far_ref[:, rows]
            highest = jnp.max(scores, axis=0, keepdims=True)
            exponent = jnp.exp(scores - highest)
            totals = jnp.sum(exponent, axis=0, keepdims=True)
            soft_weights = (exponent * (1.0 / totals)).astype(BF16)
            log_ref[h : h + 1, rows] = highest + jnp.log(totals)
            attended_ref[rows, col] = dot(values_t, soft_weights).T.astype(BF16)
    part = dot(attended_ref[...], w_ref[3 * wide :, :])
    out_ref[...] = part if first else branch_ref[...] + part


def attention_ahead(slope, normed, w, far, branch, after=()):
    rows, cols = normed.shape
    heads = slope.shape[0]
    wide = heads * HEAD_DIM
    ins = [slope, normed, w, far] + ([] if branch is None else [branch])
    outs = [shape(rows, 3 * wide, BF16), shape(rows, wide, BF16), shape(8, rows, F32)]
    outs.append(shape(rows, cols, F32))
    body = functools.partial(attention_ahead_body, heads, min(256, rows), branch is None)
    return kernel_call(body, outs, ins, 1, after=after)


def attention_behind_body(
    heads, block, first, slope_ref, branch_ref, normed_ref, w_ref, qkv_ref, attended_ref, log_ref, far_ref, *refs
):
    grad_ref = None if first else refs[0]
    weight_grad, out_slope, out_ref, out_qkv, attended_grad, keys_sum, values_sum = (
        refs if first else refs[1:]
    )
    tokens = branch_ref.shape[0]
    wide = heads * HEAD_DIM
    attended_grad[...] = dot(branch_ref[...], w_ref[3 * wide :, :], COLS).astype(BF16)
    for h in range(heads):
        col = slice(h * HEAD_DIM, (h + 1) * HEAD_DIM)
        key_col = slice(wide + col.start, wide + col.stop)
        value_col = slice(2 * wide + col.start, 2 * wide + col.stop)
        keys = qkv_ref[:, key_col]
        values = qkv_ref[:, value_col]
        keys_t = keys.T
        slope = slope_ref[h]
        for b in range(tokens // block):
            rows = slice(b * block, (b + 1) * block)
            queries = qkv_ref[rows, col]
            grad = attended_grad[rows, col]
            far = far_ref[:, rows]
            scores = dot(keys, queries, COLS) * SCALE - slope * far
            probs = jnp.exp(scores - log_ref[h : h + 1, rows])
            values_part = dot(probs.astype(BF16), grad)
            probs_grad = dot(values, grad, COLS)
            mean = jnp.sum(probs * probs_grad, axis=0, keepdims=True)
            scores_grad = probs * (probs_grad - mean)
            out_slope[h : h + 1, rows] = jnp.sum(scores_grad * far, axis=0, keepdims=True)
            scores_grad = scores_grad.astype(BF16)
            keys_part = dot(scores_grad, queries)
            if b == 0:
                keys_sum[...] = keys_part
                values_sum[...] = values_part
            else:
                keys_sum[...] += keys_part
                values_sum[...] += values_part
            queries_grad = dot(keys_t, scores_grad) * SCALE
            out_qkv[rows, col] = queries_grad.T.astype(BF16)
        out_qkv[:, key_col] = (keys_sum[...] * SCALE).astype(BF16)
        out_qkv[:, value_col] = values_sum[...].astype(BF16)
    part = dot(out_qkv[...], w_ref[: 3 * wide, :])
    weight_grad[: 3 * wide, :] = dot(out_qkv[...], normed_ref[...], ROWS).astype(BF16)
    weight_grad[3 * wide :, :] = dot(attended_ref[...], branch_ref[...], ROWS).astype(BF16)
    out_ref[...] = part if first else grad_ref[...] + part


def attention_behind(slope, branch_grad, normed, w, kept, far, grad, after=()):
    rows, cols = branch_grad.shape
    heads = slope.shape[0]
    wide = heads * HEAD_DIM
    ins = [slope, branch_grad, normed, w, *kept, far] + ([] if grad is None else [grad])
    outs = [shape(4 * wide, cols, BF16), shape(8, rows, F32), shape(rows, cols, F32)]
    scratch = [pltpu.VMEM((rows, 3 * wide), BF16), pltpu.VMEM((rows, wide), BF16)] + [pltpu.VMEM((rows, HEAD_DIM), F32)] * 2
    body = functools.partial(attention_behind_body, heads, min(256, rows), grad is None)
    return kernel_call(body, outs, ins, 1, scratch, after)


def gelu_both(values):
    square = values * values
    bend = jnp.tanh(GELU_A * values * (1.0 + GELU_B * square))
    half = 0.5 * (1.0 + bend)
    slope = half + 0.5 * values * (1.0 - bend * bend) * (
        GELU_A + (3.0 * GELU_A * GELU_B) * square
    )
    return values * half, slope


def hidden_ahead_body(count, blocks, normed_ref, *refs):
    weights, refs = refs[:count], refs[count:]
    parts, outs, held = refs[:blocks], refs[blocks:-1], refs[-1]
    tokens, cols = normed_ref.shape
    for k in range(blocks):
        rows = parts[k].shape[0]
        outs[2 * count][k * rows : (k + 1) * rows, :] = parts[k][...]
    step = 32
    for j in range(count):
        held[...] = dot(normed_ref[...], weights[j][...])
        for b in range(tokens // step):
            rows = slice(b * step, (b + 1) * step)
            active, back = gelu_both(held[rows, :])
            outs[2 * j][rows, :] = active.astype(BF16)
            outs[2 * j + 1][rows, :] = back.astype(BF16)


def hidden_ahead(normed, weights, parts=(), after=()):
    rows, cols = normed.shape
    count, wide = len(weights), weights[0].shape[1]
    outs = [shape(rows, wide, BF16)] * (2 * count)
    if parts:
        outs.append(shape(rows, cols, BF16))
    body = functools.partial(hidden_ahead_body, count, len(parts))
    scratch = [pltpu.VMEM((rows, wide), F32)]
    out = kernel_call(body, outs, [normed, *weights, *parts], 0, scratch, after)
    return out[0 : 2 * count : 2], out[1 : 2 * count : 2], out[-1]


def hidden_behind_body(count, first, cot_ref, *refs):
    active, back, shrink, expand = (refs[count * i : count * (i + 1)] for i in range(4))
    refs = refs[4 * count :]
    before, refs = ((), refs) if first else (refs[:2], refs[2:])
    grads, (added_ref, out_ref) = refs[:count], refs[count:]
    cols = cot_ref.shape[1]
    for j in range(count):
        part = dot(active[j][...], shrink[j][...])
        if j == 0:
            added_ref[...] = part if first else before[0][...] + part
        else:
            added_ref[...] += part
        active_grad = dot(cot_ref[...], shrink[j][...], COLS)
        grads[j][...] = (active_grad * back[j][...].astype(F32)).astype(BF16)
        part = dot(grads[j][...], expand[j][...], COLS)
        if j == 0:
            out_ref[...] = part if first else before[1][...] + part
        else:
            out_ref[...] += part


def hidden_behind(cotangent, active, back, shrink, expand, before=(), after=()):
    rows, cols = cotangent.shape
    count, wide = len(active), active[0].shape[1]
    outs = [shape(rows, wide, BF16)] * count + [shape(rows, cols, F32)] * 2
    body = functools.partial(hidden_behind_body, count, not before)
    ins = [cotangent, *active, *back, *shrink, *expand, *before]
    out = kernel_call(body, outs, ins, after=after)
    return out[:count], out[count:]


class Links:
    def __init__(self, pairs):
        self.pairs = pairs
        self.high = pairs // 2
        self.ring_size = 4

    def send(self, value, move):
        table = []
        for dp in range(self.pairs):
            for tensor in range(4):
                hi, lo, x, c = move(dp // 2, dp % 2, tensor // 2, tensor % 2)
                table.append((dp * 4 + tensor, (hi * 2 + lo) * 4 + x * 2 + c))
        return lax.ppermute(value, AXES, table)

    def core(self, value):
        return self.send(value, lambda hi, lo, x, c: (hi, lo, x, 1 - c))

    def across(self, value):
        return self.send(value, lambda hi, lo, x, c: (hi, lo, 1 - x, c))

    def stream(self, value):
        return self.send(value, lambda hi, lo, x, c: (hi, 1 - lo, x, c))

    def level(self, value, bit):
        return self.send(value, lambda hi, lo, x, c: (hi ^ bit, lo, x, c))

    def ring(self, value):
        n = self.ring_size
        return self.send(
            value, lambda hi, lo, x, c: (hi // n * n + (hi % n + 1) % n, lo, x, c)
        )

    def out_to_page(self, value, k):
        return self.send(value, lambda hi, lo, x, c: (hi, c ^ (k & 1), x ^ (k >> 1), lo))

    def back_to_rows(self, value, k):
        return self.send(value, lambda hi, lo, x, c: (hi, c, x ^ (k >> 1), lo ^ (k & 1)))


def add_low(a, b):
    return (a.astype(F32) + b.astype(F32)).astype(BF16)


class Clock:
    def __init__(self, start):
        self.now = start

    def passed(self, *values):
        *values, self.now = lax.optimization_barrier((*values, self.now))
        return values[0] if len(values) == 1 else values


def shards(
    text_input,
    visual_input,
    text_boxes,
    text_count,
    text_prenorm,
    text_query,
    text_key,
    text_value,
    text_output,
    text_midnorm,
    text_expand,
    text_shrink,
    visual_prenorm,
    visual_query,
    visual_key,
    visual_value,
    visual_output,
    visual_midnorm,
    visual_expand,
    visual_shrink,
    slopes,
    text_cotangent,
    visual_cotangent,
):
    dp_index = lax.axis_index("dp")
    tensor_index = lax.axis_index("tensor")
    hi, lo = dp_index // 2, dp_index % 2
    x, c = tensor_index // 2, tensor_index % 2
    links = Links(lax.axis_size("dp"))
    heads_slot = slopes.shape[0]
    half = hi % 2
    n = links.ring_size
    flags = jnp.stack([lo, x, c, half, hi % n, 2 * x + lo, tensor_index]).astype(jnp.int32)
    gains = jnp.where(
        lo == 0,
        jnp.stack([text_prenorm, text_midnorm]),
        jnp.stack([visual_prenorm, visual_midnorm]),
    ).astype(F32)

    def halves(shard):
        rows = shard.shape[0] // 4
        start = half * 2 * rows
        return [lax.dynamic_slice_in_dim(shard, start + i * rows, rows) for i in range(2)]

    def joined(first, second):
        low_rows = [jnp.where(half == 0, a, b) for a, b in zip(first, second, strict=True)]
        high_rows = [jnp.where(half == 0, b, a) for a, b in zip(first, second, strict=True)]
        return jnp.concatenate(low_rows + high_rows)

    def page_blocks(text_rows, visual_rows):
        blocks = []
        for k in range(4):
            parts = [
                lax.dynamic_index_in_dim(rows, x ^ (k >> 1), 0, False)
                for rows in (text_rows, visual_rows)
            ]
            blocks.append(jnp.where((c ^ (k & 1)) == 0, *parts))
        return blocks

    def to_page(blocks):
        return [links.out_to_page(blocks[k], k) for k in (3, 2, 1, 0)][::-1]

    def low(value):
        return value.astype(BF16)

    def add_low(a, b):
        return low(a.astype(F32) + b.astype(F32))

    clock = Clock(gains)
    passed = clock.passed

    in_blocks = to_page(page_blocks(text_input, visual_input))
    info = page_info(flags, text_count, text_boxes)
    info_theirs = links.stream(info)
    attn_own = jnp.where(
        lo == 0,
        jnp.concatenate([text_query.T, text_key.T, text_value.T, text_output]),
        jnp.concatenate([visual_query.T, visual_key.T, visual_value.T, visual_output]),
    )
    attn_half = halves(attn_own)
    attn_first = [links.across(attn_half[0])]
    slopes_other = links.across(slopes)
    attn_core = links.core(attn_own)
    slope_core = links.core(slopes)
    far = passed(distances(flags, info, info_theirs))
    slopes_other, slope_core = passed(slopes_other, slope_core)
    slope_last = links.core(slopes_other)
    in_blocks = passed(*in_blocks)
    attn_half[1] = passed(attn_half[1])
    attn_first.append(links.across(attn_half[1]))
    source, first_normed = first_norm(gains, in_blocks, [clock.now])
    first_normed, slope_last, attn_core = passed(first_normed, slope_last, attn_core)
    slope_slots = [slopes, slope_core, slopes_other, slope_last]

    saved = [None] * 4

    def ahead(j, weights, branch):
        qkv, attended, log_total, branch = attention_ahead(
            slope_slots[j], first_normed, weights, far, branch, [clock.now]
        )
        saved[j] = (qkv, attended, log_total)
        return passed(branch)

    expand_own = jnp.where(lo == 0, text_expand, visual_expand)
    expand_half = halves(expand_own)
    expand_half = passed(*expand_half)
    branch = ahead(0, attn_own, None)
    attn_first[0], expand_half[0] = passed(attn_first[0], expand_half[0])
    attn_second = [links.level(attn_first[0], 1)]
    expand_first = [links.across(expand_half[0])]
    expand_core = links.core(expand_own)
    branch = ahead(1, attn_core, branch)
    attn_first[1], expand_half[1] = passed(attn_first[1], expand_half[1])
    attn_second.append(links.level(attn_first[1], 1))
    expand_first.append(links.across(expand_half[1]))
    shrink_own = jnp.where(lo == 0, text_shrink, visual_shrink)
    shrink_half = halves(shrink_own)
    cot_blocks = page_blocks(text_cotangent, visual_cotangent)
    *shrink_half, expand_core = passed(*shrink_half, expand_core)
    cot_blocks = passed(*cot_blocks)
    attn_second = passed(*attn_second)
    attn_other = joined(attn_first, attn_second)
    expand_first[0], attn_other = passed(expand_first[0], attn_other)
    attn_last = links.core(attn_other)
    expand_second = [links.level(expand_first[0], 1)]
    cot_blocks = to_page(cot_blocks)
    shrink_core = links.core(shrink_own)
    branch = ahead(2, attn_other, branch)
    attn_last, shrink_core = passed(attn_last, shrink_core)
    expand_first[1] = passed(expand_first[1])
    expand_second.append(links.level(expand_first[1], 1))
    branch = ahead(3, attn_last, branch)
    attn_slots = [attn_own, attn_core, attn_other, attn_last]
    shrink_half = passed(*shrink_half)
    shrink_first = [links.across(shrink_half[0])]
    middle, second_normed = second_norm(source, branch, gains, [clock.now])
    second_normed = passed(second_normed)
    cot_blocks = passed(*cot_blocks)
    shrink_half[1] = passed(shrink_half[1])
    shrink_first.append(links.across(shrink_half[1]))
    active, back, cotangent = hidden_ahead(
        second_normed, [expand_own, expand_core], cot_blocks, [clock.now]
    )
    cotangent = passed(cotangent)
    expand_second = passed(*expand_second)
    expand_other = passed(joined(expand_first, expand_second))
    expand_last = links.core(expand_other)
    parts = {j: low(dot(active[j], cotangent, ROWS)) for j in (1, 0)}
    expand_last, parts[0], parts[1] = passed(expand_last, parts[0], parts[1])
    parts_core = {1: links.core(parts[1])}
    shrink_first[0] = passed(shrink_first[0])
    shrink_second = [links.level(shrink_first[0], 1)]
    active_far, back_far, unused = hidden_ahead(
        second_normed, [expand_other, expand_last], after=[clock.now]
    )
    active_far = passed(*active_far)
    active, back = [*active, *active_far], [*back, *back_far]
    expand_slots = [expand_own, expand_core, expand_other, expand_last]

    class Wave:
        def __init__(self, parts, parts_core):
            theirs = [parts_core[1], parts_core[3]]
            self.near, self.pieces = near_sums(
                flags, [parts[0], theirs[0], parts[2], theirs[1]], [clock.now]
            )
            self.near, *self.pieces = passed(self.near, *self.pieces)
            self.crossed = []
            self.moved = None
            self.chunks, self.others = [], []
            for i in range(2):
                self.cross()

        def cross(self):
            i = len(self.crossed)
            if i < 4:
                if i > 1:
                    self.pieces[i] = passed(self.pieces[i])
                self.crossed.append(links.across(self.pieces[i]))

        def add(self, step):
            received = [self.crossed[step]] + ([] if self.moved is None else [self.moved])
            total = piece_sum(step, flags, self.near, received, [clock.now])
            groups = links.high // n
            if step == n - 1 and groups > 1:
                table = [
                    [(g * n + r) * 2 + l for g in range(groups)]
                    for r in range(n)
                    for l in range(2)
                ]
                total = lax.psum(total, "dp", axis_index_groups=table)
            total = passed(total)
            self.moved = links.ring(total)
            self.cross()
            if step == n - 1:
                self.chunks.append(total)
                self.others.append(links.stream(total))

        def spread(self):
            chunk = passed(self.moved)
            self.chunks.append(chunk)
            if len(self.chunks) < n:
                self.moved = links.ring(chunk)
            self.others.append(links.stream(chunk))

        def settle(self, i):
            self.others[i] = passed(self.others[i])

    for j in (3, 2):
        parts[j] = low(dot(active[j], cotangent, ROWS))
    parts_core[3] = links.core(parts[3])
    parts[2] = passed(parts[2])
    shrink = Wave(parts, parts_core)
    shrink_first[1] = passed(shrink_first[1])
    shrink_second.append(links.level(shrink_first[1], 1))
    grads, sums = hidden_behind(
        cotangent,
        active[:2],
        back[:2],
        [shrink_own, shrink_core],
        expand_slots[:2],
        after=[clock.now],
    )
    grads = passed(*grads)
    parts = {j: low(dot(second_normed, grads[j], ROWS)) for j in (1, 0)}
    parts[0], parts[1] = passed(parts[0], parts[1])
    parts_core = {1: links.core(parts[1])}
    shrink.add(0)
    shrink_second = passed(*shrink_second)
    shrink_other = passed(joined(shrink_first, shrink_second))
    shrink_last = passed(links.core(shrink_other))
    grads_far, (added, second_grad) = hidden_behind(
        cotangent,
        active[2:],
        back[2:],
        [shrink_other, shrink_last],
        expand_slots[2:],
        sums,
        [clock.now],
    )
    grads_far = passed(*grads_far)
    shrink.add(1)
    for j in (3, 2):
        parts[j] = low(dot(second_normed, grads_far[j - 2], ROWS))
    parts_core[3] = links.core(parts[3])
    parts[2] = passed(parts[2])
    middle_grad, branch_grad, midnorm_grad, result = second_back(
        middle, gains, second_grad, cotangent, added, [clock.now]
    )
    branch_grad = passed(branch_grad)
    expand = Wave(parts, parts_core)

    parts, parts_core = [None] * 4, {}
    slope_rows = [None] * 4
    first_grad = None
    for step, j in enumerate((1, 3, 0, 2)):
        if step < 2:
            shrink.add(step + 2)
        else:
            expand.add(step - 2)
            shrink.spread()
            shrink.settle(step - 2)
        parts[j], slope_rows[j], first_grad = attention_behind(
            slope_slots[j],
            branch_grad,
            first_normed,
            attn_slots[j],
            saved[j],
            far,
            first_grad,
            [clock.now],
        )
        first_grad, parts[j] = passed(first_grad, parts[j])
        if step < 2:
            parts_core[j] = links.core(parts[j])
    attn = Wave(parts, parts_core)
    expand.add(2)
    shrink.spread()
    shrink.settle(2)
    rows_out, small = first_back(
        heads_slot,
        flags,
        source,
        gains,
        first_grad,
        middle_grad,
        midnorm_grad,
        result,
        slope_rows,
        [clock.now],
    )
    small, *rows_out = passed(small, *rows_out)
    small_moved = links.core(small)
    attn.add(0)
    expand.add(3)
    shrink.settle(3)
    small = passed(small + small_moved)
    small_moved = links.across(small)
    attn.add(1)
    expand.spread()
    expand.settle(0)
    (text_sh,), (visual_sh,) = lay(
        flags, shrink.chunks, shrink.others, [(0, text_shrink.shape[0])], [clock.now]
    )
    small = passed(small + small_moved)
    bit = 1
    while bit < links.high:
        small_moved = links.level(small, bit)
        if bit == 1:
            rows_out = passed(*rows_out)
            rows_back = [links.back_to_rows(rows_out[k], k) for k in range(4)]
            attn.add(2)
            expand.spread()
            expand.settle(1)
        elif bit == 2:
            attn.add(3)
            expand.spread()
            expand.settle(2)
        small = passed(small + small_moved)
        bit *= 2
    small_other = links.stream(small)
    rows_back = passed(*rows_back)
    text_result, visual_result, text_input_grad, visual_input_grad = sort_rows(
        flags, rows_back, [clock.now]
    )
    attn.spread()
    expand.settle(3)
    attn.settle(0)
    small_other = passed(small_other)
    (text_ex,), (visual_ex,) = lay(
        flags, expand.chunks, expand.others, [(0, text_expand.shape[0])], [clock.now]
    )
    attn.spread()
    attn.settle(1)
    attn.spread()
    attn.settle(2)
    wide = text_output.shape[0]
    text_at, visual_at = lay(
        flags, attn.chunks, attn.others, [(i * wide, (i + 1) * wide) for i in range(4)]
    )

    text_small = jnp.where(lo == 0, small, small_other)
    visual_small = jnp.where(lo == 0, small_other, small)
    slope_sum = lax.dynamic_slice(
        (text_small + visual_small)[2], (tensor_index * heads_slot,), (heads_slot,)
    )
    return (
        text_result,
        visual_result,
        text_input_grad,
        visual_input_grad,
        text_small[0],
        *(grad.T for grad in text_at[:3]),
        text_at[3],
        text_small[1],
        text_ex,
        text_sh,
        visual_small[0],
        *(grad.T for grad in visual_at[:3]),
        visual_at[3],
        visual_small[1],
        visual_ex,
        visual_sh,
        slope_sum,
    )


def solution(mesh):
    rows = P("dp", "tensor", None)
    split_out = P(None, "tensor")
    split_in = P("tensor", None)
    weights = (P(), split_out, split_out, split_out, split_in, P(), split_out, split_in)
    return jax.shard_map(
        shards,
        mesh=mesh,
        in_specs=(
            rows,
            rows,
            P("dp", None, None),
            P("dp"),
            *weights,
            *weights,
            P("tensor"),
            rows,
            rows,
        ),
        out_specs=(rows, rows, rows, rows, *weights, *weights, P("tensor")),
        check_vma=False,
    )
```

```python
import functools

import jax
import jax.numpy as jnp
from jax import lax
from jax.experimental import pallas as pl
from jax.experimental.pallas import tpu as pltpu
from jax.sharding import PartitionSpec as P

HEAD_DIM = 64
GRID_W = 32
NBIN = 1000
EPSILON = 1e-05
AXES = ("dp", "tensor")
ROWS = (((0,), (0,)), ((), ()))
COLS = (((1,), (1,)), ((), ()))
F32 = jnp.float32
BF16 = jnp.bfloat16
FAR = 1e30
GELU_A = 0.7978845608028654
GELU_B = 0.044715
SCALE = HEAD_DIM ** (-0.5)
FLAG_LO, FLAG_X, FLAG_C, FLAG_HALF, FLAG_RING, FLAG_PLACE, FLAG_TENSOR = range(7)
FLOPS_US = 1150000000
LIGHT, HEAVY = 0.001, 20
VMEM_LIMIT = 16 * 1024 * 1024
IN_VMEM = pl.BlockSpec(memory_space=pltpu.VMEM)
IN_SMEM = pl.BlockSpec(memory_space=pltpu.SMEM)
IN_ANY = pl.BlockSpec(memory_space=pl.ANY)
IN_HBM = pl.BlockSpec(memory_space=pltpu.HBM)


def dot(a, b, dims=None):
    if dims is None:
        return jnp.dot(a, b, preferred_element_type=F32)
    return lax.dot_general(a, b, dims, preferred_element_type=F32)


def kernel_call(body, outs, ins, scalars=0, scratch=(), after=(), far_ins=0, far_outs=0, hbm_outs=0, cost=LIGHT):
    count = len(ins)

    def whole(*refs):
        body(*refs[:count], *refs[count + len(after) :])

    near = [IN_SMEM] * scalars + [IN_VMEM] * (count - scalars - far_ins) + [IN_ANY] * far_ins
    return pl.pallas_call(
        whole,
        out_shape=outs,
        in_specs=near + [IN_ANY] * len(after),
        out_specs=[IN_HBM] * hbm_outs
        + [IN_VMEM] * (len(outs) - hbm_outs - far_outs)
        + [IN_ANY] * far_outs,
        scratch_shapes=list(scratch),
        compiler_params=pltpu.CompilerParams(vmem_limit_bytes=VMEM_LIMIT),
        cost_estimate=pl.CostEstimate(flops=int(FLOPS_US * cost), bytes_accessed=1000, transcendentals=0),
    )(*ins, *after)


def shape(rows, cols, dtype):
    return jax.ShapeDtypeStruct((rows, cols), dtype)


def norm_parts(values):
    center = values - jnp.mean(values, axis=-1, keepdims=True)
    spread = jnp.mean(center * center, axis=-1, keepdims=True)
    scale = lax.rsqrt(spread + EPSILON)
    return center * scale, scale


def norm_back(normed, scale, gain, grad):
    inner = grad * gain
    mean_inner = jnp.mean(inner, axis=-1, keepdims=True)
    mean_both = jnp.mean(inner * normed, axis=-1, keepdims=True)
    return scale * (inner - mean_inner - normed * mean_both)


def first_norm_body(gain_ref, *refs):
    blocks, (source_ref, out_ref) = refs[:-2], refs[-2:]
    rows = blocks[0].shape[0]
    for k, block in enumerate(blocks):
        at = slice(k * rows, (k + 1) * rows)
        values = block[...]
        source_ref[at, :] = values
        normed, unused = norm_parts(values.astype(F32))
        out_ref[at, :] = (normed * gain_ref[...]).astype(BF16)


def first_norm(gain, blocks, after):
    rows, cols = blocks[0].shape
    outs = [shape(rows * len(blocks), cols, BF16)] * 2
    return kernel_call(first_norm_body, outs, [gain, *blocks], after=after)


def second_norm_body(source_ref, branch_ref, gain_ref, middle_ref, out_ref):
    middle = source_ref[...].astype(F32) + branch_ref[...]
    middle_ref[...] = middle
    normed, unused = norm_parts(middle)
    out_ref[...] = (normed * gain_ref[...]).astype(BF16)


def second_norm(source, branch, gain, after):
    outs = [shape(*source.shape, F32), shape(*source.shape, BF16)]
    return kernel_call(second_norm_body, outs, [source, branch, gain], after=after)


def second_back_body(
    middle_ref, gain_ref, grad_ref, cot_ref, added_ref, mid_ref, branch_ref, gain_out, result_ref
):
    middle = middle_ref[...]
    normed, scale = norm_parts(middle)
    grad = grad_ref[...]
    total = cot_ref[...].astype(F32) + norm_back(normed, scale, gain_ref[...], grad)
    mid_ref[...] = total
    branch_ref[...] = total.astype(BF16)
    gain_out[...] = jnp.sum(grad * normed, axis=0, keepdims=True)
    result_ref[...] = (middle + added_ref[...]).astype(BF16)


def second_back(middle, gain, grad, cotangent, added, after):
    rows, cols = middle.shape
    outs = [shape(rows, cols, F32), shape(rows, cols, BF16), shape(1, cols, F32)]
    outs.append(shape(rows, cols, BF16))
    return kernel_call(second_back_body, outs, [middle, gain, grad, cotangent, added], after=after)


def first_back_body(
    heads, flags, source_ref, gain_ref, grad_ref, mid_ref, midnorm_ref, result_ref, *refs
):
    slopes, blocks, small_ref = refs[:4], refs[4:8], refs[8]
    normed, scale = norm_parts(source_ref[...].astype(F32))
    grad = grad_ref[...]
    out = (mid_ref[...] + norm_back(normed, scale, gain_ref[...], grad)).astype(BF16)
    rows = result_ref.shape[0] // 4
    for k in range(4):
        blocks[k][:rows, :] = result_ref[k * rows : (k + 1) * rows, :]
        blocks[k][rows:, :] = out[k * rows : (k + 1) * rows, :]
    small_ref[...] = jnp.zeros_like(small_ref)
    small_ref[0:1, :] = jnp.sum(grad * normed, axis=0, keepdims=True)
    small_ref[1:2, :] = midnorm_ref[...]
    lane = lax.broadcasted_iota(jnp.int32, midnorm_ref.shape, 1)
    row = jnp.zeros(midnorm_ref.shape, F32)
    for j in range(4):
        sums = -jnp.sum(slopes[j][...], axis=1, keepdims=True)
        for h in range(heads):
            spot = (flags[FLAG_TENSOR] ^ j) * heads + h
            row = row + jnp.where(lane == spot, sums[h : h + 1, :], 0.0)
    small_ref[2:3, :] = row


def first_back(heads, flags, source, gain, grad, middle_grad, midnorm_grad, result, slope_rows, after):
    rows, cols = source.shape
    outs = [shape(rows // 2, cols, BF16)] * 4 + [shape(8, cols, F32)]
    ins = [flags, source, gain, grad, middle_grad, midnorm_grad, result, *slope_rows]
    out = kernel_call(functools.partial(first_back_body, heads), outs, ins, 1, after=after)
    return out[:4], out[4]


def each(flag, one, other):
    pl.when(flag == 0)(one)
    pl.when(flag != 0)(other)


def info_body(flags, counts, boxes_ref, info_ref):
    info_ref[...] = jnp.zeros_like(info_ref)
    info_ref[0:2, :] = boxes_ref[flags[FLAG_X]]
    info_ref[2:3, :] = jnp.full((1, info_ref.shape[1]), counts[flags[FLAG_X]], jnp.int32)


def page_info(flags, counts, boxes):
    outs = [shape(8, boxes.shape[2], jnp.int32)]
    return kernel_call(info_body, outs, [flags, counts, boxes], 2)[0]


def distance_body(flags, own_ref, theirs_ref, far_ref, info):
    tokens = far_ref.shape[0]
    block = tokens // 4
    mine = 1 - (flags[FLAG_LO] ^ flags[FLAG_C])
    text = 1 - flags[FLAG_LO]
    share = text.astype(F32)
    for k in range(4):
        at = slice(k * block, (k + 1) * block)
        shard = flags[FLAG_PLACE] ^ k
        there = pl.ds(pl.multiple_of(shard * block, block), block)
        boxes = own_ref[:, there] * mine + theirs_ref[:, there] * (1 - mine)
        index = lax.broadcasted_iota(jnp.int32, (1, block), 1) + shard * block
        column = (index & (GRID_W - 1)).astype(F32)
        line = (index >> (GRID_W.bit_length() - 1)).astype(F32)
        text_place = boxes[0:2, :].astype(F32) / NBIN
        coord_x = text_place[0:1, :] * share + (column + 0.5) / GRID_W * (1.0 - share)
        coord_y = text_place[1:2, :] * share + (line + 0.5) / (tokens // GRID_W) * (1.0 - share)
        count = boxes[2:3, :] * text + tokens * (1 - text)
        info[...] = jnp.zeros_like(info) if k == 0 else info[...]
        info[0:1, at] = coord_x
        info[1:2, at] = coord_y
        info[2:3, at] = jnp.where(index < count, 0.0, 1.0)
    turned = info[...].T
    delta_x = turned[:, 0:1] - info[0:1, :]
    delta_y = turned[:, 1:2] - info[1:2, :]
    distance = jnp.sqrt(delta_x * delta_x + delta_y * delta_y)
    far_ref[...] = jnp.where(turned[:, 2:3] > 0.5, FAR, distance)


def distances(flags, own, theirs, after=()):
    tokens = own.shape[1]
    scratch = [pltpu.VMEM((8, tokens), F32)]
    return kernel_call(
        distance_body, [shape(tokens, tokens, F32)], [flags, own, theirs], 1, scratch, after
    )[0]


def both(a, b):
    return (a.astype(F32) + b.astype(F32)).astype(BF16)


def near_body(own_ref, core_ref, out_ref):
    out_ref[...] = both(own_ref[...], core_ref[...])


def near_sum(own, core, after):
    return kernel_call(near_body, [shape(*own.shape, BF16)], [own, core], after=after)[0]


def far_body(flags, own_ref, core_ref, *pieces):
    rows = own_ref.shape[0] // 4
    share = 4 // len(pieces)
    for i in range(4):
        at = pl.ds(pl.multiple_of(((flags[FLAG_RING] + 3 - i) & 3) * rows, rows), rows)
        place = slice(i % share * rows, (i % share + 1) * rows)
        pieces[i // share][place, :] = both(own_ref[at, :], core_ref[at, :])


def far_sum(flags, own, core, count, after):
    rows, cols = own.shape
    outs = [shape(rows // count, cols, BF16)] * count
    return kernel_call(far_body, outs, [flags, own, core], 1, after=after)


class Span:
    def __init__(self, array, start, rows):
        self.array, self.start, self.rows = array, start, rows


def turn_body(plan, flags, *refs):
    ins, outs = refs[: plan["ins"]], refs[plan["ins"] :]

    def rows_of(span):
        index, start, rows = span
        return ins[index][start : start + rows, :]

    for step, near, spans, places in plan["sums"]:
        rows = spans[0][2]
        at = pl.ds(pl.multiple_of(((flags[FLAG_RING] + 3 - step) & 3) * rows, rows), rows)
        total = ins[near][at, :].astype(F32)
        for span in spans:
            total = total + rows_of(span).astype(F32)
        total = total.astype(BF16)
        for out, start in places:
            outs[out][start : start + rows, :] = total
    for span, places in plan["moves"]:
        for out, start in places:
            outs[out][start : start + span[2], :] = rows_of(span)


def turn(flags, sums, moves, after):
    ins, index = [flags], {}

    def place_of(array):
        if id(array) not in index:
            index[id(array)] = len(ins) - 1
            ins.append(array)
        return index[id(array)]

    def static(span):
        return (place_of(span.array), span.start, span.rows)

    heights = {}

    def places_of(outs, rows):
        places = []
        for out in outs:
            places.append((out, heights.get(out, 0)))
            heights[out] = heights.get(out, 0) + rows
        return places

    plan = {"sums": [], "moves": []}
    for step, near, spans, outs in sums:
        rows = spans[0].rows
        plan["sums"].append(
            (step, place_of(near), [static(s) for s in spans], places_of(outs, rows))
        )
    for span, outs in moves:
        plan["moves"].append((static(span), places_of(outs, span.rows)))
    plan["ins"] = len(ins) - 1
    order = sorted(heights)
    number = {out: i for i, out in enumerate(order)}
    for kind in ("sums", "moves"):
        plan[kind] = [
            (*item[:-1], [(number[out], start) for out, start in item[-1]]) for item in plan[kind]
        ]
    cols = ins[1].shape[1]
    shapes = [shape(heights[out], cols, BF16) for out in order]
    body = functools.partial(turn_body, plan)
    made = kernel_call(body, shapes, ins, 1, after=after)
    places = [
        {order[out]: start for out, start in item[-1]} for kind in ("sums", "moves") for item in plan[kind]
    ]
    return dict(zip(order, made, strict=True)), places


def piece_sum(flags, step, near, spans, after):
    made, places = turn(flags, [(step, near, spans, [0])], [], after)
    return made[0]


def grad_body(left_ref, right_ref, out_ref):
    out_ref[...] = dot(left_ref[...], right_ref[...], ROWS).astype(BF16)


def grad_of(left, right, after, cost=LIGHT):
    outs = [shape(left.shape[1], right.shape[1], BF16)]
    return kernel_call(grad_body, outs, [left, right], after=after, cost=cost)[0]


def add_body(left_ref, right_ref, out_ref):
    out_ref[...] = left_ref[...] + right_ref[...]


def add(left, right, after):
    return kernel_call(add_body, [shape(*left.shape, left.dtype)], [left, right], after=after)[0]


def expand_output_body(normed_ref, hidden_ref, attended_ref, branch_ref, out_ref):
    rows = normed_ref.shape[1]
    out_ref[:rows, :] = dot(normed_ref[...], hidden_ref[...], ROWS).astype(BF16)
    out_ref[rows:, :] = dot(attended_ref[...], branch_ref[...], ROWS).astype(BF16)


def expand_output_grad(normed, hidden_grad, attended, branch_grad, after, cost=LIGHT):
    rows = normed.shape[1] + attended.shape[1]
    outs = [shape(rows, normed.shape[1], BF16)]
    ins = [normed, hidden_grad, attended, branch_grad]
    return kernel_call(expand_output_body, outs, ins, after=after, cost=cost)[0]


def join_body(flags, *refs):
    pieces, out_ref = refs[:-1], refs[-1]
    rows, count = pieces[0].shape[0], len(pieces) // 2
    for i, piece in enumerate(pieces):
        side = flags[FLAG_HALF] if i < count else 1 - flags[FLAG_HALF]
        start = (side * count + i % count) * rows
        out_ref[pl.ds(pl.multiple_of(start, rows), rows), :] = piece[...]


def join(flags, first, second, after):
    rows, cols = first[0].shape
    outs = [shape(2 * len(first) * rows, cols, BF16)]
    return kernel_call(join_body, outs, [flags, *first, *second], 1, after=after)[0]


def lay_body(groups, r, start, flags, *refs):
    size = len(groups)
    chunks, refs = refs[:2], refs[2:]
    outs, (held, sems) = refs[-2 * size - 2 : -2], refs[-2:]
    rows = held.shape[1]
    spot = (flags[FLAG_RING] + 4 - r) & 3
    waits = []
    for side in range(2):
        slot, sem = held.at[side], sems.at[side]
        slot[...] = chunks[side][start : start + rows, :].astype(F32)
        stream = flags[FLAG_LO] ^ side
        for p in range(4):
            for g, (low, high) in enumerate(groups):
                first, last = max(p * rows, low), min((p + 1) * rows, high)
                if first >= last:
                    continue
                piece = slot.at[pl.ds(first - p * rows, last - first)]
                place = pl.ds(first - low, last - first)
                for s in range(2):
                    copy = pltpu.make_async_copy(piece, outs[s * size + g].at[place], sem)
                    pl.when((spot == p) & (stream == s))(copy.start)
        waits.append(pltpu.make_async_copy(slot, outs[0].at[pl.ds(0, rows)], sem))
    for copy in waits:
        copy.wait()


def lay(flags, r, mine, theirs, start, rows, groups, laid, after):
    cols = mine.shape[1]
    outs = [shape(high - low, cols, F32) for low, high in groups] * 2
    ins = [flags, mine, theirs]
    first = len(ins)
    body = functools.partial(lay_body, groups, r, start)
    laid = [] if laid is None else list(laid)

    def whole(*refs):
        body(*refs[:first], *refs[first + len(laid) + len(after) :])

    return pl.pallas_call(
        whole,
        out_shape=outs,
        in_specs=[IN_SMEM, IN_VMEM, IN_VMEM] + [IN_ANY] * (len(laid) + len(after)),
        out_specs=[IN_ANY] * len(outs),
        scratch_shapes=[pltpu.VMEM((2, rows, cols), F32), pltpu.SemaphoreType.DMA((2,))],
        input_output_aliases={first + i: i for i in range(len(laid))},
        compiler_params=pltpu.CompilerParams(vmem_limit_bytes=VMEM_LIMIT),
        cost_estimate=pl.CostEstimate(
            flops=int(FLOPS_US * LIGHT), bytes_accessed=1000, transcendentals=0
        ),
    )(*ins, *laid, *after)


def sort_body(flags, *refs):
    parts, outs, sems = refs[:4], refs[4:8], refs[8]
    rows = outs[0].shape[1]
    copies = []
    for k in range(4):
        stream = flags[FLAG_C] ^ (k & 1)
        page = flags[FLAG_X] ^ (k >> 1)
        for n in range(2):
            piece = parts[k].at[pl.ds(n * rows, rows)]
            sem = sems.at[2 * k + n]

            def move(out, piece=piece, page=page, sem=sem):
                pltpu.make_async_copy(piece, out.at[page], sem).start()

            each(
                stream,
                functools.partial(move, outs[2 * n]),
                functools.partial(move, outs[2 * n + 1]),
            )
            copies.append(pltpu.make_async_copy(piece, outs[0].at[0], sem))
    for copy in copies:
        copy.wait()


def sort_rows(flags, parts, after=()):
    rows, cols = parts[0].shape
    outs = [jax.ShapeDtypeStruct((2, rows // 2, cols), BF16)] * 4
    scratch = [pltpu.SemaphoreType.DMA((8,))]
    return kernel_call(sort_body, outs, [flags, *parts], 1, scratch, after, far_ins=4, far_outs=4)


def slope_of(w_ref, wide, h):
    rows = [w_ref[4 * wide + i : 4 * wide + i + 1, h : h + 1].astype(F32) for i in range(3)]
    return rows[0] + rows[1] + rows[2]


def attention_ahead_body(heads, block, first, normed_ref, w_ref, far_ref, *refs):
    branch_ref, refs = (None, refs) if first else (refs[0], refs[1:])
    kept, (out_ref, *held, sems) = refs[:3], refs[3:]
    qkv_ref, attended_ref, log_ref = held
    keep = [pltpu.make_async_copy(held[i], kept[i], sems.at[i]) for i in range(3)]
    tokens = normed_ref.shape[0]
    wide = heads * HEAD_DIM
    qkv_ref[...] = dot(normed_ref[...], w_ref[: 3 * wide, :], COLS).astype(BF16)
    log_ref[...] = jnp.zeros_like(log_ref)
    keep[0].start()
    for h in range(heads):
        col = slice(h * HEAD_DIM, (h + 1) * HEAD_DIM)
        keys = qkv_ref[:, wide + col.start : wide + col.stop]
        values_t = qkv_ref[:, 2 * wide + col.start : 2 * wide + col.stop].T
        slope = slope_of(w_ref, wide, h)
        for b in range(tokens // block):
            rows = slice(b * block, (b + 1) * block)
            scores = dot(keys, qkv_ref[rows, col], COLS) * SCALE - slope * far_ref[:, rows]
            highest = jnp.max(scores, axis=0, keepdims=True)
            exponent = jnp.exp(scores - highest)
            totals = jnp.sum(exponent, axis=0, keepdims=True)
            soft_weights = (exponent * (1.0 / totals)).astype(BF16)
            log_ref[h : h + 1, rows] = highest + jnp.log(totals)
            attended_ref[rows, col] = dot(values_t, soft_weights).T.astype(BF16)
    keep[1].start()
    keep[2].start()
    part = dot(attended_ref[...], w_ref[3 * wide : 4 * wide, :])
    out_ref[...] = part if first else branch_ref[...] + part
    for copy in keep:
        copy.wait()


def attention_ahead(heads, normed, w, far, branch, after=(), cost=LIGHT):
    rows, cols = normed.shape
    wide = heads * HEAD_DIM
    ins = [normed, w, far] + ([] if branch is None else [branch])
    outs = [shape(rows, 3 * wide, BF16), shape(rows, wide, BF16), shape(8, rows, F32)]
    scratch = [pltpu.VMEM(out.shape, out.dtype) for out in outs] + [pltpu.SemaphoreType.DMA((3,))]
    outs.append(shape(rows, cols, F32))
    body = functools.partial(attention_ahead_body, heads, min(256, rows), branch is None)
    return kernel_call(body, outs, ins, 0, scratch, after, hbm_outs=3, cost=cost)


def attention_behind_body(
    heads, block, first, branch_ref, normed_ref, w_ref, qkv_ref, log_ref, far_ref, *refs
):
    grad_ref = None if first else refs[0]
    weight_grad, out_slope, out_ref, out_qkv, attended_grad, keys_sum, values_sum = (
        refs if first else refs[1:]
    )
    tokens = branch_ref.shape[0]
    wide = heads * HEAD_DIM
    attended_grad[...] = dot(branch_ref[...], w_ref[3 * wide : 4 * wide, :], COLS).astype(BF16)
    for h in range(heads):
        col = slice(h * HEAD_DIM, (h + 1) * HEAD_DIM)
        key_col = slice(wide + col.start, wide + col.stop)
        value_col = slice(2 * wide + col.start, 2 * wide + col.stop)
        keys = qkv_ref[:, key_col]
        values = qkv_ref[:, value_col]
        keys_t = keys.T
        slope = slope_of(w_ref, wide, h)
        for b in range(tokens // block):
            rows = slice(b * block, (b + 1) * block)
            queries = qkv_ref[rows, col]
            grad = attended_grad[rows, col]
            far = far_ref[:, rows]
            scores = dot(keys, queries, COLS) * SCALE - slope * far
            probs = jnp.exp(scores - log_ref[h : h + 1, rows])
            values_part = dot(probs.astype(BF16), grad)
            probs_grad = dot(values, grad, COLS)
            mean = jnp.sum(probs * probs_grad, axis=0, keepdims=True)
            scores_grad = probs * (probs_grad - mean)
            out_slope[h : h + 1, rows] = jnp.sum(scores_grad * far, axis=0, keepdims=True)
            scores_grad = scores_grad.astype(BF16)
            keys_part = dot(scores_grad, queries)
            if b == 0:
                keys_sum[...] = keys_part
                values_sum[...] = values_part
            else:
                keys_sum[...] += keys_part
                values_sum[...] += values_part
            queries_grad = dot(keys_t, scores_grad) * SCALE
            out_qkv[rows, col] = queries_grad.T.astype(BF16)
        out_qkv[:, key_col] = (keys_sum[...] * SCALE).astype(BF16)
        out_qkv[:, value_col] = values_sum[...].astype(BF16)
    part = dot(out_qkv[...], w_ref[: 3 * wide, :])
    weight_grad[...] = dot(out_qkv[...], normed_ref[...], ROWS).astype(BF16)
    out_ref[...] = part if first else grad_ref[...] + part


def attention_behind(heads, branch_grad, normed, w, kept, far, grad, after=(), cost=LIGHT):
    rows, cols = branch_grad.shape
    wide = heads * HEAD_DIM
    ins = [branch_grad, normed, w, *kept, far] + ([] if grad is None else [grad])
    outs = [shape(3 * wide, cols, BF16), shape(8, rows, F32), shape(rows, cols, F32)]
    scratch = [pltpu.VMEM((rows, 3 * wide), BF16), pltpu.VMEM((rows, wide), BF16)] + [pltpu.VMEM((rows, HEAD_DIM), F32)] * 2
    body = functools.partial(attention_behind_body, heads, min(256, rows), grad is None)
    return kernel_call(body, outs, ins, 0, scratch, after, cost=cost)


def gelu_both(values):
    square = values * values
    bend = jnp.tanh(GELU_A * values * (1.0 + GELU_B * square))
    half = 0.5 * (1.0 + bend)
    slope = half + 0.5 * values * (1.0 - bend * bend) * (
        GELU_A + (3.0 * GELU_A * GELU_B) * square
    )
    return values * half, slope


def hidden_ahead_body(count, blocks, normed_ref, *refs):
    weights, refs = refs[:count], refs[count:]
    parts, outs, held = refs[:blocks], refs[blocks:-1], refs[-1]
    tokens, cols = normed_ref.shape
    for k in range(blocks):
        rows = parts[k].shape[0]
        outs[2 * count][k * rows : (k + 1) * rows, :] = parts[k][...]
    step = 32
    for j in range(count):
        held[...] = dot(normed_ref[...], weights[j][...])
        for b in range(tokens // step):
            rows = slice(b * step, (b + 1) * step)
            active, back = gelu_both(held[rows, :])
            outs[2 * j][rows, :] = active.astype(BF16)
            outs[2 * j + 1][rows, :] = back.astype(BF16)


def hidden_ahead(normed, weights, parts=(), after=(), cost=LIGHT):
    rows, cols = normed.shape
    count, wide = len(weights), weights[0].shape[1]
    outs = [shape(rows, wide, BF16)] * (2 * count)
    if parts:
        outs.append(shape(rows, cols, BF16))
    body = functools.partial(hidden_ahead_body, count, len(parts))
    scratch = [pltpu.VMEM((rows, wide), F32)]
    out = kernel_call(body, outs, [normed, *weights, *parts], 0, scratch, after, cost=cost)
    return out[0 : 2 * count : 2], out[1 : 2 * count : 2], out[-1]


def hidden_behind_body(count, first, cot_ref, *refs):
    active, back, shrink, expand = (refs[count * i : count * (i + 1)] for i in range(4))
    refs = refs[4 * count :]
    before, refs = ((), refs) if first else (refs[:2], refs[2:])
    grads, (added_ref, out_ref) = refs[:count], refs[count:]
    cols = cot_ref.shape[1]
    for j in range(count):
        part = dot(active[j][...], shrink[j][...])
        if j == 0:
            added_ref[...] = part if first else before[0][...] + part
        else:
            added_ref[...] += part
        active_grad = dot(cot_ref[...], shrink[j][...], COLS)
        grads[j][...] = (active_grad * back[j][...].astype(F32)).astype(BF16)
        part = dot(grads[j][...], expand[j][...], COLS)
        if j == 0:
            out_ref[...] = part if first else before[1][...] + part
        else:
            out_ref[...] += part


def hidden_behind(cotangent, active, back, shrink, expand, before=(), after=(), cost=LIGHT):
    rows, cols = cotangent.shape
    count, wide = len(active), active[0].shape[1]
    outs = [shape(rows, wide, BF16)] * count + [shape(rows, cols, F32)] * 2
    body = functools.partial(hidden_behind_body, count, not before)
    ins = [cotangent, *active, *back, *shrink, *expand, *before]
    out = kernel_call(body, outs, ins, after=after, cost=cost)
    return out[:count], out[count:]


class Links:
    def __init__(self, pairs):
        self.pairs = pairs
        self.high = pairs // 2
        self.ring_size = 4

    def send(self, value, move):
        table = []
        for dp in range(self.pairs):
            for tensor in range(4):
                hi, lo, x, c = move(dp // 2, dp % 2, tensor // 2, tensor % 2)
                table.append((dp * 4 + tensor, (hi * 2 + lo) * 4 + x * 2 + c))
        return lax.ppermute(value, AXES, table)

    def core(self, value):
        return self.send(value, lambda hi, lo, x, c: (hi, lo, x, 1 - c))

    def across(self, value):
        return self.send(value, lambda hi, lo, x, c: (hi, lo, 1 - x, c))

    def stream(self, value):
        return self.send(value, lambda hi, lo, x, c: (hi, 1 - lo, x, c))

    def level(self, value, bit):
        return self.send(value, lambda hi, lo, x, c: (hi ^ bit, lo, x, c))

    def ring(self, value):
        n = self.ring_size
        return self.send(
            value, lambda hi, lo, x, c: (hi // n * n + (hi % n + 1) % n, lo, x, c)
        )

    def out_to_page(self, value, k):
        return self.send(value, lambda hi, lo, x, c: (hi, c ^ (k & 1), x ^ (k >> 1), lo))

    def back_to_rows(self, value, k):
        return self.send(value, lambda hi, lo, x, c: (hi, c, x ^ (k >> 1), lo ^ (k & 1)))


def add_low(a, b):
    return (a.astype(F32) + b.astype(F32)).astype(BF16)


class Clock:
    def __init__(self, start):
        self.now = start

    def passed(self, *values):
        values, self.now = lax.optimization_barrier((list(values), self.now))
        return values[0] if len(values) == 1 else values


def shards(
    text_input,
    visual_input,
    text_boxes,
    text_count,
    text_prenorm,
    text_query,
    text_key,
    text_value,
    text_output,
    text_midnorm,
    text_expand,
    text_shrink,
    visual_prenorm,
    visual_query,
    visual_key,
    visual_value,
    visual_output,
    visual_midnorm,
    visual_expand,
    visual_shrink,
    slopes,
    text_cotangent,
    visual_cotangent,
):
    dp_index = lax.axis_index("dp")
    tensor_index = lax.axis_index("tensor")
    hi, lo = dp_index // 2, dp_index % 2
    x, c = tensor_index // 2, tensor_index % 2
    links = Links(lax.axis_size("dp"))
    heads_slot = slopes.shape[0]
    half = hi % 2
    n = links.ring_size
    flags = jnp.stack([lo, x, c, half, hi % n, 2 * x + lo, tensor_index]).astype(jnp.int32)
    gain_first, gain_second = (
        jnp.where(lo == 0, text, visual).astype(F32)[None]
        for text, visual in ((text_prenorm, visual_prenorm), (text_midnorm, visual_midnorm))
    )

    def own_half(shard):
        rows = shard.shape[0] // 2
        return lax.dynamic_slice_in_dim(shard, half * rows, rows)

    def joined(first, second):
        return passed(join(flags, first, second, [clock.now]))

    def page_blocks(text_rows, visual_rows):
        blocks = []
        for k in range(4):
            parts = [
                lax.dynamic_index_in_dim(rows, x ^ (k >> 1), 0, False)
                for rows in (text_rows, visual_rows)
            ]
            blocks.append(jnp.where((c ^ (k & 1)) == 0, *parts))
        return blocks

    def to_page(blocks, chosen=(3, 2, 1, 0)):
        return [links.out_to_page(blocks[k], k) for k in chosen][::-1]

    def low(value):
        return value.astype(BF16)

    def add_low(a, b):
        return low(a.astype(F32) + b.astype(F32))

    clock = Clock(slopes)
    passed = clock.passed

    slope_parts = []
    rest = slopes
    for i in range(3):
        slope_parts.append(low(rest))
        rest = rest - slope_parts[i].astype(F32)
    tail = jnp.zeros((64, text_output.shape[1]), BF16)
    tail = tail.at[:3, :heads_slot].set(jnp.stack(slope_parts))
    attn_own = jnp.concatenate(
        [
            jnp.where(
                lo == 0,
                jnp.concatenate([text_query.T, text_key.T, text_value.T, text_output]),
                jnp.concatenate([visual_query.T, visual_key.T, visual_value.T, visual_output]),
            ),
            tail,
        ]
    )
    attn_half = own_half(attn_own)
    info = page_info(flags, text_count, text_boxes)
    attn_half, info = passed(attn_half, info)
    attn_first = links.across(attn_half)
    info_theirs = links.stream(info)
    text_rows, visual_rows = passed(text_input, visual_input)
    in_blocks = to_page(passed(page_blocks(text_rows, visual_rows)))
    info_theirs = passed(info_theirs)
    far = passed(distances(flags, info, info_theirs, [clock.now]))
    expand_own = jnp.where(lo == 0, text_expand, visual_expand)
    expand_half = own_half(expand_own)
    expand_half, gain_first, gain_second = passed(expand_half, gain_first, gain_second)
    attn_first = passed(attn_first)
    attn_second = links.level(attn_first, 1)
    in_blocks = passed(in_blocks)
    source, first_normed = passed(*first_norm(gain_first, in_blocks, [clock.now]))

    saved = [None] * 4

    def ahead(j, weights, branch, cost=LIGHT):
        qkv, attended, log_total, branch = attention_ahead(
            heads_slot, first_normed, weights, far, branch, [clock.now], cost
        )
        saved[j] = (qkv, log_total, attended)
        return passed(branch)

    cot_parts = page_blocks(text_cotangent, visual_cotangent)
    cot_parts, expand_half = passed(cot_parts, expand_half)
    expand_first = links.across(expand_half)
    attn_core = links.core(attn_own)
    cot_blocks = to_page(cot_parts, (1, 0))
    branch = ahead(0, attn_own, None, HEAVY)
    attn_core = passed(attn_core)
    branch = ahead(1, attn_core, branch)
    shrink_own = jnp.where(lo == 0, text_shrink, visual_shrink)
    shrink_half = own_half(shrink_own)
    shrink_half, cot_blocks = passed(shrink_half, cot_blocks)
    attn_second, expand_first = passed(attn_second, expand_first)
    attn_other = joined([attn_first], [attn_second])

    attn_last = links.core(attn_other)
    expand_second = links.level(expand_first, 1)
    cot_far = to_page(passed(cot_parts), (3, 2))
    expand_core = links.core(expand_own)
    branch = ahead(2, attn_other, branch, HEAVY)
    attn_last = passed(attn_last)
    branch = ahead(3, attn_last, branch)
    attn_slots = [attn_own, attn_core, attn_other, attn_last]
    expand_second, expand_core, cot_far = passed(expand_second, expand_core, cot_far)
    cot_blocks = [*cot_blocks, *cot_far]
    expand_other = joined([expand_first], [expand_second])

    expand_last = links.core(expand_other)
    shrink_first = links.across(shrink_half)
    shrink_core = links.core(shrink_own)
    middle, second_normed = second_norm(source, branch, gain_second, [clock.now])
    second_normed = passed(second_normed)
    active, back, cotangent = hidden_ahead(
        second_normed, [expand_own, expand_core], cot_blocks, [clock.now], HEAVY
    )
    active, cotangent = passed(active, cotangent)
    expand_last = passed(expand_last)
    active_far, back_far, unused = hidden_ahead(
        second_normed, [expand_other, expand_last], after=[clock.now]
    )
    active, back = [*active, *passed(active_far)], [*back, *back_far]
    expand_slots = [expand_own, expand_core, expand_other, expand_last]
    parts, parts_core = {}, {}
    for j in (3, 1):
        parts[j] = passed(grad_of(active[j], cotangent, [clock.now]))
    shrink_first, shrink_core = passed(shrink_first, shrink_core)
    for j in (3, 1):
        parts_core[j] = links.core(parts[j])
    shrink_second = links.level(shrink_first, 1)
    for j, cost in ((2, HEAVY), (0, LIGHT)):
        parts[j] = passed(grad_of(active[j], cotangent, [clock.now], cost))
    parts_core = passed(parts_core)

    class Wave:
        def __init__(self, count, rows, groups):
            self.count, self.rows, self.groups = count, rows, groups
            self.added = self.came = 0
            self.moved, self.laid = None, None
            self.crossed, self.chunks = [], []

        def far(self, own, core):
            self.pieces = passed(list(far_sum(flags, own, core, self.count, [clock.now])))

        def near(self, own, core):
            self.kept = passed(near_sum(own, core, [clock.now]))

        def lay(self, *chunks):
            for k in chunks:
                mine, theirs, start = self.chunks[k]
                self.laid = lay(
                    flags,
                    k,
                    mine,
                    theirs.array,
                    start,
                    self.rows,
                    self.groups,
                    self.laid,
                    [clock.now],
                )
                self.laid = passed(list(self.laid))

    wide, width = text_output.shape
    tall = text_shrink.shape[0]
    shrink = Wave(2, tall // 4, [(0, tall)])
    expand = Wave(4, (width + wide) // 4, [(0, width), (width, width + wide)])
    attn = Wave(4, 3 * wide // 4, [(i * wide, (i + 1) * wide) for i in range(3)])
    groups = links.high // n

    def cross(*waves):
        for wave in waves:
            piece = wave.pieces[len(wave.crossed)]
            wave.crossed.append(Span(links.across(piece), 0, piece.shape[0]))

    def spin(*waves, crossing=()):
        sums, moves, users = [], [], []
        for wave in waves:
            step = wave.added
            if step < n:
                piece = wave.crossed[step * wave.count // 4]
                share = 4 // wave.count
                spans = [Span(piece.array, piece.start + step % share * wave.rows, wave.rows)]
                spans += [] if wave.moved is None else [wave.moved]
                last = step == n - 1
                wave.added += 1
                if last and groups > 1:
                    table = [
                        [(g * n + r) * 2 + l for g in range(groups)]
                        for r in range(n)
                        for l in range(2)
                    ]
                    total = piece_sum(flags, step, wave.kept, spans, [clock.now])
                    total = passed(lax.psum(total, "dp", axis_index_groups=table))
                    moves.append((Span(total, 0, wave.rows), ["z", "y"]))
                    users.append(("move", wave))
                else:
                    sums.append((step, wave.kept, spans, ["z", "y"] if last else ["z"]))
                    users.append(("sum", wave))
            else:
                outs = ["z", "y"] if len(wave.chunks) < n - 1 else ["y"]
                moves.append((wave.moved, outs))
                users.append(("move", wave))
        for wave in crossing:
            moves.append((Span(wave.pieces[len(wave.crossed)], 0, wave.rows), ["x"]))
            users.append(("move", wave))
        users = [u for u in users if u[0] == "sum"] + [u for u in users if u[0] == "move"]
        made, places = turn(flags, sums, moves, [clock.now])
        names = sorted(made)
        made = dict(zip(names, passed([made[name] for name in names]), strict=True))
        sent = {}
        if "z" in made:
            sent["z"] = links.ring(made["z"])
        if "y" in made:
            sent["y"] = links.stream(made["y"])
        if "x" in made:
            sent["x"] = links.across(made["x"])
        for (kind, wave), place in zip(users, places, strict=True):
            if "x" in place:
                wave.crossed.append(Span(sent["x"], place["x"], wave.rows))
            if "z" in place:
                wave.moved = Span(sent["z"], place["z"], wave.rows)
            if "y" in place:
                wave.chunks.append(
                    [made["y"], Span(sent["y"], place["y"], wave.rows), place["y"]]
                )

    def settle(spans):
        arrays = {id(s.array): s.array for s in spans}
        keys = list(arrays)
        fresh = dict(zip(keys, passed([arrays[k] for k in keys], [])[0], strict=True))
        for s in {id(s): s for s in spans}.values():
            s.array = fresh[id(s.array)]

    def arrive(*waves):
        spans = []
        for wave in waves:
            spans += wave.crossed + ([] if wave.moved is None else [wave.moved])
        settle(spans)

    def landed(wave, *chunks):
        settle([wave.chunks[k][1] for k in chunks])
        wave.lay(*chunks)

    shrink.far(parts[2], parts_core[3])
    shrink.near(parts[0], parts_core[1])
    cross(shrink)
    grads, sums = hidden_behind(
        cotangent,
        active[:2],
        back[:2],
        [shrink_own, shrink_core],
        expand_slots[:2],
        after=[clock.now],
        cost=HEAVY,
    )
    grads, sums = passed(grads, list(sums))
    shrink_second = passed(shrink_second)
    arrive(shrink)
    shrink_other = joined([shrink_first], [shrink_second])

    shrink_last = links.core(shrink_other)
    spin(shrink)
    cross(shrink)
    shrink_last = passed(shrink_last)
    grads_far, (added, second_grad) = hidden_behind(
        cotangent,
        active[2:],
        back[2:],
        [shrink_other, shrink_last],
        expand_slots[2:],
        sums,
        [clock.now],
        HEAVY,
    )
    hidden_grad = [*grads, *passed(grads_far)]
    middle_grad, branch_grad, midnorm_grad, result = second_back(
        middle, gain_second, second_grad, cotangent, added, [clock.now]
    )
    branch_grad = passed(branch_grad)

    def expand_part(j, cost=LIGHT):
        return passed(
            expand_output_grad(
                second_normed, hidden_grad[j], saved[j][2], branch_grad, [clock.now], cost
            )
        )

    parts = {j: expand_part(j) for j in (3, 2)}
    arrive(shrink)
    spin(shrink)
    parts_core = links.core(parts[3])
    parts.update({1: expand_part(1, HEAVY), 0: expand_part(0)})
    expand.far(parts[2], passed(parts_core))

    slope_rows = [None] * 4
    first_grad = None
    for step, j in enumerate((3, 2, 1, 0)):
        if step == 0:
            cross(expand)
            parts_core = links.core(parts[1])
        elif step == 1:
            spin(shrink, expand)
            cross(expand)
            part_core = links.core(part)
        elif step == 2:
            attn.far(part, part_core)
            spin(shrink, expand, crossing=(expand, attn))
        else:
            spin(shrink, expand, crossing=(expand, attn))
            part_core = links.core(part)
        part, slope_rows[j], first_grad = attention_behind(
            heads_slot,
            branch_grad,
            first_normed,
            attn_slots[j],
            saved[j][:2],
            far,
            first_grad,
            [clock.now],
            HEAVY,
        )
        first_grad, part = passed(first_grad, part)
        if step == 0:
            expand.near(parts[0], passed(parts_core))
            arrive(shrink, expand)
        elif step == 1:
            part_core = passed(part_core)
            arrive(shrink, expand)
        elif step == 2:
            arrive(shrink, expand, attn)
        else:
            rows_out, small = first_back(
                heads_slot,
                flags,
                source,
                gain_first,
                first_grad,
                middle_grad,
                midnorm_grad,
                result,
                slope_rows,
                [clock.now],
            )
            small, rows_out = passed(small, list(rows_out))
            attn.near(part, passed(part_core))
            arrive(shrink, expand, attn)

    rows_back = [None] * 4

    def hop(value, moved):
        return passed(add(value, moved, [clock.now]))

    def send_back(k):
        rows_back[k] = links.back_to_rows(rows_out[k], k)

    def sent_back(k):
        rows_back[k] = passed(rows_back[k])

    spin(shrink, expand, attn, crossing=(attn,))
    send_back(2)
    small_moved = links.core(small)
    landed(shrink, 0, 1)
    arrive(shrink, expand, attn)
    small = hop(small, passed(small_moved))

    spin(shrink, expand, attn, crossing=(attn,))
    sent_back(2)
    small_moved = links.across(small)
    landed(shrink, 2)
    landed(expand, 0)
    arrive(shrink, expand, attn)
    small = hop(small, passed(small_moved))

    spin(expand, attn)
    send_back(3)
    small_moved = links.level(small, 1)
    landed(shrink, 3)
    landed(expand, 1)
    arrive(expand, attn)
    small = hop(small, passed(small_moved))
    bit = 4
    while bit < links.high:
        small = hop(small, passed(links.level(small, bit)))
        bit *= 2

    spin(expand, attn)
    sent_back(3)
    send_back(0)
    small_moved = links.level(small, 2)
    landed(expand, 2)
    arrive(expand, attn)
    small = hop(small, passed(small_moved))

    spin(attn)
    sent_back(0)
    send_back(1)
    small_other = links.stream(small)
    arrive(attn)

    spin(attn)
    landed(expand, 3)
    small_other = passed(small_other)
    arrive(attn)

    spin(attn)
    sent_back(1)
    text_result, visual_result, text_input_grad, visual_input_grad = passed(
        *sort_rows(flags, rows_back, [clock.now])
    )
    landed(attn, 0, 1)
    landed(attn, 2)
    landed(attn, 3)

    text_sh, visual_sh = shrink.laid
    text_ex, text_out, visual_ex, visual_out = expand.laid
    text_at, visual_at = attn.laid[:3], attn.laid[3:]
    text_small = jnp.where(lo == 0, small, small_other)
    visual_small = jnp.where(lo == 0, small_other, small)
    slope_sum = lax.dynamic_slice(
        (text_small + visual_small)[2], (tensor_index * heads_slot,), (heads_slot,)
    )
    return (
        text_result,
        visual_result,
        text_input_grad,
        visual_input_grad,
        text_small[0],
        *(grad.T for grad in text_at),
        text_out,
        text_small[1],
        text_ex,
        text_sh,
        visual_small[0],
        *(grad.T for grad in visual_at),
        visual_out,
        visual_small[1],
        visual_ex,
        visual_sh,
        slope_sum,
    )


def solution(mesh):
    rows = P("dp", "tensor", None)
    split_out = P(None, "tensor")
    split_in = P("tensor", None)
    weights = (P(), split_out, split_out, split_out, split_in, P(), split_out, split_in)
    return jax.shard_map(
        shards,
        mesh=mesh,
        in_specs=(
            rows,
            rows,
            P("dp", None, None),
            P("dp"),
            *weights,
            *weights,
            P("tensor"),
            rows,
            rows,
        ),
        out_specs=(rows, rows, rows, rows, *weights, *weights, P("tensor")),
        check_vma=False,
    )
```

```python
import functools

import jax
import jax.numpy as jnp
from jax import lax
from jax.experimental import pallas as pl
from jax.experimental.pallas import tpu as pltpu
from jax.sharding import PartitionSpec as P

HEAD_DIM = 64
GRID_W = 32
NBIN = 1000
EPSILON = 1e-05
AXES = ("dp", "tensor")
ROWS = (((0,), (0,)), ((), ()))
COLS = (((1,), (1,)), ((), ()))
F32 = jnp.float32
BF16 = jnp.bfloat16
FAR = 1e30
GELU_A = 0.7978845608028654
GELU_B = 0.044715
SCALE = HEAD_DIM ** (-0.5)
FLAG_LO, FLAG_X, FLAG_C, FLAG_HALF, FLAG_RING, FLAG_PLACE, FLAG_TENSOR = range(7)
FLOPS_US = 1_150_000_000
LIGHT, HEAVY = 0.001, 20
VMEM_LIMIT = 16 * 1024 * 1024
IN_VMEM = pl.BlockSpec(memory_space=pltpu.VMEM)
IN_SMEM = pl.BlockSpec(memory_space=pltpu.SMEM)
IN_ANY = pl.BlockSpec(memory_space=pl.ANY)
IN_HBM = pl.BlockSpec(memory_space=pltpu.HBM)


def dot(a, b, dims=None):
    if dims is None:
        return jnp.dot(a, b, preferred_element_type=F32)
    return lax.dot_general(a, b, dims, preferred_element_type=F32)


def kernel_call(body, outs, ins, scalars=0, scratch=(), after=(), far_ins=0, far_outs=0, hbm_outs=0, cost=LIGHT):
    count = len(ins)

    def whole(*refs):
        body(*refs[:count], *refs[count + len(after) :])

    near = [IN_SMEM] * scalars + [IN_VMEM] * (count - scalars - far_ins) + [IN_ANY] * far_ins
    return pl.pallas_call(
        whole,
        out_shape=outs,
        in_specs=near + [IN_ANY] * len(after),
        out_specs=[IN_HBM] * hbm_outs
        + [IN_VMEM] * (len(outs) - hbm_outs - far_outs)
        + [IN_ANY] * far_outs,
        scratch_shapes=list(scratch),
        compiler_params=pltpu.CompilerParams(vmem_limit_bytes=VMEM_LIMIT),
        cost_estimate=pl.CostEstimate(flops=int(FLOPS_US * cost), bytes_accessed=1000, transcendentals=0),
    )(*ins, *after)


def shape(rows, cols, dtype):
    return jax.ShapeDtypeStruct((rows, cols), dtype)


def norm_parts(values):
    center = values - jnp.mean(values, axis=-1, keepdims=True)
    spread = jnp.mean(center * center, axis=-1, keepdims=True)
    scale = lax.rsqrt(spread + EPSILON)
    return center * scale, scale


def norm_back(normed, scale, gain, grad):
    inner = grad * gain
    mean_inner = jnp.mean(inner, axis=-1, keepdims=True)
    mean_both = jnp.mean(inner * normed, axis=-1, keepdims=True)
    return scale * (inner - mean_inner - normed * mean_both)


def first_norm_body(gain_ref, *refs):
    blocks, (source_ref, out_ref) = refs[:-2], refs[-2:]
    rows = source_ref.shape[0] // len(blocks)
    for k, block in enumerate(blocks):
        at = slice(k * rows, (k + 1) * rows)
        values = block[:rows, :]
        source_ref[at, :] = values
        normed, unused = norm_parts(values.astype(F32))
        out_ref[at, :] = (normed * gain_ref[...]).astype(BF16)


def first_norm(gain, blocks, rows, after):
    outs = [shape(rows * len(blocks), blocks[0].shape[1], BF16)] * 2
    return kernel_call(first_norm_body, outs, [gain, *blocks], after=after, cost=HEAVY)


def second_norm_body(source_ref, branch_ref, gain_ref, middle_ref, out_ref):
    middle = source_ref[...].astype(F32) + branch_ref[...]
    middle_ref[...] = middle
    normed, unused = norm_parts(middle)
    out_ref[...] = (normed * gain_ref[...]).astype(BF16)


def second_norm(source, branch, gain, after):
    outs = [shape(*source.shape, F32), shape(*source.shape, BF16)]
    return kernel_call(second_norm_body, outs, [source, branch, gain], after=after)


def second_back_body(
    middle_ref, gain_ref, grad_ref, cot_ref, added_ref, mid_ref, branch_ref, gain_out, result_ref
):
    middle = middle_ref[...]
    normed, scale = norm_parts(middle)
    grad = grad_ref[...]
    total = cot_ref[...].astype(F32) + norm_back(normed, scale, gain_ref[...], grad)
    mid_ref[...] = total
    branch_ref[...] = total.astype(BF16)
    gain_out[...] = jnp.sum(grad * normed, axis=0, keepdims=True)
    result_ref[...] = (middle + added_ref[...]).astype(BF16)


def second_back(middle, gain, grad, cotangent, added, after):
    rows, cols = middle.shape
    outs = [shape(rows, cols, F32), shape(rows, cols, BF16), shape(1, cols, F32)]
    outs.append(shape(rows, cols, BF16))
    ins = [middle, gain, grad, cotangent, added]
    return kernel_call(second_back_body, outs, ins, after=after)


def first_back_body(
    heads, flags, source_ref, gain_ref, grad_ref, mid_ref, midnorm_ref, result_ref, *refs
):
    slopes, blocks, small_ref = refs[:4], refs[4:8], refs[8]
    normed, scale = norm_parts(source_ref[...].astype(F32))
    grad = grad_ref[...]
    out = (mid_ref[...] + norm_back(normed, scale, gain_ref[...], grad)).astype(BF16)
    rows = result_ref.shape[0] // 4
    for k in range(4):
        blocks[k][:rows, :] = result_ref[k * rows : (k + 1) * rows, :]
        blocks[k][rows:, :] = out[k * rows : (k + 1) * rows, :]
    small_ref[...] = jnp.zeros_like(small_ref)
    small_ref[0:1, :] = jnp.sum(grad * normed, axis=0, keepdims=True)
    small_ref[1:2, :] = midnorm_ref[...]
    lane = lax.broadcasted_iota(jnp.int32, midnorm_ref.shape, 1)
    row = jnp.zeros(midnorm_ref.shape, F32)
    for j in range(4):
        sums = -jnp.sum(slopes[j][...], axis=1, keepdims=True)
        for h in range(heads):
            spot = (flags[FLAG_TENSOR] ^ j) * heads + h
            row = row + jnp.where(lane == spot, sums[h : h + 1, :], 0.0)
    small_ref[2:3, :] = row


def first_back(heads, flags, source, gain, grad, middle_grad, midnorm_grad, result, slope_rows, after):
    rows, cols = source.shape
    outs = [shape(rows // 2, cols, BF16)] * 4 + [shape(8, cols, F32)]
    ins = [flags, source, gain, grad, middle_grad, midnorm_grad, result, *slope_rows]
    out = kernel_call(functools.partial(first_back_body, heads), outs, ins, 1, after=after)
    return out[:4], out[4]


def each(flag, one, other):
    pl.when(flag == 0)(one)
    pl.when(flag != 0)(other)


def info_body(flags, counts, boxes_ref, info_ref):
    info_ref[...] = jnp.zeros_like(info_ref)
    info_ref[0:2, :] = boxes_ref[flags[FLAG_X]]
    info_ref[2:3, :] = jnp.full((1, info_ref.shape[1]), counts[flags[FLAG_X]], jnp.int32)


def page_info(flags, counts, boxes, after):
    outs = [shape(8, boxes.shape[2], jnp.int32)]
    return kernel_call(info_body, outs, [flags, counts, boxes], 2, after=after)[0]


def distance_body(flags, own_ref, theirs_ref, far_ref, info):
    tokens = far_ref.shape[0]
    block = tokens // 4
    mine = 1 - (flags[FLAG_LO] ^ flags[FLAG_C])
    text = 1 - flags[FLAG_LO]
    share = text.astype(F32)
    for k in range(4):
        at = slice(k * block, (k + 1) * block)
        shard = flags[FLAG_PLACE] ^ k
        there = pl.ds(pl.multiple_of(shard * block, block), block)
        boxes = own_ref[:, there] * mine + theirs_ref[:, there] * (1 - mine)
        index = lax.broadcasted_iota(jnp.int32, (1, block), 1) + shard * block
        column = (index & (GRID_W - 1)).astype(F32)
        line = (index >> (GRID_W.bit_length() - 1)).astype(F32)
        text_place = boxes[0:2, :].astype(F32) / NBIN
        coord_x = text_place[0:1, :] * share + (column + 0.5) / GRID_W * (1.0 - share)
        coord_y = text_place[1:2, :] * share + (line + 0.5) / (tokens // GRID_W) * (1.0 - share)
        count = boxes[2:3, :] * text + tokens * (1 - text)
        info[...] = jnp.zeros_like(info) if k == 0 else info[...]
        info[0:1, at] = coord_x
        info[1:2, at] = coord_y
        info[2:3, at] = jnp.where(index < count, 0.0, 1.0)
    turned = info[...].T
    delta_x = turned[:, 0:1] - info[0:1, :]
    delta_y = turned[:, 1:2] - info[1:2, :]
    distance = jnp.sqrt(delta_x * delta_x + delta_y * delta_y)
    far_ref[...] = jnp.where(turned[:, 2:3] > 0.5, FAR, distance)


def distances(flags, own, theirs, after=()):
    tokens = own.shape[1]
    scratch = [pltpu.VMEM((8, tokens), F32)]
    return kernel_call(
        distance_body, [shape(tokens, tokens, F32)], [flags, own, theirs], 1, scratch, after
    )[0]


def both(a, b):
    return (a.astype(F32) + b.astype(F32)).astype(BF16)


def near_body(own_ref, core_ref, out_ref):
    out_ref[...] = both(own_ref[...], core_ref[...])


def near_sum(own, core, after):
    return kernel_call(near_body, [shape(*own.shape, BF16)], [own, core], after=after)[0]


def far_body(flags, own_ref, core_ref, *pieces):
    rows = own_ref.shape[0] // 4
    share = 4 // len(pieces)
    for i in range(4):
        at = pl.ds(pl.multiple_of(((flags[FLAG_RING] + 3 - i) & 3) * rows, rows), rows)
        place = slice(i % share * rows, (i % share + 1) * rows)
        pieces[i // share][place, :] = both(own_ref[at, :], core_ref[at, :])


def far_sum(flags, own, core, count, after):
    rows, cols = own.shape
    outs = [shape(rows // count, cols, BF16)] * count
    return kernel_call(far_body, outs, [flags, own, core], 1, after=after)


class Span:
    def __init__(self, array, start, rows):
        self.array, self.start, self.rows = array, start, rows


def turn_body(plan, flags, *refs):
    ins, outs = refs[: plan["ins"]], refs[plan["ins"] :]

    def rows_of(span):
        index, start, rows = span
        return ins[index][start : start + rows, :]

    for step, near, spans, places in plan["sums"]:
        rows = spans[0][2]
        at = pl.ds(pl.multiple_of(((flags[FLAG_RING] + 3 - step) & 3) * rows, rows), rows)
        total = ins[near][at, :].astype(F32)
        for span in spans:
            total = total + rows_of(span).astype(F32)
        total = total.astype(BF16)
        for out, start in places:
            outs[out][start : start + rows, :] = total
    for span, places in plan["moves"]:
        for out, start in places:
            outs[out][start : start + span[2], :] = rows_of(span)


def turn(flags, sums, moves, after):
    ins, index = [flags], {}

    def place_of(array):
        if id(array) not in index:
            index[id(array)] = len(ins) - 1
            ins.append(array)
        return index[id(array)]

    def static(span):
        return (place_of(span.array), span.start, span.rows)

    heights = {}

    def places_of(outs, rows):
        places = []
        for out in outs:
            places.append((out, heights.get(out, 0)))
            heights[out] = heights.get(out, 0) + rows
        return places

    plan = {"sums": [], "moves": []}
    for step, near, spans, outs in sums:
        rows = spans[0].rows
        plan["sums"].append(
            (step, place_of(near), [static(s) for s in spans], places_of(outs, rows))
        )
    for span, outs in moves:
        plan["moves"].append((static(span), places_of(outs, span.rows)))
    plan["ins"] = len(ins) - 1
    order = sorted(heights)
    number = {out: i for i, out in enumerate(order)}
    for kind in ("sums", "moves"):
        plan[kind] = [
            (*item[:-1], [(number[out], start) for out, start in item[-1]]) for item in plan[kind]
        ]
    cols = ins[1].shape[1]
    shapes = [shape(heights[out], cols, BF16) for out in order]
    body = functools.partial(turn_body, plan)
    made = kernel_call(body, shapes, ins, 1, after=after)
    places = [
        {order[out]: start for out, start in item[-1]} for kind in ("sums", "moves") for item in plan[kind]
    ]
    return dict(zip(order, made, strict=True)), places


def piece_sum(flags, step, near, spans, after):
    made, places = turn(flags, [(step, near, spans, [0])], [], after)
    return made[0]


def grad_body(left_ref, right_ref, out_ref):
    out_ref[...] = dot(left_ref[...], right_ref[...], ROWS).astype(BF16)


def grad_of(left, right, after, cost=LIGHT):
    outs = [shape(left.shape[1], right.shape[1], BF16)]
    return kernel_call(grad_body, outs, [left, right], after=after, cost=cost)[0]


def add_body(left_ref, right_ref, out_ref):
    out_ref[...] = left_ref[...] + right_ref[...]


def add(left, right, after):
    return kernel_call(add_body, [shape(*left.shape, left.dtype)], [left, right], after=after)[0]


def expand_output_body(normed_ref, hidden_ref, attended_ref, branch_ref, out_ref):
    rows = normed_ref.shape[1]
    out_ref[:rows, :] = dot(normed_ref[...], hidden_ref[...], ROWS).astype(BF16)
    out_ref[rows:, :] = dot(attended_ref[...], branch_ref[...], ROWS).astype(BF16)


def expand_output_grad(normed, hidden_grad, attended, branch_grad, after, cost=LIGHT):
    rows = normed.shape[1] + attended.shape[1]
    outs = [shape(rows, normed.shape[1], BF16)]
    ins = [normed, hidden_grad, attended, branch_grad]
    return kernel_call(expand_output_body, outs, ins, after=after, cost=cost)[0]


def join_body(heights, flags, first_ref, second_ref, out_ref):
    start = low = 0
    for height in heights:
        for ref, side in ((first_ref, flags[FLAG_HALF]), (second_ref, 1 - flags[FLAG_HALF])):
            at = pl.multiple_of(low + side * height, height)
            out_ref[pl.ds(at, height), :] = ref[start : start + height, :]
        start += height
        low += 2 * height
    rest = out_ref.shape[0] - low
    if rest:
        out_ref[low:, :] = first_ref[start : start + rest, :]


def join(flags, first, second, heights, after):
    rows = first.shape[0] + sum(heights)
    outs = [shape(rows, first.shape[1], BF16)]
    body = functools.partial(join_body, heights)
    return kernel_call(body, outs, [flags, first, second], 1, after=after)[0]


def join_ring_body(flags, *refs):
    pieces, out_ref = refs[:-1], refs[-1]
    rows = pieces[0].shape[0]
    for r, piece in enumerate(pieces):
        at = pl.multiple_of(((flags[FLAG_RING] + 4 - r) & 3) * rows, rows)
        out_ref[pl.ds(at, rows), :] = piece[...]


def join_ring(flags, pieces, after):
    rows, cols = pieces[0].shape
    outs = [shape(4 * rows, cols, BF16)]
    return kernel_call(join_ring_body, outs, [flags, *pieces], 1, after=after)[0]


def lay_body(groups, r, start, flags, *refs):
    size = len(groups)
    chunks, refs = refs[:2], refs[2:]
    outs, (held, sems) = refs[-2 * size - 2 : -2], refs[-2:]
    rows = held.shape[1]
    spot = (flags[FLAG_RING] + 4 - r) & 3
    waits = []
    for side in range(2):
        slot, sem = held.at[side], sems.at[side]
        slot[...] = chunks[side][start : start + rows, :].astype(F32)
        stream = flags[FLAG_LO] ^ side
        for p in range(4):
            for g, (low, high) in enumerate(groups):
                first, last = max(p * rows, low), min((p + 1) * rows, high)
                if first >= last:
                    continue
                piece = slot.at[pl.ds(first - p * rows, last - first)]
                place = pl.ds(first - low, last - first)
                for s in range(2):
                    copy = pltpu.make_async_copy(piece, outs[s * size + g].at[place], sem)
                    pl.when((spot == p) & (stream == s))(copy.start)
        waits.append(pltpu.make_async_copy(slot, outs[0].at[pl.ds(0, rows)], sem))
    for copy in waits:
        copy.wait()


def lay(flags, r, mine, theirs, start, rows, groups, laid, after):
    cols = mine.shape[1]
    outs = [shape(high - low, cols, F32) for low, high in groups] * 2
    ins = [flags, mine, theirs]
    first = len(ins)
    body = functools.partial(lay_body, groups, r, start)
    laid = [] if laid is None else list(laid)

    def whole(*refs):
        body(*refs[:first], *refs[first + len(laid) + len(after) :])

    return pl.pallas_call(
        whole,
        out_shape=outs,
        in_specs=[IN_SMEM, IN_VMEM, IN_VMEM] + [IN_ANY] * (len(laid) + len(after)),
        out_specs=[IN_ANY] * len(outs),
        scratch_shapes=[pltpu.VMEM((2, rows, cols), F32), pltpu.SemaphoreType.DMA((2,))],
        input_output_aliases={first + i: i for i in range(len(laid))},
        compiler_params=pltpu.CompilerParams(vmem_limit_bytes=VMEM_LIMIT),
        cost_estimate=pl.CostEstimate(
            flops=int(FLOPS_US * LIGHT), bytes_accessed=1000, transcendentals=0
        ),
    )(*ins, *laid, *after)


def sort_body(flags, *refs):
    parts, outs, sems = refs[:4], refs[4:8], refs[8]
    rows = outs[0].shape[1]
    copies = []
    for k in range(4):
        stream = flags[FLAG_C] ^ (k & 1)
        page = flags[FLAG_X] ^ (k >> 1)
        for n in range(2):
            piece = parts[k].at[pl.ds(n * rows, rows)]
            sem = sems.at[2 * k + n]

            def move(out, piece=piece, page=page, sem=sem):
                pltpu.make_async_copy(piece, out.at[page], sem).start()

            each(
                stream,
                functools.partial(move, outs[2 * n]),
                functools.partial(move, outs[2 * n + 1]),
            )
            copies.append(pltpu.make_async_copy(piece, outs[0].at[0], sem))
    for copy in copies:
        copy.wait()


def sort_rows(flags, parts, after=()):
    rows, cols = parts[0].shape
    outs = [jax.ShapeDtypeStruct((2, rows // 2, cols), BF16)] * 4
    scratch = [pltpu.SemaphoreType.DMA((8,))]
    return kernel_call(sort_body, outs, [flags, *parts], 1, scratch, after, far_ins=4, far_outs=4)


def slope_of(w_ref, wide, h):
    rows = [w_ref[4 * wide + i : 4 * wide + i + 1, h : h + 1].astype(F32) for i in range(3)]
    return rows[0] + rows[1] + rows[2]


def attention_ahead_body(heads, block, first, normed_ref, w_ref, far_ref, *refs):
    branch_ref, refs = (None, refs) if first else (refs[0], refs[1:])
    kept, (out_ref, *held, sems) = refs[:3], refs[3:]
    qkv_ref, attended_ref, log_ref = held
    keep = [pltpu.make_async_copy(held[i], kept[i], sems.at[i]) for i in range(3)]
    tokens = normed_ref.shape[0]
    wide = heads * HEAD_DIM
    qkv_ref[...] = dot(normed_ref[...], w_ref[: 3 * wide, :], COLS).astype(BF16)
    log_ref[...] = jnp.zeros_like(log_ref)
    keep[0].start()
    for h in range(heads):
        col = slice(h * HEAD_DIM, (h + 1) * HEAD_DIM)
        keys = qkv_ref[:, wide + col.start : wide + col.stop]
        values_t = qkv_ref[:, 2 * wide + col.start : 2 * wide + col.stop].T
        slope = slope_of(w_ref, wide, h)
        for b in range(tokens // block):
            rows = slice(b * block, (b + 1) * block)
            scores = dot(keys, qkv_ref[rows, col], COLS) * SCALE - slope * far_ref[:, rows]
            highest = jnp.max(scores, axis=0, keepdims=True)
            exponent = jnp.exp(scores - highest)
            totals = jnp.sum(exponent, axis=0, keepdims=True)
            soft_weights = (exponent * (1.0 / totals)).astype(BF16)
            log_ref[h : h + 1, rows] = highest + jnp.log(totals)
            attended_ref[rows, col] = dot(values_t, soft_weights).T.astype(BF16)
    keep[1].start()
    keep[2].start()
    part = dot(attended_ref[...], w_ref[3 * wide : 4 * wide, :])
    out_ref[...] = part if first else branch_ref[...] + part
    for copy in keep:
        copy.wait()


def attention_ahead(heads, normed, w, far, branch, after=(), cost=LIGHT):
    rows, cols = normed.shape
    wide = heads * HEAD_DIM
    ins = [normed, w, far] + ([] if branch is None else [branch])
    outs = [shape(rows, 3 * wide, BF16), shape(rows, wide, BF16), shape(8, rows, F32)]
    scratch = [pltpu.VMEM(out.shape, out.dtype) for out in outs] + [pltpu.SemaphoreType.DMA((3,))]
    outs.append(shape(rows, cols, F32))
    body = functools.partial(attention_ahead_body, heads, min(256, rows), branch is None)
    return kernel_call(body, outs, ins, 0, scratch, after, hbm_outs=3, cost=cost)


def attention_behind_body(
    heads, block, first, branch_ref, normed_ref, w_ref, qkv_ref, log_ref, far_ref, *refs
):
    grad_ref = None if first else refs[0]
    weight_grad, out_slope, out_ref, out_qkv, attended_grad, keys_sum, values_sum = (
        refs if first else refs[1:]
    )
    tokens = branch_ref.shape[0]
    wide = heads * HEAD_DIM
    attended_grad[...] = dot(branch_ref[...], w_ref[3 * wide : 4 * wide, :], COLS).astype(BF16)
    for h in range(heads):
        col = slice(h * HEAD_DIM, (h + 1) * HEAD_DIM)
        key_col = slice(wide + col.start, wide + col.stop)
        value_col = slice(2 * wide + col.start, 2 * wide + col.stop)
        keys = qkv_ref[:, key_col]
        values = qkv_ref[:, value_col]
        keys_t = keys.T
        slope = slope_of(w_ref, wide, h)
        for b in range(tokens // block):
            rows = slice(b * block, (b + 1) * block)
            queries = qkv_ref[rows, col]
            grad = attended_grad[rows, col]
            far = far_ref[:, rows]
            scores = dot(keys, queries, COLS) * SCALE - slope * far
            probs = jnp.exp(scores - log_ref[h : h + 1, rows])
            values_part = dot(probs.astype(BF16), grad)
            probs_grad = dot(values, grad, COLS)
            mean = jnp.sum(probs * probs_grad, axis=0, keepdims=True)
            scores_grad = probs * (probs_grad - mean)
            out_slope[h : h + 1, rows] = jnp.sum(scores_grad * far, axis=0, keepdims=True)
            scores_grad = scores_grad.astype(BF16)
            keys_part = dot(scores_grad, queries)
            if b == 0:
                keys_sum[...] = keys_part
                values_sum[...] = values_part
            else:
                keys_sum[...] += keys_part
                values_sum[...] += values_part
            queries_grad = dot(keys_t, scores_grad) * SCALE
            out_qkv[rows, col] = queries_grad.T.astype(BF16)
        out_qkv[:, key_col] = (keys_sum[...] * SCALE).astype(BF16)
        out_qkv[:, value_col] = values_sum[...].astype(BF16)
    part = dot(out_qkv[...], w_ref[: 3 * wide, :])
    weight_grad[...] = dot(out_qkv[...], normed_ref[...], ROWS).astype(BF16)
    out_ref[...] = part if first else grad_ref[...] + part


def attention_behind(heads, branch_grad, normed, w, kept, far, grad, after=(), cost=LIGHT):
    rows, cols = branch_grad.shape
    wide = heads * HEAD_DIM
    ins = [branch_grad, normed, w, *kept, far] + ([] if grad is None else [grad])
    outs = [shape(3 * wide, cols, BF16), shape(8, rows, F32), shape(rows, cols, F32)]
    scratch = [pltpu.VMEM((rows, 3 * wide), BF16), pltpu.VMEM((rows, wide), BF16)] + [pltpu.VMEM((rows, HEAD_DIM), F32)] * 2
    body = functools.partial(attention_behind_body, heads, min(256, rows), grad is None)
    return kernel_call(body, outs, ins, 0, scratch, after, cost=cost)


def gelu_both(values):
    square = values * values
    bend = jnp.tanh(GELU_A * values * (1.0 + GELU_B * square))
    half = 0.5 * (1.0 + bend)
    slope = half + 0.5 * values * (1.0 - bend * bend) * (
        GELU_A + (3.0 * GELU_A * GELU_B) * square
    )
    return values * half, slope


def hidden_ahead_body(count, blocks, starts, normed_ref, *refs):
    weights, refs = refs[:count], refs[count:]
    parts, outs, held = refs[:blocks], refs[blocks:-1], refs[-1]
    tokens, cols = normed_ref.shape
    for k in range(blocks):
        rows = tokens // blocks
        outs[2 * count][k * rows : (k + 1) * rows, :] = parts[k][parts[k].shape[0] - rows :, :]
    step = 32
    for j in range(count):
        held[...] = dot(normed_ref[...], weights[j][starts[j] : starts[j] + cols, :])
        for b in range(tokens // step):
            rows = slice(b * step, (b + 1) * step)
            active, back = gelu_both(held[rows, :])
            outs[2 * j][rows, :] = active.astype(BF16)
            outs[2 * j + 1][rows, :] = back.astype(BF16)


def hidden_ahead(normed, weights, parts=(), after=(), cost=LIGHT):
    rows, cols = normed.shape
    arrays, starts = zip(*weights, strict=True)
    count, wide = len(weights), arrays[0].shape[1]
    outs = [shape(rows, wide, BF16)] * (2 * count)
    if parts:
        outs.append(shape(rows, cols, BF16))
    body = functools.partial(hidden_ahead_body, count, len(parts), starts)
    scratch = [pltpu.VMEM((rows, wide), F32)]
    out = kernel_call(body, outs, [normed, *arrays, *parts], 0, scratch, after, cost=cost)
    return out[0 : 2 * count : 2], out[1 : 2 * count : 2], out[-1]


def hidden_behind_body(count, first, starts, cot_ref, *refs):
    active, back, shrink, expand = (refs[count * i : count * (i + 1)] for i in range(4))
    refs = refs[4 * count :]
    before, refs = ((), refs) if first else (refs[:2], refs[2:])
    grads, (added_ref, out_ref) = refs[:count], refs[count:]
    cols, wide = cot_ref.shape[1], active[0].shape[1]
    for j in range(count):
        down = slice(starts[0][j], starts[0][j] + wide)
        up = slice(starts[1][j], starts[1][j] + cols)
        part = dot(active[j][...], shrink[j][down, :])
        if j == 0:
            added_ref[...] = part if first else before[0][...] + part
        else:
            added_ref[...] += part
        active_grad = dot(cot_ref[...], shrink[j][down, :], COLS)
        grads[j][...] = (active_grad * back[j][...].astype(F32)).astype(BF16)
        part = dot(grads[j][...], expand[j][up, :], COLS)
        if j == 0:
            out_ref[...] = part if first else before[1][...] + part
        else:
            out_ref[...] += part


def hidden_behind(cotangent, active, back, shrink, expand, before=(), after=(), cost=LIGHT):
    rows, cols = cotangent.shape
    count, wide = len(active), active[0].shape[1]
    downs, ups = zip(*shrink, strict=True), zip(*expand, strict=True)
    (downs, down_starts), (ups, up_starts) = downs, ups
    outs = [shape(rows, wide, BF16)] * count + [shape(rows, cols, F32)] * 2
    body = functools.partial(hidden_behind_body, count, not before, (down_starts, up_starts))
    ins = [cotangent, *active, *back, *downs, *ups, *before]
    out = kernel_call(body, outs, ins, after=after, cost=cost)
    return out[:count], out[count:]


class Links:
    def __init__(self, pairs):
        self.pairs = pairs
        self.high = pairs // 2
        self.ring_size = 4

    def send(self, value, move):
        table = []
        for dp in range(self.pairs):
            for tensor in range(4):
                hi, lo, x, c = move(dp // 2, dp % 2, tensor // 2, tensor % 2)
                table.append((dp * 4 + tensor, (hi * 2 + lo) * 4 + x * 2 + c))
        return lax.ppermute(value, AXES, table)

    def core(self, value):
        return self.send(value, lambda hi, lo, x, c: (hi, lo, x, 1 - c))

    def across(self, value):
        return self.send(value, lambda hi, lo, x, c: (hi, lo, 1 - x, c))

    def stream(self, value):
        return self.send(value, lambda hi, lo, x, c: (hi, 1 - lo, x, c))

    def level(self, value, bit):
        return self.send(value, lambda hi, lo, x, c: (hi ^ bit, lo, x, c))

    def ring(self, value):
        after = (1, 3, 0, 2)
        return self.send(value, lambda hi, lo, x, c: (hi // 4 * 4 + after[hi % 4], lo, x, c))

    def out_to_page(self, value, k):
        return self.send(value, lambda hi, lo, x, c: (hi, c ^ (k & 1), x ^ (k >> 1), lo))

    def back_to_rows(self, value, k):
        return self.send(value, lambda hi, lo, x, c: (hi, c, x ^ (k >> 1), lo ^ (k & 1)))


def add_low(a, b):
    return (a.astype(F32) + b.astype(F32)).astype(BF16)


class Clock:
    def __init__(self, start):
        self.now = start

    def passed(self, *values):
        values, self.now = lax.optimization_barrier((list(values), self.now))
        return values[0] if len(values) == 1 else values


def shards(
    text_input,
    visual_input,
    text_boxes,
    text_count,
    text_prenorm,
    text_query,
    text_key,
    text_value,
    text_output,
    text_midnorm,
    text_expand,
    text_shrink,
    visual_prenorm,
    visual_query,
    visual_key,
    visual_value,
    visual_output,
    visual_midnorm,
    visual_expand,
    visual_shrink,
    slopes,
    text_cotangent,
    visual_cotangent,
):
    dp_index = lax.axis_index("dp")
    tensor_index = lax.axis_index("tensor")
    hi, lo = dp_index // 2, dp_index % 2
    x, c = tensor_index // 2, tensor_index % 2
    links = Links(lax.axis_size("dp"))
    heads_slot = slopes.shape[0]
    half = hi % 2
    n = links.ring_size
    spot = (hi % n) ^ ((hi % n) >> 1)
    flags = jnp.stack([lo, x, c, half, spot, 2 * x + lo, tensor_index]).astype(jnp.int32)
    gain_first, gain_second = (
        jnp.where(lo == 0, text, visual).astype(F32)[None]
        for text, visual in ((text_prenorm, visual_prenorm), (text_midnorm, visual_midnorm))
    )

    def half_rows(shard):
        return lax.dynamic_slice_in_dim(shard, half * (shard.shape[0] // 2), shard.shape[0] // 2)

    def page_blocks(text_rows, visual_rows):
        blocks = []
        for k in range(4):
            parts = [
                lax.dynamic_index_in_dim(rows, x ^ (k >> 1), 0, False)
                for rows in (text_rows, visual_rows)
            ]
            blocks.append(jnp.where((c ^ (k & 1)) == 0, *parts))
        return blocks

    def to_page(blocks, chosen=(3, 2, 1, 0)):
        return [links.out_to_page(blocks[k], k) for k in chosen][::-1]

    def low(value):
        return value.astype(BF16)

    def add_low(a, b):
        return low(a.astype(F32) + b.astype(F32))

    clock = Clock(slopes)
    passed = clock.passed

    text_attn = [text_query.T, text_key.T, text_value.T, text_output]
    visual_attn = [visual_query.T, visual_key.T, visual_value.T, visual_output]
    slope_parts = []
    rest = slopes
    for i in range(3):
        slope_parts.append(low(rest))
        rest = rest - slope_parts[i].astype(F32)
    wide, width = text_output.shape
    tail = jnp.zeros((16, width), BF16).at[:3, :heads_slot].set(jnp.stack(slope_parts))
    heights = [2 * wide]
    attn_own = jnp.concatenate(
        [
            jnp.where(
                lo == 0,
                jnp.concatenate([text_query.T, text_key.T, text_value.T, text_output]),
                jnp.concatenate([visual_query.T, visual_key.T, visual_value.T, visual_output]),
            ),
            tail,
        ]
    )

    attn_half = passed(jnp.concatenate([half_rows(attn_own[: 4 * wide]), tail]))
    attn_first = links.across(attn_half)
    text_rows, visual_rows = passed(text_input, visual_input)
    in_blocks = page_blocks(text_rows, visual_rows)
    cot_parts = page_blocks(text_cotangent, visual_cotangent)
    in_blocks = [
        jnp.concatenate([in_blocks[k], cot_parts[k]]) if k < 2 else in_blocks[k] for k in range(4)
    ]
    in_blocks = to_page(passed(in_blocks))
    info = passed(page_info(flags, text_count, text_boxes, [clock.now]))
    info_theirs = links.stream(info)
    expand_own = jnp.where(lo == 0, text_expand, visual_expand)
    shrink_own = jnp.where(lo == 0, text_shrink, visual_shrink)
    expand_half = half_rows(expand_own)
    info_theirs = passed(info_theirs)
    far = passed(distances(flags, info, info_theirs, [clock.now]))
    expand_half, cot_parts, gain_first, gain_second = passed(
        expand_half, cot_parts, gain_first, gain_second
    )
    attn_first = passed(attn_first)
    attn_second = links.level(attn_first, 1)
    in_blocks = passed(in_blocks)
    attn_own, expand_half, cot_parts = passed(attn_own, expand_half, cot_parts)
    attn_core = links.core(attn_own)
    expand_first = links.across(expand_half)
    expand_core = links.core(expand_own)
    source, first_normed = passed(*first_norm(gain_first, in_blocks, text_input.shape[1], [clock.now]))

    saved = [None] * 4

    def ahead(j, weights, branch, cost=LIGHT):
        qkv, attended, log_total, branch = attention_ahead(
            heads_slot, first_normed, weights, far, branch, [clock.now], cost
        )
        saved[j] = (qkv, log_total, attended)
        return passed(branch)

    branch = ahead(0, attn_own, None)
    attn_core = passed(attn_core)
    branch = ahead(1, attn_core, branch)
    quarter = shrink_own.shape[0] // 4
    shrink_part = passed(lax.dynamic_slice_in_dim(shrink_own, spot * quarter, quarter))
    attn_second = passed(attn_second)
    expand_first, expand_core = passed(expand_first, expand_core)
    attn_other = passed(join(flags, attn_first, attn_second, heights, [clock.now]))

    expand_second = links.level(expand_first, 1)
    attn_last = links.core(attn_other)
    cot_parts, shrink_part = passed(cot_parts, shrink_part)
    shrink_parts = [links.across(shrink_part)]
    cot_far = to_page(cot_parts, (3, 2))
    branch = ahead(2, attn_other, branch, HEAVY)
    attn_last = passed(attn_last)
    branch = ahead(3, attn_last, branch)
    attn_slots = [attn_own, attn_core, attn_other, attn_last]
    expand_second = passed(expand_second)
    shrink_parts[0] = passed(shrink_parts[0])
    cot_far = passed(cot_far)
    expand_other = passed(join(flags, expand_first, expand_second, [width // 2], [clock.now]))

    shrink_own = passed(shrink_own)
    expand_last = links.core(expand_other)
    shrink_parts.append(links.ring(shrink_parts[0]))
    shrink_core = links.core(shrink_own)
    middle, second_normed = second_norm(source, branch, gain_second, [clock.now])
    second_normed = passed(second_normed)
    active, back = [], []
    for j in range(4):
        weights = (expand_own, expand_core, expand_other, expand_last)[j]
        some, other, joined = hidden_ahead(
            second_normed,
            [(weights, 0)],
            [*in_blocks[:2], *cot_far] if j == 0 else [],
            [clock.now],
            HEAVY if j == 0 else LIGHT,
        )
        active += [passed(some[0])]
        back += other
        if j == 0:
            cotangent = passed(joined)
        if j == 1:
            expand_last = passed(expand_last)
    expand_slots = [(w, 0) for w in (expand_own, expand_core, expand_other, expand_last)]
    parts, parts_core = {}, {}
    for j in (3, 1):
        parts[j] = passed(grad_of(active[j], cotangent, [clock.now]))
    shrink_parts[1], shrink_core = passed(shrink_parts[1], shrink_core)
    for j in (3, 1):
        parts_core[j] = links.core(parts[j])
    shrink_parts.append(links.ring(shrink_parts[1]))
    shrink_slots = [(shrink_own, 0), (shrink_core, 0)]
    for j, cost in ((2, HEAVY), (0, LIGHT)):
        parts[j] = passed(grad_of(active[j], cotangent, [clock.now], cost))
    parts_core = passed(parts_core)

    class Wave:
        def __init__(self, count, rows, groups):
            self.count, self.rows, self.groups = count, rows, groups
            self.added = self.came = 0
            self.moved, self.laid = None, None
            self.crossed, self.chunks = [], []

        def far(self, own, core):
            self.pieces = passed(list(far_sum(flags, own, core, self.count, [clock.now])))

        def near(self, own, core):
            self.kept = passed(near_sum(own, core, [clock.now]))

        def lay(self, *chunks):
            for k in chunks:
                mine, theirs, start = self.chunks[k]
                self.laid = lay(
                    flags,
                    k,
                    mine,
                    theirs.array,
                    start,
                    self.rows,
                    self.groups,
                    self.laid,
                    [clock.now],
                )
                self.laid = passed(list(self.laid))

    tall = text_shrink.shape[0]
    shrink = Wave(4, tall // 4, [(0, tall)])
    expand = Wave(4, (width + wide) // 4, [(0, width), (width, width + wide)])
    attn = Wave(4, 3 * wide // 4, [(i * wide, (i + 1) * wide) for i in range(3)])
    groups = links.high // n

    def cross(*waves):
        for wave in waves:
            piece = wave.pieces[len(wave.crossed)]
            wave.crossed.append(Span(links.across(piece), 0, piece.shape[0]))

    def spin(*waves, crossing=()):
        sums, moves, users = [], [], []
        for wave in waves:
            step = wave.added
            if step < n:
                piece = wave.crossed[step * wave.count // 4]
                share = 4 // wave.count
                spans = [Span(piece.array, piece.start + step % share * wave.rows, wave.rows)]
                spans += [] if wave.moved is None else [wave.moved]
                last = step == n - 1
                wave.added += 1
                if last and groups > 1:
                    table = [
                        [(g * n + r) * 2 + l for g in range(groups)]
                        for r in range(n)
                        for l in range(2)
                    ]
                    total = piece_sum(flags, step, wave.kept, spans, [clock.now])
                    total = passed(lax.psum(total, "dp", axis_index_groups=table))
                    moves.append((Span(total, 0, wave.rows), ["z", "y"]))
                    users.append(("move", wave))
                else:
                    sums.append((step, wave.kept, spans, ["z", "y"] if last else ["z"]))
                    users.append(("sum", wave))
            else:
                outs = ["z", "y"] if len(wave.chunks) < n - 1 else ["y"]
                moves.append((wave.moved, outs))
                users.append(("move", wave))
        pending = {}
        for wave in crossing:
            k = len(wave.crossed) + pending.get(id(wave), 0)
            pending[id(wave)] = pending.get(id(wave), 0) + 1
            moves.append((Span(wave.pieces[k], 0, wave.rows), ["x"]))
            users.append(("move", wave))
        users = [u for u in users if u[0] == "sum"] + [u for u in users if u[0] == "move"]
        made, places = turn(flags, sums, moves, [clock.now])
        names = sorted(made)
        made = dict(zip(names, passed([made[name] for name in names]), strict=True))
        sent = {}
        if "z" in made:
            sent["z"] = links.ring(made["z"])
        if "y" in made:
            sent["y"] = links.stream(made["y"])
        if "x" in made:
            sent["x"] = links.across(made["x"])
        for (kind, wave), place in zip(users, places, strict=True):
            if "x" in place:
                wave.crossed.append(Span(sent["x"], place["x"], wave.rows))
            if "z" in place:
                wave.moved = Span(sent["z"], place["z"], wave.rows)
            if "y" in place:
                wave.chunks.append(
                    [made["y"], Span(sent["y"], place["y"], wave.rows), place["y"]]
                )

    def settle(spans):
        arrays = {id(s.array): s.array for s in spans}
        keys = list(arrays)
        fresh = dict(zip(keys, passed([arrays[k] for k in keys], [])[0], strict=True))
        for s in {id(s): s for s in spans}.values():
            s.array = fresh[id(s.array)]

    def arrive(*waves):
        spans = []
        for wave in waves:
            if wave.added < n:
                spans.append(wave.crossed[wave.added * wave.count // 4])
            spans += [] if wave.moved is None else [wave.moved]
        settle(spans)

    def landed(wave, *chunks):
        settle([wave.chunks[k][1] for k in chunks])
        wave.lay(*chunks)

    shrink.far(parts[2], parts_core[3])
    shrink.near(parts[0], parts_core[1])
    shrink_parts[2] = passed(shrink_parts[2])
    cross(shrink)
    shrink_parts.append(links.ring(shrink_parts[2]))
    grads, sums = hidden_behind(
        cotangent,
        active[:2],
        back[:2],
        shrink_slots,
        expand_slots[:2],
        after=[clock.now],
        cost=HEAVY,
    )
    grads, sums = passed(grads, list(sums))
    arrive(shrink)
    shrink_parts[3] = passed(shrink_parts[3])
    shrink_other = passed(join_ring(flags, shrink_parts, [clock.now]))
    shrink_last = links.core(shrink_other)
    spin(shrink, crossing=(shrink,))
    shrink_last = passed(shrink_last)
    shrink_slots += [(shrink_other, 0), (shrink_last, 0)]
    grads_far, (added, second_grad) = hidden_behind(
        cotangent,
        active[2:],
        back[2:],
        shrink_slots[2:],
        expand_slots[2:],
        sums,
        [clock.now],
        HEAVY,
    )
    hidden_grad = [*grads, *passed(grads_far)]
    middle_grad, branch_grad, midnorm_grad, result = second_back(
        middle, gain_second, second_grad, cotangent, added, [clock.now]
    )
    branch_grad = passed(branch_grad)

    def expand_part(j, cost=LIGHT):
        return passed(
            expand_output_grad(
                second_normed, hidden_grad[j], saved[j][2], branch_grad, [clock.now], cost
            )
        )

    parts = {j: expand_part(j) for j in (3, 2)}
    arrive(shrink)
    spin(shrink, crossing=(shrink,))
    parts_core = links.core(parts[3])
    parts.update({1: expand_part(1, HEAVY), 0: expand_part(0)})
    parts_core = passed(parts_core)
    arrive(shrink)
    expand.far(parts[2], parts_core)
    spin(shrink, crossing=(shrink, expand))

    slope_rows = [None] * 4
    first_grad = None
    for step, j in enumerate((3, 2, 1, 0)):
        if step == 0:
            parts_core = links.core(parts[1])
        elif step == 1:
            spin(shrink, expand, crossing=(expand,))
            part_core = links.core(part)
        elif step == 2:
            attn.far(part, part_core)
            spin(shrink, expand, crossing=(expand, attn))
        else:
            spin(shrink, expand, crossing=(expand, attn))
            part_core = links.core(part)
        part, slope_rows[j], first_grad = attention_behind(
            heads_slot,
            branch_grad,
            first_normed,
            attn_slots[j],
            saved[j][:2],
            far,
            first_grad,
            [clock.now],
            HEAVY,
        )
        first_grad, part = passed(first_grad, part)
        if step == 0:
            expand.near(parts[0], passed(parts_core))
        elif step == 1:
            part_core = passed(part_core)
        elif step == 3:
            rows_out, small = first_back(
                heads_slot,
                flags,
                source,
                gain_first,
                first_grad,
                middle_grad,
                midnorm_grad,
                result,
                slope_rows,
                [clock.now],
            )
            small, rows_out = passed(small, list(rows_out))
            attn.near(part, passed(part_core))
        arrive(*((shrink, expand) if step < 3 else (shrink, expand, attn)))

    rows_back = [None] * 4

    def hop(value, moved):
        return passed(add(value, moved, [clock.now]))

    def send_back(k):
        rows_back[k] = links.back_to_rows(rows_out[k], k)

    def sent_back(k):
        rows_back[k] = passed(rows_back[k])

    def under_way(wave, *chunks):
        settle([wave.chunks[k][1] for k in chunks])

    under_way(shrink, 0, 1)
    spin(shrink, expand, attn, crossing=(attn, attn))
    small_moved = links.core(small)
    shrink.lay(0, 1)
    arrive(expand, attn)
    small = hop(small, passed(small_moved))

    spin(expand, attn)
    small_moved = links.across(small)
    arrive(expand, attn)
    under_way(shrink, 2, 3)
    small = hop(small, passed(small_moved))

    spin(expand, attn)
    small_moved = links.level(small, 1)
    send_back(2)
    shrink.lay(2, 3)
    expand.lay(0)
    arrive(expand, attn)
    under_way(expand, 1)
    small = hop(small, passed(small_moved))
    bit = 4
    while bit < links.high:
        small = hop(small, passed(links.level(small, bit)))
        bit *= 2

    spin(expand, attn)
    small_moved = links.level(small, 2)
    send_back(0)
    expand.lay(1)
    arrive(attn)
    sent_back(2)
    under_way(expand, 2)
    small = hop(small, passed(small_moved))

    spin(attn)
    small_other = links.stream(small)
    send_back(3)
    expand.lay(2)
    arrive(attn)
    sent_back(0)

    spin(attn)
    send_back(1)
    arrive(attn)
    under_way(expand, 3)
    under_way(attn, 0)

    spin(attn)
    expand.lay(3)
    attn.lay(0)
    landed(attn, 1)
    small_other = passed(small_other)
    sent_back(3)
    sent_back(1)
    text_result, visual_result, text_input_grad, visual_input_grad = passed(
        *sort_rows(flags, rows_back, [clock.now])
    )
    landed(attn, 2)
    landed(attn, 3)

    text_sh, visual_sh = shrink.laid
    text_ex, text_out, visual_ex, visual_out = expand.laid
    text_at, visual_at = attn.laid[:3], attn.laid[3:]
    text_small = jnp.where(lo == 0, small, small_other)
    visual_small = jnp.where(lo == 0, small_other, small)
    slope_sum = lax.dynamic_slice(
        (text_small + visual_small)[2], (tensor_index * heads_slot,), (heads_slot,)
    )
    return (
        text_result,
        visual_result,
        text_input_grad,
        visual_input_grad,
        text_small[0],
        *(grad.T for grad in text_at),
        text_out,
        text_small[1],
        text_ex,
        text_sh,
        visual_small[0],
        *(grad.T for grad in visual_at),
        visual_out,
        visual_small[1],
        visual_ex,
        visual_sh,
        slope_sum,
    )


def solution(mesh):
    rows = P("dp", "tensor", None)
    split_out = P(None, "tensor")
    split_in = P("tensor", None)
    weights = (P(), split_out, split_out, split_out, split_in, P(), split_out, split_in)
    return jax.shard_map(
        shards,
        mesh=mesh,
        in_specs=(
            rows,
            rows,
            P("dp", None, None),
            P("dp"),
            *weights,
            *weights,
            P("tensor"),
            rows,
            rows,
        ),
        out_specs=(rows, rows, rows, rows, *weights, *weights, P("tensor")),
        check_vma=False,
    )
```

```python
import functools

import jax
import jax.numpy as jnp
from jax import lax
from jax.experimental import pallas as pl
from jax.experimental.pallas import tpu as pltpu
from jax.sharding import PartitionSpec as P

HEAD_DIM = 64
GRID_W = 32
NBIN = 1000
EPSILON = 1e-05
AXES = ("dp", "tensor")
ROWS = (((0,), (0,)), ((), ()))
COLS = (((1,), (1,)), ((), ()))
F32 = jnp.float32
BF16 = jnp.bfloat16
FAR = 1e30
GELU_A = 0.7978845608028654
GELU_B = 0.044715
SCALE = HEAD_DIM ** (-0.5)
FLAG_LO, FLAG_X, FLAG_C, FLAG_HALF, FLAG_RING, FLAG_PLACE, FLAG_TENSOR = range(7)
FLOPS_US = 1_150_000_000
LIGHT, HEAVY = 0.001, 20
VMEM_LIMIT = 16 * 1024 * 1024
IN_VMEM = pl.BlockSpec(memory_space=pltpu.VMEM)
IN_SMEM = pl.BlockSpec(memory_space=pltpu.SMEM)
IN_ANY = pl.BlockSpec(memory_space=pl.ANY)
IN_HBM = pl.BlockSpec(memory_space=pltpu.HBM)


def dot(a, b, dims=None):
    if dims is None:
        return jnp.dot(a, b, preferred_element_type=F32)
    return lax.dot_general(a, b, dims, preferred_element_type=F32)


def kernel_call(body, outs, ins, scalars=0, scratch=(), after=(), far_ins=0, far_outs=0, hbm_outs=0, cost=LIGHT):
    count = len(ins)

    def whole(*refs):
        body(*refs[:count], *refs[count + len(after) :])

    near = [IN_SMEM] * scalars + [IN_VMEM] * (count - scalars - far_ins) + [IN_ANY] * far_ins
    return pl.pallas_call(
        whole,
        out_shape=outs,
        in_specs=near + [IN_ANY] * len(after),
        out_specs=[IN_HBM] * hbm_outs
        + [IN_VMEM] * (len(outs) - hbm_outs - far_outs)
        + [IN_ANY] * far_outs,
        scratch_shapes=list(scratch),
        compiler_params=pltpu.CompilerParams(vmem_limit_bytes=VMEM_LIMIT),
        cost_estimate=pl.CostEstimate(flops=int(FLOPS_US * cost), bytes_accessed=1000, transcendentals=0),
    )(*ins, *after)


def shape(rows, cols, dtype):
    return jax.ShapeDtypeStruct((rows, cols), dtype)


def norm_parts(values):
    center = values - jnp.mean(values, axis=-1, keepdims=True)
    spread = jnp.mean(center * center, axis=-1, keepdims=True)
    scale = lax.rsqrt(spread + EPSILON)
    return center * scale, scale


def norm_back(normed, scale, gain, grad):
    inner = grad * gain
    mean_inner = jnp.mean(inner, axis=-1, keepdims=True)
    mean_both = jnp.mean(inner * normed, axis=-1, keepdims=True)
    return scale * (inner - mean_inner - normed * mean_both)


def first_norm_body(gain_ref, *refs):
    blocks, (source_ref, out_ref) = refs[:-2], refs[-2:]
    rows = source_ref.shape[0] // len(blocks)
    for k, block in enumerate(blocks):
        at = slice(k * rows, (k + 1) * rows)
        values = block[:rows, :]
        source_ref[at, :] = values
        normed, unused = norm_parts(values.astype(F32))
        out_ref[at, :] = (normed * gain_ref[...]).astype(BF16)


def first_norm(gain, blocks, rows, after):
    outs = [shape(rows * len(blocks), blocks[0].shape[1], BF16)] * 2
    return kernel_call(first_norm_body, outs, [gain, *blocks], after=after, cost=HEAVY)


def second_norm_body(source_ref, branch_ref, gain_ref, middle_ref, out_ref):
    middle = source_ref[...].astype(F32) + branch_ref[...]
    middle_ref[...] = middle
    normed, unused = norm_parts(middle)
    out_ref[...] = (normed * gain_ref[...]).astype(BF16)


def second_norm(source, branch, gain, after):
    outs = [shape(*source.shape, F32), shape(*source.shape, BF16)]
    return kernel_call(second_norm_body, outs, [source, branch, gain], after=after)


def second_back_body(
    middle_ref, gain_ref, grad_ref, cot_ref, added_ref, mid_ref, branch_ref, gain_out, result_ref
):
    middle = middle_ref[...]
    normed, scale = norm_parts(middle)
    grad = grad_ref[...]
    total = cot_ref[...].astype(F32) + norm_back(normed, scale, gain_ref[...], grad)
    mid_ref[...] = total
    branch_ref[...] = total.astype(BF16)
    gain_out[...] = jnp.sum(grad * normed, axis=0, keepdims=True)
    result_ref[...] = (middle + added_ref[...]).astype(BF16)


def second_back(middle, gain, grad, cotangent, added, after):
    rows, cols = middle.shape
    outs = [shape(rows, cols, F32), shape(rows, cols, BF16), shape(1, cols, F32)]
    outs.append(shape(rows, cols, BF16))
    ins = [middle, gain, grad, cotangent, added]
    return kernel_call(second_back_body, outs, ins, after=after)


def first_back_body(
    heads, flags, source_ref, gain_ref, grad_ref, mid_ref, midnorm_ref, result_ref, *refs
):
    slopes, blocks, small_ref = refs[:4], refs[4:8], refs[8]
    normed, scale = norm_parts(source_ref[...].astype(F32))
    grad = grad_ref[...]
    out = (mid_ref[...] + norm_back(normed, scale, gain_ref[...], grad)).astype(BF16)
    rows = result_ref.shape[0] // 4
    for k in range(4):
        blocks[k][:rows, :] = result_ref[k * rows : (k + 1) * rows, :]
        blocks[k][rows:, :] = out[k * rows : (k + 1) * rows, :]
    small_ref[...] = jnp.zeros_like(small_ref)
    small_ref[0:1, :] = jnp.sum(grad * normed, axis=0, keepdims=True)
    small_ref[1:2, :] = midnorm_ref[...]
    lane = lax.broadcasted_iota(jnp.int32, midnorm_ref.shape, 1)
    row = jnp.zeros(midnorm_ref.shape, F32)
    for j in range(4):
        sums = -jnp.sum(slopes[j][...], axis=1, keepdims=True)
        for h in range(heads):
            spot = (flags[FLAG_TENSOR] ^ j) * heads + h
            row = row + jnp.where(lane == spot, sums[h : h + 1, :], 0.0)
    small_ref[2:3, :] = row


def first_back(heads, flags, source, gain, grad, middle_grad, midnorm_grad, result, slope_rows, after):
    rows, cols = source.shape
    outs = [shape(rows // 2, cols, BF16)] * 4 + [shape(8, cols, F32)]
    ins = [flags, source, gain, grad, middle_grad, midnorm_grad, result, *slope_rows]
    out = kernel_call(functools.partial(first_back_body, heads), outs, ins, 1, after=after)
    return out[:4], out[4]


def each(flag, one, other):
    pl.when(flag == 0)(one)
    pl.when(flag != 0)(other)


def info_body(flags, counts, boxes_ref, info_ref):
    info_ref[...] = jnp.zeros_like(info_ref)
    info_ref[0:2, :] = boxes_ref[flags[FLAG_X]]
    info_ref[2:3, :] = jnp.full((1, info_ref.shape[1]), counts[flags[FLAG_X]], jnp.int32)


def page_info(flags, counts, boxes, after):
    outs = [shape(8, boxes.shape[2], jnp.int32)]
    return kernel_call(info_body, outs, [flags, counts, boxes], 2, after=after)[0]


def distance_body(flags, own_ref, theirs_ref, far_ref, info):
    tokens = far_ref.shape[0]
    block = tokens // 4
    mine = 1 - (flags[FLAG_LO] ^ flags[FLAG_C])
    text = 1 - flags[FLAG_LO]
    share = text.astype(F32)
    for k in range(4):
        at = slice(k * block, (k + 1) * block)
        shard = flags[FLAG_PLACE] ^ k
        there = pl.ds(pl.multiple_of(shard * block, block), block)
        boxes = own_ref[:, there] * mine + theirs_ref[:, there] * (1 - mine)
        index = lax.broadcasted_iota(jnp.int32, (1, block), 1) + shard * block
        column = (index & (GRID_W - 1)).astype(F32)
        line = (index >> (GRID_W.bit_length() - 1)).astype(F32)
        text_place = boxes[0:2, :].astype(F32) / NBIN
        coord_x = text_place[0:1, :] * share + (column + 0.5) / GRID_W * (1.0 - share)
        coord_y = text_place[1:2, :] * share + (line + 0.5) / (tokens // GRID_W) * (1.0 - share)
        count = boxes[2:3, :] * text + tokens * (1 - text)
        info[...] = jnp.zeros_like(info) if k == 0 else info[...]
        info[0:1, at] = coord_x
        info[1:2, at] = coord_y
        info[2:3, at] = jnp.where(index < count, 0.0, 1.0)
    turned = info[...].T
    delta_x = turned[:, 0:1] - info[0:1, :]
    delta_y = turned[:, 1:2] - info[1:2, :]
    distance = jnp.sqrt(delta_x * delta_x + delta_y * delta_y)
    far_ref[...] = jnp.where(turned[:, 2:3] > 0.5, FAR, distance)


def distances(flags, own, theirs, after=()):
    tokens = own.shape[1]
    scratch = [pltpu.VMEM((8, tokens), F32)]
    return kernel_call(
        distance_body, [shape(tokens, tokens, F32)], [flags, own, theirs], 1, scratch, after
    )[0]


def both(a, b):
    return (a.astype(F32) + b.astype(F32)).astype(BF16)


def near_body(own_ref, core_ref, out_ref):
    out_ref[...] = both(own_ref[...], core_ref[...])


def near_sum(own, core, after):
    return kernel_call(near_body, [shape(*own.shape, BF16)], [own, core], after=after)[0]


def far_body(flags, own_ref, core_ref, *pieces):
    rows = own_ref.shape[0] // 4
    share = 4 // len(pieces)
    for i in range(4):
        at = pl.ds(pl.multiple_of(((flags[FLAG_RING] + 3 - i) & 3) * rows, rows), rows)
        place = slice(i % share * rows, (i % share + 1) * rows)
        pieces[i // share][place, :] = both(own_ref[at, :], core_ref[at, :])


def far_sum(flags, own, core, count, after):
    rows, cols = own.shape
    outs = [shape(rows // count, cols, BF16)] * count
    return kernel_call(far_body, outs, [flags, own, core], 1, after=after)


class Span:
    def __init__(self, array, start, rows):
        self.array, self.start, self.rows = array, start, rows


def turn_body(plan, flags, *refs):
    ins, outs = refs[: plan["ins"]], refs[plan["ins"] :]

    def rows_of(span):
        index, start, rows = span
        return ins[index][start : start + rows, :]

    for step, near, spans, places in plan["sums"]:
        rows = spans[0][2]
        at = pl.ds(pl.multiple_of(((flags[FLAG_RING] + 3 - step) & 3) * rows, rows), rows)
        total = ins[near][at, :].astype(F32)
        for span in spans:
            total = total + rows_of(span).astype(F32)
        total = total.astype(BF16)
        for out, start in places:
            outs[out][start : start + rows, :] = total
    for span, places in plan["moves"]:
        for out, start in places:
            outs[out][start : start + span[2], :] = rows_of(span)


def turn(flags, sums, moves, after):
    ins, index = [flags], {}

    def place_of(array):
        if id(array) not in index:
            index[id(array)] = len(ins) - 1
            ins.append(array)
        return index[id(array)]

    def static(span):
        return (place_of(span.array), span.start, span.rows)

    heights = {}

    def places_of(outs, rows):
        places = []
        for out in outs:
            places.append((out, heights.get(out, 0)))
            heights[out] = heights.get(out, 0) + rows
        return places

    plan = {"sums": [], "moves": []}
    for step, near, spans, outs in sums:
        rows = spans[0].rows
        plan["sums"].append(
            (step, place_of(near), [static(s) for s in spans], places_of(outs, rows))
        )
    for span, outs in moves:
        plan["moves"].append((static(span), places_of(outs, span.rows)))
    plan["ins"] = len(ins) - 1
    order = sorted(heights)
    number = {out: i for i, out in enumerate(order)}
    for kind in ("sums", "moves"):
        plan[kind] = [
            (*item[:-1], [(number[out], start) for out, start in item[-1]]) for item in plan[kind]
        ]
    cols = ins[1].shape[1]
    shapes = [shape(heights[out], cols, BF16) for out in order]
    body = functools.partial(turn_body, plan)
    made = kernel_call(body, shapes, ins, 1, after=after)
    places = [
        {order[out]: start for out, start in item[-1]} for kind in ("sums", "moves") for item in plan[kind]
    ]
    return dict(zip(order, made, strict=True)), places


def piece_sum(flags, step, near, spans, after):
    made, places = turn(flags, [(step, near, spans, [0])], [], after)
    return made[0]


def grad_body(left_ref, right_ref, out_ref):
    out_ref[...] = dot(left_ref[...], right_ref[...], ROWS).astype(BF16)


def grad_of(left, right, after, cost=LIGHT):
    outs = [shape(left.shape[1], right.shape[1], BF16)]
    return kernel_call(grad_body, outs, [left, right], after=after, cost=cost)[0]


def add_body(left_ref, right_ref, out_ref):
    out_ref[...] = left_ref[...] + right_ref[...]


def add(left, right, after):
    return kernel_call(add_body, [shape(*left.shape, left.dtype)], [left, right], after=after)[0]


def expand_output_body(normed_ref, hidden_ref, attended_ref, branch_ref, out_ref):
    rows = normed_ref.shape[1]
    out_ref[:rows, :] = dot(normed_ref[...], hidden_ref[...], ROWS).astype(BF16)
    out_ref[rows:, :] = dot(attended_ref[...], branch_ref[...], ROWS).astype(BF16)


def expand_output_grad(normed, hidden_grad, attended, branch_grad, after, cost=LIGHT):
    rows = normed.shape[1] + attended.shape[1]
    outs = [shape(rows, normed.shape[1], BF16)]
    ins = [normed, hidden_grad, attended, branch_grad]
    return kernel_call(expand_output_body, outs, ins, after=after, cost=cost)[0]


def join_body(heights, flags, first_ref, second_ref, out_ref):
    start = low = 0
    for height in heights:
        for ref, side in ((first_ref, flags[FLAG_HALF]), (second_ref, 1 - flags[FLAG_HALF])):
            at = pl.multiple_of(low + side * height, height)
            out_ref[pl.ds(at, height), :] = ref[start : start + height, :]
        start += height
        low += 2 * height
    rest = out_ref.shape[0] - low
    if rest:
        out_ref[low:, :] = first_ref[start : start + rest, :]


def join(flags, first, second, heights, after):
    rows = first.shape[0] + sum(heights)
    outs = [shape(rows, first.shape[1], BF16)]
    body = functools.partial(join_body, heights)
    return kernel_call(body, outs, [flags, first, second], 1, after=after)[0]


def join_ring_body(flags, *refs):
    pieces, out_ref = refs[:-1], refs[-1]
    rows = pieces[0].shape[0]
    for r, piece in enumerate(pieces):
        at = pl.multiple_of(((flags[FLAG_RING] + 4 - r) & 3) * rows, rows)
        out_ref[pl.ds(at, rows), :] = piece[...]


def join_ring(flags, pieces, after):
    rows, cols = pieces[0].shape
    outs = [shape(4 * rows, cols, BF16)]
    return kernel_call(join_ring_body, outs, [flags, *pieces], 1, after=after)[0]


def lay_body(groups, r, start, flags, *refs):
    size = len(groups)
    chunks, refs = refs[:2], refs[2:]
    outs, (held, sems) = refs[-2 * size - 2 : -2], refs[-2:]
    rows = held.shape[1]
    spot = (flags[FLAG_RING] + 4 - r) & 3
    waits = []
    for side in range(2):
        slot, sem = held.at[side], sems.at[side]
        slot[...] = chunks[side][start : start + rows, :].astype(F32)
        stream = flags[FLAG_LO] ^ side
        for p in range(4):
            for g, (low, high) in enumerate(groups):
                first, last = max(p * rows, low), min((p + 1) * rows, high)
                if first >= last:
                    continue
                piece = slot.at[pl.ds(first - p * rows, last - first)]
                place = pl.ds(first - low, last - first)
                for s in range(2):
                    copy = pltpu.make_async_copy(piece, outs[s * size + g].at[place], sem)
                    pl.when((spot == p) & (stream == s))(copy.start)
        waits.append(pltpu.make_async_copy(slot, outs[0].at[pl.ds(0, rows)], sem))
    for copy in waits:
        copy.wait()


def lay(flags, r, mine, theirs, start, rows, groups, laid, after, cost):
    cols = mine.shape[1]
    outs = [shape(high - low, cols, F32) for low, high in groups] * 2
    ins = [flags, mine, theirs]
    first = len(ins)
    body = functools.partial(lay_body, groups, r, start)
    laid = [] if laid is None else list(laid)

    def whole(*refs):
        body(*refs[:first], *refs[first + len(laid) + len(after) :])

    return pl.pallas_call(
        whole,
        out_shape=outs,
        in_specs=[IN_SMEM, IN_VMEM, IN_VMEM] + [IN_ANY] * (len(laid) + len(after)),
        out_specs=[IN_ANY] * len(outs),
        scratch_shapes=[pltpu.VMEM((2, rows, cols), F32), pltpu.SemaphoreType.DMA((2,))],
        input_output_aliases={first + i: i for i in range(len(laid))},
        compiler_params=pltpu.CompilerParams(vmem_limit_bytes=VMEM_LIMIT),
        cost_estimate=pl.CostEstimate(
            flops=int(FLOPS_US * cost), bytes_accessed=1000, transcendentals=0
        ),
    )(*ins, *laid, *after)


def sort_body(flags, *refs):
    parts, outs, sems = refs[:4], refs[4:8], refs[8]
    rows = outs[0].shape[1]
    copies = []
    for k in range(4):
        stream = flags[FLAG_C] ^ (k & 1)
        page = flags[FLAG_X] ^ (k >> 1)
        for n in range(2):
            piece = parts[k].at[pl.ds(n * rows, rows)]
            sem = sems.at[2 * k + n]

            def move(out, piece=piece, page=page, sem=sem):
                pltpu.make_async_copy(piece, out.at[page], sem).start()

            each(
                stream,
                functools.partial(move, outs[2 * n]),
                functools.partial(move, outs[2 * n + 1]),
            )
            copies.append(pltpu.make_async_copy(piece, outs[0].at[0], sem))
    for copy in copies:
        copy.wait()


def sort_rows(flags, parts, after=()):
    rows, cols = parts[0].shape
    outs = [jax.ShapeDtypeStruct((2, rows // 2, cols), BF16)] * 4
    scratch = [pltpu.SemaphoreType.DMA((8,))]
    return kernel_call(sort_body, outs, [flags, *parts], 1, scratch, after, far_ins=4, far_outs=4)


def slope_of(w_ref, wide, h):
    rows = [w_ref[4 * wide + i : 4 * wide + i + 1, h : h + 1].astype(F32) for i in range(3)]
    return rows[0] + rows[1] + rows[2]


def attention_ahead_body(heads, block, first, normed_ref, w_ref, far_ref, *refs):
    branch_ref, refs = (None, refs) if first else (refs[0], refs[1:])
    kept, (out_ref, *held, sems) = refs[:3], refs[3:]
    qkv_ref, attended_ref, log_ref = held
    keep = [pltpu.make_async_copy(held[i], kept[i], sems.at[i]) for i in range(3)]
    tokens = normed_ref.shape[0]
    wide = heads * HEAD_DIM
    qkv_ref[...] = dot(normed_ref[...], w_ref[: 3 * wide, :], COLS).astype(BF16)
    log_ref[...] = jnp.zeros_like(log_ref)
    keep[0].start()
    for h in range(heads):
        col = slice(h * HEAD_DIM, (h + 1) * HEAD_DIM)
        keys = qkv_ref[:, wide + col.start : wide + col.stop]
        values_t = qkv_ref[:, 2 * wide + col.start : 2 * wide + col.stop].T
        slope = slope_of(w_ref, wide, h)
        for b in range(tokens // block):
            rows = slice(b * block, (b + 1) * block)
            scores = dot(keys, qkv_ref[rows, col], COLS) * SCALE - slope * far_ref[:, rows]
            highest = jnp.max(scores, axis=0, keepdims=True)
            exponent = jnp.exp(scores - highest)
            totals = jnp.sum(exponent, axis=0, keepdims=True)
            soft_weights = (exponent * (1.0 / totals)).astype(BF16)
            log_ref[h : h + 1, rows] = highest + jnp.log(totals)
            attended_ref[rows, col] = dot(values_t, soft_weights).T.astype(BF16)
    keep[1].start()
    keep[2].start()
    part = dot(attended_ref[...], w_ref[3 * wide : 4 * wide, :])
    out_ref[...] = part if first else branch_ref[...] + part
    for copy in keep:
        copy.wait()


def attention_ahead(heads, normed, w, far, branch, after=(), cost=LIGHT):
    rows, cols = normed.shape
    wide = heads * HEAD_DIM
    ins = [normed, w, far] + ([] if branch is None else [branch])
    outs = [shape(rows, 3 * wide, BF16), shape(rows, wide, BF16), shape(8, rows, F32)]
    scratch = [pltpu.VMEM(out.shape, out.dtype) for out in outs] + [pltpu.SemaphoreType.DMA((3,))]
    outs.append(shape(rows, cols, F32))
    body = functools.partial(attention_ahead_body, heads, min(256, rows), branch is None)
    return kernel_call(body, outs, ins, 0, scratch, after, hbm_outs=3, cost=cost)


def attention_behind_body(
    heads, block, first, branch_ref, normed_ref, w_ref, qkv_ref, log_ref, far_ref, *refs
):
    grad_ref = None if first else refs[0]
    weight_grad, out_slope, out_ref, out_qkv, attended_grad, keys_sum, values_sum = (
        refs if first else refs[1:]
    )
    tokens = branch_ref.shape[0]
    wide = heads * HEAD_DIM
    attended_grad[...] = dot(branch_ref[...], w_ref[3 * wide : 4 * wide, :], COLS).astype(BF16)
    for h in range(heads):
        col = slice(h * HEAD_DIM, (h + 1) * HEAD_DIM)
        key_col = slice(wide + col.start, wide + col.stop)
        value_col = slice(2 * wide + col.start, 2 * wide + col.stop)
        keys = qkv_ref[:, key_col]
        values = qkv_ref[:, value_col]
        keys_t = keys.T
        slope = slope_of(w_ref, wide, h)
        for b in range(tokens // block):
            rows = slice(b * block, (b + 1) * block)
            queries = qkv_ref[rows, col]
            grad = attended_grad[rows, col]
            far = far_ref[:, rows]
            scores = dot(keys, queries, COLS) * SCALE - slope * far
            probs = jnp.exp(scores - log_ref[h : h + 1, rows])
            values_part = dot(probs.astype(BF16), grad)
            probs_grad = dot(values, grad, COLS)
            mean = jnp.sum(probs * probs_grad, axis=0, keepdims=True)
            scores_grad = probs * (probs_grad - mean)
            out_slope[h : h + 1, rows] = jnp.sum(scores_grad * far, axis=0, keepdims=True)
            scores_grad = scores_grad.astype(BF16)
            keys_part = dot(scores_grad, queries)
            if b == 0:
                keys_sum[...] = keys_part
                values_sum[...] = values_part
            else:
                keys_sum[...] += keys_part
                values_sum[...] += values_part
            queries_grad = dot(keys_t, scores_grad) * SCALE
            out_qkv[rows, col] = queries_grad.T.astype(BF16)
        out_qkv[:, key_col] = (keys_sum[...] * SCALE).astype(BF16)
        out_qkv[:, value_col] = values_sum[...].astype(BF16)
    part = dot(out_qkv[...], w_ref[: 3 * wide, :])
    weight_grad[...] = dot(out_qkv[...], normed_ref[...], ROWS).astype(BF16)
    out_ref[...] = part if first else grad_ref[...] + part


def attention_behind(heads, branch_grad, normed, w, kept, far, grad, after=(), cost=LIGHT):
    rows, cols = branch_grad.shape
    wide = heads * HEAD_DIM
    ins = [branch_grad, normed, w, *kept, far] + ([] if grad is None else [grad])
    outs = [shape(3 * wide, cols, BF16), shape(8, rows, F32), shape(rows, cols, F32)]
    scratch = [pltpu.VMEM((rows, 3 * wide), BF16), pltpu.VMEM((rows, wide), BF16)] + [pltpu.VMEM((rows, HEAD_DIM), F32)] * 2
    body = functools.partial(attention_behind_body, heads, min(256, rows), grad is None)
    return kernel_call(body, outs, ins, 0, scratch, after, cost=cost)


def gelu_both(values):
    square = values * values
    bend = jnp.tanh(GELU_A * values * (1.0 + GELU_B * square))
    half = 0.5 * (1.0 + bend)
    slope = half + 0.5 * values * (1.0 - bend * bend) * (
        GELU_A + (3.0 * GELU_A * GELU_B) * square
    )
    return values * half, slope


def hidden_ahead_body(count, blocks, starts, normed_ref, *refs):
    weights, refs = refs[:count], refs[count:]
    parts, outs, held = refs[:blocks], refs[blocks:-1], refs[-1]
    tokens, cols = normed_ref.shape
    for k in range(blocks):
        rows = tokens // blocks
        outs[2 * count][k * rows : (k + 1) * rows, :] = parts[k][parts[k].shape[0] - rows :, :]
    step = 32
    for j in range(count):
        held[...] = dot(normed_ref[...], weights[j][starts[j] : starts[j] + cols, :])
        for b in range(tokens // step):
            rows = slice(b * step, (b + 1) * step)
            active, back = gelu_both(held[rows, :])
            outs[2 * j][rows, :] = active.astype(BF16)
            outs[2 * j + 1][rows, :] = back.astype(BF16)


def hidden_ahead(normed, weights, parts=(), after=(), cost=LIGHT):
    rows, cols = normed.shape
    arrays, starts = zip(*weights, strict=True)
    count, wide = len(weights), arrays[0].shape[1]
    outs = [shape(rows, wide, BF16)] * (2 * count)
    if parts:
        outs.append(shape(rows, cols, BF16))
    body = functools.partial(hidden_ahead_body, count, len(parts), starts)
    scratch = [pltpu.VMEM((rows, wide), F32)]
    out = kernel_call(body, outs, [normed, *arrays, *parts], 0, scratch, after, cost=cost)
    return out[0 : 2 * count : 2], out[1 : 2 * count : 2], out[-1]


def hidden_behind_body(count, first, starts, cot_ref, *refs):
    active, back, shrink, expand = (refs[count * i : count * (i + 1)] for i in range(4))
    refs = refs[4 * count :]
    before, refs = ((), refs) if first else (refs[:2], refs[2:])
    grads, (added_ref, out_ref) = refs[:count], refs[count:]
    cols, wide = cot_ref.shape[1], active[0].shape[1]
    for j in range(count):
        down = slice(starts[0][j], starts[0][j] + wide)
        up = slice(starts[1][j], starts[1][j] + cols)
        part = dot(active[j][...], shrink[j][down, :])
        if j == 0:
            added_ref[...] = part if first else before[0][...] + part
        else:
            added_ref[...] += part
        active_grad = dot(cot_ref[...], shrink[j][down, :], COLS)
        grads[j][...] = (active_grad * back[j][...].astype(F32)).astype(BF16)
        part = dot(grads[j][...], expand[j][up, :], COLS)
        if j == 0:
            out_ref[...] = part if first else before[1][...] + part
        else:
            out_ref[...] += part


def hidden_behind(cotangent, active, back, shrink, expand, before=(), after=(), cost=LIGHT):
    rows, cols = cotangent.shape
    count, wide = len(active), active[0].shape[1]
    downs, ups = zip(*shrink, strict=True), zip(*expand, strict=True)
    (downs, down_starts), (ups, up_starts) = downs, ups
    outs = [shape(rows, wide, BF16)] * count + [shape(rows, cols, F32)] * 2
    body = functools.partial(hidden_behind_body, count, not before, (down_starts, up_starts))
    ins = [cotangent, *active, *back, *downs, *ups, *before]
    out = kernel_call(body, outs, ins, after=after, cost=cost)
    return out[:count], out[count:]


class Links:
    def __init__(self, pairs):
        self.pairs = pairs
        self.high = pairs // 2
        self.ring_size = 4

    def send(self, value, move):
        table = []
        for dp in range(self.pairs):
            for tensor in range(4):
                hi, lo, x, c = move(dp // 2, dp % 2, tensor // 2, tensor % 2)
                table.append((dp * 4 + tensor, (hi * 2 + lo) * 4 + x * 2 + c))
        return lax.ppermute(value, AXES, table)

    def core(self, value):
        return self.send(value, lambda hi, lo, x, c: (hi, lo, x, 1 - c))

    def across(self, value):
        return self.send(value, lambda hi, lo, x, c: (hi, lo, 1 - x, c))

    def stream(self, value):
        return self.send(value, lambda hi, lo, x, c: (hi, 1 - lo, x, c))

    def level(self, value, bit):
        return self.send(value, lambda hi, lo, x, c: (hi ^ bit, lo, x, c))

    def ring(self, value):
        after = (1, 3, 0, 2)
        return self.send(value, lambda hi, lo, x, c: (hi // 4 * 4 + after[hi % 4], lo, x, c))

    def out_to_page(self, value, k):
        return self.send(value, lambda hi, lo, x, c: (hi, c ^ (k & 1), x ^ (k >> 1), lo))

    def back_to_rows(self, value, k):
        return self.send(value, lambda hi, lo, x, c: (hi, c, x ^ (k >> 1), lo ^ (k & 1)))


def add_low(a, b):
    return (a.astype(F32) + b.astype(F32)).astype(BF16)


class Clock:
    def __init__(self, start):
        self.now = start

    def passed(self, *values):
        values, self.now = lax.optimization_barrier((list(values), self.now))
        return values[0] if len(values) == 1 else values


def shards(
    text_input,
    visual_input,
    text_boxes,
    text_count,
    text_prenorm,
    text_query,
    text_key,
    text_value,
    text_output,
    text_midnorm,
    text_expand,
    text_shrink,
    visual_prenorm,
    visual_query,
    visual_key,
    visual_value,
    visual_output,
    visual_midnorm,
    visual_expand,
    visual_shrink,
    slopes,
    text_cotangent,
    visual_cotangent,
):
    dp_index = lax.axis_index("dp")
    tensor_index = lax.axis_index("tensor")
    hi, lo = dp_index // 2, dp_index % 2
    x, c = tensor_index // 2, tensor_index % 2
    links = Links(lax.axis_size("dp"))
    heads_slot = slopes.shape[0]
    half = hi % 2
    n = links.ring_size
    spot = (hi % n) ^ ((hi % n) >> 1)
    flags = jnp.stack([lo, x, c, half, spot, 2 * x + lo, tensor_index]).astype(jnp.int32)
    gain_first, gain_second = (
        jnp.where(lo == 0, text, visual).astype(F32)[None]
        for text, visual in ((text_prenorm, visual_prenorm), (text_midnorm, visual_midnorm))
    )

    def half_rows(shard):
        return lax.dynamic_slice_in_dim(shard, half * (shard.shape[0] // 2), shard.shape[0] // 2)

    def page_blocks(text_rows, visual_rows):
        blocks = []
        for k in range(4):
            parts = [
                lax.dynamic_index_in_dim(rows, x ^ (k >> 1), 0, False)
                for rows in (text_rows, visual_rows)
            ]
            blocks.append(jnp.where((c ^ (k & 1)) == 0, *parts))
        return blocks

    def to_page(blocks, chosen=(3, 2, 1, 0)):
        return [links.out_to_page(blocks[k], k) for k in chosen][::-1]

    def low(value):
        return value.astype(BF16)

    def add_low(a, b):
        return low(a.astype(F32) + b.astype(F32))

    clock = Clock(slopes)
    passed = clock.passed

    text_attn = [text_query.T, text_key.T, text_value.T, text_output]
    visual_attn = [visual_query.T, visual_key.T, visual_value.T, visual_output]
    slope_parts = []
    rest = slopes
    for i in range(3):
        slope_parts.append(low(rest))
        rest = rest - slope_parts[i].astype(F32)
    wide, width = text_output.shape
    tail = jnp.zeros((16, width), BF16).at[:3, :heads_slot].set(jnp.stack(slope_parts))
    heights = [2 * wide]
    attn_own = jnp.concatenate(
        [
            jnp.where(
                lo == 0,
                jnp.concatenate([text_query.T, text_key.T, text_value.T, text_output]),
                jnp.concatenate([visual_query.T, visual_key.T, visual_value.T, visual_output]),
            ),
            tail,
        ]
    )

    attn_half = passed(jnp.concatenate([half_rows(attn_own[: 4 * wide]), tail]))
    attn_first = links.across(attn_half)
    text_rows, visual_rows = passed(text_input, visual_input)
    in_blocks = page_blocks(text_rows, visual_rows)
    cot_parts = page_blocks(text_cotangent, visual_cotangent)
    in_blocks = [
        jnp.concatenate([in_blocks[k], cot_parts[k]]) if k < 2 else in_blocks[k] for k in range(4)
    ]
    in_blocks = to_page(passed(in_blocks))
    info = passed(page_info(flags, text_count, text_boxes, [clock.now]))
    info_theirs = links.stream(info)
    expand_own = jnp.where(lo == 0, text_expand, visual_expand)
    shrink_own = jnp.where(lo == 0, text_shrink, visual_shrink)
    expand_half = half_rows(expand_own)
    info_theirs = passed(info_theirs)
    far = passed(distances(flags, info, info_theirs, [clock.now]))
    expand_half, cot_parts, gain_first, gain_second = passed(
        expand_half, cot_parts, gain_first, gain_second
    )
    attn_first = passed(attn_first)
    attn_second = links.level(attn_first, 1)
    in_blocks = passed(in_blocks)
    attn_own, expand_half, cot_parts = passed(attn_own, expand_half, cot_parts)
    attn_core = links.core(attn_own)
    expand_first = links.across(expand_half)
    expand_core = links.core(expand_own)
    source, first_normed = passed(*first_norm(gain_first, in_blocks, text_input.shape[1], [clock.now]))

    saved = [None] * 4

    def ahead(j, weights, branch, cost=LIGHT):
        qkv, attended, log_total, branch = attention_ahead(
            heads_slot, first_normed, weights, far, branch, [clock.now], cost
        )
        saved[j] = (qkv, log_total, attended)
        return passed(branch)

    branch = ahead(0, attn_own, None)
    attn_core = passed(attn_core)
    branch = ahead(1, attn_core, branch)
    quarter = shrink_own.shape[0] // 4
    shrink_part = passed(lax.dynamic_slice_in_dim(shrink_own, spot * quarter, quarter))
    attn_second = passed(attn_second)
    expand_first, expand_core = passed(expand_first, expand_core)
    attn_other = passed(join(flags, attn_first, attn_second, heights, [clock.now]))

    expand_second = links.level(expand_first, 1)
    attn_last = links.core(attn_other)
    cot_parts, shrink_part = passed(cot_parts, shrink_part)
    shrink_parts = [links.across(shrink_part)]
    cot_far = to_page(cot_parts, (3, 2))
    branch = ahead(2, attn_other, branch, HEAVY)
    attn_last = passed(attn_last)
    branch = ahead(3, attn_last, branch)
    attn_slots = [attn_own, attn_core, attn_other, attn_last]
    expand_second = passed(expand_second)
    shrink_parts[0] = passed(shrink_parts[0])
    cot_far = passed(cot_far)
    expand_other = passed(join(flags, expand_first, expand_second, [width // 2], [clock.now]))

    shrink_own = passed(shrink_own)
    expand_last = links.core(expand_other)
    shrink_parts.append(links.ring(shrink_parts[0]))
    shrink_core = links.core(shrink_own)
    middle, second_normed = second_norm(source, branch, gain_second, [clock.now])
    second_normed = passed(second_normed)
    active, back = [], []
    for j in range(4):
        weights = (expand_own, expand_core, expand_other, expand_last)[j]
        some, other, joined = hidden_ahead(
            second_normed,
            [(weights, 0)],
            [*in_blocks[:2], *cot_far] if j == 0 else [],
            [clock.now],
            HEAVY if j == 0 else LIGHT,
        )
        active += [passed(some[0])]
        back += other
        if j == 0:
            cotangent = passed(joined)
        if j == 1:
            expand_last = passed(expand_last)
    expand_slots = [(w, 0) for w in (expand_own, expand_core, expand_other, expand_last)]
    parts, parts_core = {}, {}
    for j in (3, 1):
        parts[j] = passed(grad_of(active[j], cotangent, [clock.now]))
    shrink_parts[1], shrink_core = passed(shrink_parts[1], shrink_core)
    for j in (3, 1):
        parts_core[j] = links.core(parts[j])
    shrink_parts.append(links.ring(shrink_parts[1]))
    shrink_slots = [(shrink_own, 0), (shrink_core, 0)]
    for j, cost in ((2, HEAVY), (0, LIGHT)):
        parts[j] = passed(grad_of(active[j], cotangent, [clock.now], cost))
    parts_core = passed(parts_core)

    class Wave:
        def __init__(self, count, rows, groups):
            self.count, self.rows, self.groups = count, rows, groups
            self.added = self.came = 0
            self.moved, self.laid = None, None
            self.crossed, self.chunks = [], []

        def far(self, own, core):
            self.pieces = passed(list(far_sum(flags, own, core, self.count, [clock.now])))

        def near(self, own, core):
            self.kept = passed(near_sum(own, core, [clock.now]))

        def lay(self, *chunks, cost=LIGHT):
            for k in chunks:
                mine, theirs, start = self.chunks[k]
                self.laid = lay(
                    flags,
                    k,
                    mine,
                    theirs.array,
                    start,
                    self.rows,
                    self.groups,
                    self.laid,
                    [clock.now],
                    cost,
                )
                self.laid = passed(list(self.laid))

    tall = text_shrink.shape[0]
    shrink = Wave(4, tall // 4, [(0, tall)])
    expand = Wave(4, (width + wide) // 4, [(0, width), (width, width + wide)])
    attn = Wave(4, 3 * wide // 4, [(i * wide, (i + 1) * wide) for i in range(3)])
    groups = links.high // n

    def cross(*waves):
        for wave in waves:
            piece = wave.pieces[len(wave.crossed)]
            wave.crossed.append(Span(links.across(piece), 0, piece.shape[0]))

    def spin(*waves, crossing=()):
        sums, moves, users = [], [], []
        for wave in waves:
            step = wave.added
            if step < n:
                piece = wave.crossed[step * wave.count // 4]
                share = 4 // wave.count
                spans = [Span(piece.array, piece.start + step % share * wave.rows, wave.rows)]
                spans += [] if wave.moved is None else [wave.moved]
                last = step == n - 1
                wave.added += 1
                if last and groups > 1:
                    table = [
                        [(g * n + r) * 2 + l for g in range(groups)]
                        for r in range(n)
                        for l in range(2)
                    ]
                    total = piece_sum(flags, step, wave.kept, spans, [clock.now])
                    total = passed(lax.psum(total, "dp", axis_index_groups=table))
                    moves.append((Span(total, 0, wave.rows), ["z", "y"]))
                    users.append(("move", wave))
                else:
                    sums.append((step, wave.kept, spans, ["z", "y"] if last else ["z"]))
                    users.append(("sum", wave))
            else:
                outs = ["z", "y"] if len(wave.chunks) < n - 1 else ["y"]
                moves.append((wave.moved, outs))
                users.append(("move", wave))
        pending = {}
        for wave in crossing:
            k = len(wave.crossed) + pending.get(id(wave), 0)
            pending[id(wave)] = pending.get(id(wave), 0) + 1
            moves.append((Span(wave.pieces[k], 0, wave.rows), ["x"]))
            users.append(("move", wave))
        users = [u for u in users if u[0] == "sum"] + [u for u in users if u[0] == "move"]
        made, places = turn(flags, sums, moves, [clock.now])
        names = sorted(made)
        made = dict(zip(names, passed([made[name] for name in names]), strict=True))
        sent = {}
        if "z" in made:
            sent["z"] = links.ring(made["z"])
        if "y" in made:
            sent["y"] = links.stream(made["y"])
        if "x" in made:
            sent["x"] = links.across(made["x"])
        for (kind, wave), place in zip(users, places, strict=True):
            if "x" in place:
                wave.crossed.append(Span(sent["x"], place["x"], wave.rows))
            if "z" in place:
                wave.moved = Span(sent["z"], place["z"], wave.rows)
            if "y" in place:
                wave.chunks.append(
                    [made["y"], Span(sent["y"], place["y"], wave.rows), place["y"]]
                )

    def settle(spans):
        arrays = {id(s.array): s.array for s in spans}
        keys = list(arrays)
        fresh = dict(zip(keys, passed([arrays[k] for k in keys], [])[0], strict=True))
        for s in {id(s): s for s in spans}.values():
            s.array = fresh[id(s.array)]

    def arrive(*waves):
        spans = []
        for wave in waves:
            if wave.added < n:
                spans.append(wave.crossed[wave.added * wave.count // 4])
            spans += [] if wave.moved is None else [wave.moved]
        settle(spans)

    def landed(wave, *chunks):
        settle([wave.chunks[k][1] for k in chunks])
        wave.lay(*chunks)

    shrink.far(parts[2], parts_core[3])
    shrink.near(parts[0], parts_core[1])
    shrink_parts[2] = passed(shrink_parts[2])
    cross(shrink)
    shrink_parts.append(links.ring(shrink_parts[2]))
    grads, sums = hidden_behind(
        cotangent,
        active[:2],
        back[:2],
        shrink_slots,
        expand_slots[:2],
        after=[clock.now],
        cost=HEAVY,
    )
    grads, sums = passed(grads, list(sums))
    arrive(shrink)
    shrink_parts[3] = passed(shrink_parts[3])
    shrink_other = passed(join_ring(flags, shrink_parts, [clock.now]))
    shrink_last = links.core(shrink_other)
    spin(shrink, crossing=(shrink,))
    shrink_last = passed(shrink_last)
    shrink_slots += [(shrink_other, 0), (shrink_last, 0)]
    grads_far, (added, second_grad) = hidden_behind(
        cotangent,
        active[2:],
        back[2:],
        shrink_slots[2:],
        expand_slots[2:],
        sums,
        [clock.now],
        HEAVY,
    )
    hidden_grad = [*grads, *passed(grads_far)]
    middle_grad, branch_grad, midnorm_grad, result = second_back(
        middle, gain_second, second_grad, cotangent, added, [clock.now]
    )
    branch_grad = passed(branch_grad)

    def expand_part(j, cost=LIGHT):
        return passed(
            expand_output_grad(
                second_normed, hidden_grad[j], saved[j][2], branch_grad, [clock.now], cost
            )
        )

    parts = {j: expand_part(j) for j in (3, 2)}
    arrive(shrink)
    spin(shrink, crossing=(shrink,))
    parts_core = links.core(parts[3])
    parts.update({1: expand_part(1, HEAVY), 0: expand_part(0)})
    parts_core = passed(parts_core)
    arrive(shrink)
    expand.far(parts[2], parts_core)
    spin(shrink, crossing=(shrink, expand))

    def under_way(wave, *chunks):
        settle([wave.chunks[k][1] for k in chunks])

    slope_rows = [None] * 4
    first_grad = None
    for step, j in enumerate((3, 2, 1, 0)):
        if step == 0:
            parts_core = links.core(parts[1])
        elif step == 1:
            spin(shrink, expand, crossing=(expand,))
            part_core = links.core(part)
        elif step == 2:
            attn.far(part, part_core)
            spin(shrink, expand, crossing=(expand, attn))
        else:
            spin(shrink, expand, crossing=(expand, attn))
            part_core = links.core(part)
        part, slope_rows[j], first_grad = attention_behind(
            heads_slot,
            branch_grad,
            first_normed,
            attn_slots[j],
            saved[j][:2],
            far,
            first_grad,
            [clock.now],
            HEAVY,
        )
        first_grad, part = passed(first_grad, part)
        if step == 0:
            expand.near(parts[0], passed(parts_core))
        elif step == 1:
            part_core = passed(part_core)
        elif step == 3:
            rows_out, small = first_back(
                heads_slot,
                flags,
                source,
                gain_first,
                first_grad,
                middle_grad,
                midnorm_grad,
                result,
                slope_rows,
                [clock.now],
            )
            small, rows_out = passed(small, list(rows_out))
            attn.near(part, passed(part_core))
        arrive(*((shrink, expand) if step < 3 else (shrink, expand, attn)))
        if step == 2:
            under_way(shrink, 0)
        if step == 3:
            under_way(shrink, 1, 2)

    rows_back = [None] * 4

    def hop(value, moved):
        return passed(add(value, moved, [clock.now]))

    def send_back(k):
        rows_back[k] = links.back_to_rows(rows_out[k], k)

    def sent_back(k):
        rows_back[k] = passed(rows_back[k])

    spin(shrink, expand, attn, crossing=(attn, attn))
    small_moved = links.core(small)
    shrink.lay(0)
    shrink.lay(1)
    shrink.lay(2)
    arrive(expand, attn)
    small = hop(small, passed(small_moved))

    spin(expand, attn)
    small_moved = links.across(small)
    arrive(expand, attn)
    under_way(shrink, 3)
    under_way(expand, 1)
    small = hop(small, passed(small_moved))

    spin(expand, attn)
    small_moved = links.level(small, 1)
    send_back(0)
    send_back(2)
    shrink.lay(3)
    expand.lay(0)
    expand.lay(1)
    arrive(expand, attn)
    under_way(expand, 2)
    small = hop(small, passed(small_moved))
    bit = 4
    while bit < links.high:
        small = hop(small, passed(links.level(small, bit)))
        bit *= 2

    spin(expand, attn)
    small_moved = links.level(small, 2)
    expand.lay(2)
    arrive(attn)
    sent_back(0)
    sent_back(2)
    small = hop(small, passed(small_moved))

    spin(attn)
    small_other = links.stream(small)
    send_back(3)
    arrive(attn)
    small_other = passed(small_other)
    under_way(expand, 3)
    text_small = jnp.where(lo == 0, small, small_other)
    visual_small = jnp.where(lo == 0, small_other, small)
    slope_sum = lax.dynamic_slice(
        (text_small + visual_small)[2], (tensor_index * heads_slot,), (heads_slot,)
    )
    text_small, visual_small, slope_sum = passed(text_small, visual_small, slope_sum)

    spin(attn)
    send_back(1)
    expand.lay(3)
    attn.lay(0)
    arrive(attn)
    under_way(attn, 1)
    sent_back(3)

    spin(attn)
    attn.lay(1, cost=HEAVY)
    sent_back(1)
    text_result, visual_result, text_input_grad, visual_input_grad = passed(
        *sort_rows(flags, rows_back, [clock.now])
    )
    landed(attn, 2)
    landed(attn, 3)

    text_sh, visual_sh = shrink.laid
    text_ex, text_out, visual_ex, visual_out = expand.laid
    text_at, visual_at = attn.laid[:3], attn.laid[3:]
    return (
        text_result,
        visual_result,
        text_input_grad,
        visual_input_grad,
        text_small[0],
        *(grad.T for grad in text_at),
        text_out,
        text_small[1],
        text_ex,
        text_sh,
        visual_small[0],
        *(grad.T for grad in visual_at),
        visual_out,
        visual_small[1],
        visual_ex,
        visual_sh,
        slope_sum,
    )


def solution(mesh):
    rows = P("dp", "tensor", None)
    split_out = P(None, "tensor")
    split_in = P("tensor", None)
    weights = (P(), split_out, split_out, split_out, split_in, P(), split_out, split_in)
    return jax.shard_map(
        shards,
        mesh=mesh,
        in_specs=(
            rows,
            rows,
            P("dp", None, None),
            P("dp"),
            *weights,
            *weights,
            P("tensor"),
            rows,
            rows,
        ),
        out_specs=(rows, rows, rows, rows, *weights, *weights, P("tensor")),
        check_vma=False,
    )
```

```python
import functools

import jax
import jax.numpy as jnp
from jax import lax
from jax.experimental import pallas as pl
from jax.experimental.pallas import tpu as pltpu
from jax.sharding import PartitionSpec as P

HEAD_DIM = 64
GRID_W = 32
NBIN = 1000
EPSILON = 1e-05
AXES = ("dp", "tensor")
ROWS = (((0,), (0,)), ((), ()))
COLS = (((1,), (1,)), ((), ()))
F32 = jnp.float32
BF16 = jnp.bfloat16
FAR = 1e30
GELU_A = 0.7978845608028654
GELU_B = 0.044715
SCALE = HEAD_DIM ** (-0.5)
FLAG_LO, FLAG_X, FLAG_C, FLAG_HALF, FLAG_RING, FLAG_PLACE, FLAG_TENSOR = range(7)
FLOPS_US = 1_150_000_000
LIGHT, HEAVY = 0.001, 20
VMEM_LIMIT = 16 * 1024 * 1024
IN_VMEM = pl.BlockSpec(memory_space=pltpu.VMEM)
IN_SMEM = pl.BlockSpec(memory_space=pltpu.SMEM)
IN_ANY = pl.BlockSpec(memory_space=pl.ANY)
IN_HBM = pl.BlockSpec(memory_space=pltpu.HBM)


def dot(a, b, dims=None):
    if dims is None:
        return jnp.dot(a, b, preferred_element_type=F32)
    return lax.dot_general(a, b, dims, preferred_element_type=F32)


def kernel_call(body, outs, ins, scalars=0, scratch=(), after=(), far_ins=0, far_outs=0, hbm_outs=0, cost=LIGHT):
    count = len(ins)

    def whole(*refs):
        body(*refs[:count], *refs[count + len(after) :])

    near = [IN_SMEM] * scalars + [IN_VMEM] * (count - scalars - far_ins) + [IN_ANY] * far_ins
    return pl.pallas_call(
        whole,
        out_shape=outs,
        in_specs=near + [IN_ANY] * len(after),
        out_specs=[IN_HBM] * hbm_outs
        + [IN_VMEM] * (len(outs) - hbm_outs - far_outs)
        + [IN_ANY] * far_outs,
        scratch_shapes=list(scratch),
        compiler_params=pltpu.CompilerParams(vmem_limit_bytes=VMEM_LIMIT),
        cost_estimate=pl.CostEstimate(flops=int(FLOPS_US * cost), bytes_accessed=1000, transcendentals=0),
    )(*ins, *after)


def shape(rows, cols, dtype):
    return jax.ShapeDtypeStruct((rows, cols), dtype)


def norm_parts(values):
    center = values - jnp.mean(values, axis=-1, keepdims=True)
    spread = jnp.mean(center * center, axis=-1, keepdims=True)
    scale = lax.rsqrt(spread + EPSILON)
    return center * scale, scale


def norm_back(normed, scale, gain, grad):
    inner = grad * gain
    mean_inner = jnp.mean(inner, axis=-1, keepdims=True)
    mean_both = jnp.mean(inner * normed, axis=-1, keepdims=True)
    return scale * (inner - mean_inner - normed * mean_both)


def first_norm_body(gain_ref, *refs):
    blocks, (source_ref, out_ref) = refs[:-2], refs[-2:]
    rows = source_ref.shape[0] // len(blocks)
    for k, block in enumerate(blocks):
        at = slice(k * rows, (k + 1) * rows)
        values = block[:rows, :]
        source_ref[at, :] = values
        normed, unused = norm_parts(values.astype(F32))
        out_ref[at, :] = (normed * gain_ref[...]).astype(BF16)


def first_norm(gain, blocks, rows, after):
    outs = [shape(rows * len(blocks), blocks[0].shape[1], BF16)] * 2
    return kernel_call(first_norm_body, outs, [gain, *blocks], after=after, cost=HEAVY)


def second_norm_body(source_ref, branch_ref, gain_ref, middle_ref, out_ref):
    middle = source_ref[...].astype(F32) + branch_ref[...]
    middle_ref[...] = middle
    normed, unused = norm_parts(middle)
    out_ref[...] = (normed * gain_ref[...]).astype(BF16)


def second_norm(source, branch, gain, after):
    outs = [shape(*source.shape, F32), shape(*source.shape, BF16)]
    return kernel_call(second_norm_body, outs, [source, branch, gain], after=after)


def second_back_body(
    middle_ref, gain_ref, grad_ref, cot_ref, added_ref, mid_ref, branch_ref, gain_out, result_ref
):
    middle = middle_ref[...]
    normed, scale = norm_parts(middle)
    grad = grad_ref[...]
    total = cot_ref[...].astype(F32) + norm_back(normed, scale, gain_ref[...], grad)
    mid_ref[...] = total
    branch_ref[...] = total.astype(BF16)
    gain_out[...] = jnp.sum(grad * normed, axis=0, keepdims=True)
    result_ref[...] = (middle + added_ref[...]).astype(BF16)


def second_back(middle, gain, grad, cotangent, added, after):
    rows, cols = middle.shape
    outs = [shape(rows, cols, F32), shape(rows, cols, BF16), shape(1, cols, F32)]
    outs.append(shape(rows, cols, BF16))
    ins = [middle, gain, grad, cotangent, added]
    return kernel_call(second_back_body, outs, ins, after=after)


def first_back_body(
    heads, flags, source_ref, gain_ref, grad_ref, mid_ref, midnorm_ref, result_ref, *refs
):
    slopes, blocks, small_ref = refs[:4], refs[4:8], refs[8]
    normed, scale = norm_parts(source_ref[...].astype(F32))
    grad = grad_ref[...]
    out = (mid_ref[...] + norm_back(normed, scale, gain_ref[...], grad)).astype(BF16)
    rows = result_ref.shape[0] // 4
    for k in range(4):
        blocks[k][:rows, :] = result_ref[k * rows : (k + 1) * rows, :]
        blocks[k][rows:, :] = out[k * rows : (k + 1) * rows, :]
    small_ref[...] = jnp.zeros_like(small_ref)
    small_ref[0:1, :] = jnp.sum(grad * normed, axis=0, keepdims=True)
    small_ref[1:2, :] = midnorm_ref[...]
    lane = lax.broadcasted_iota(jnp.int32, midnorm_ref.shape, 1)
    row = jnp.zeros(midnorm_ref.shape, F32)
    for j in range(4):
        sums = -jnp.sum(slopes[j][...], axis=1, keepdims=True)
        for h in range(heads):
            spot = (flags[FLAG_TENSOR] ^ j) * heads + h
            row = row + jnp.where(lane == spot, sums[h : h + 1, :], 0.0)
    small_ref[2:3, :] = row


def first_back(heads, flags, source, gain, grad, middle_grad, midnorm_grad, result, slope_rows, after):
    rows, cols = source.shape
    outs = [shape(rows // 2, cols, BF16)] * 4 + [shape(8, cols, F32)]
    ins = [flags, source, gain, grad, middle_grad, midnorm_grad, result, *slope_rows]
    out = kernel_call(functools.partial(first_back_body, heads), outs, ins, 1, after=after)
    return out[:4], out[4]


def each(flag, one, other):
    pl.when(flag == 0)(one)
    pl.when(flag != 0)(other)


def info_body(flags, counts, boxes_ref, info_ref):
    info_ref[...] = jnp.zeros_like(info_ref)
    info_ref[0:2, :] = boxes_ref[flags[FLAG_X]]
    info_ref[2:3, :] = jnp.full((1, info_ref.shape[1]), counts[flags[FLAG_X]], jnp.int32)


def page_info(flags, counts, boxes, after):
    outs = [shape(8, boxes.shape[2], jnp.int32)]
    return kernel_call(info_body, outs, [flags, counts, boxes], 2, after=after)[0]


def distance_body(flags, own_ref, theirs_ref, far_ref, info):
    tokens = far_ref.shape[0]
    block = tokens // 4
    mine = 1 - (flags[FLAG_LO] ^ flags[FLAG_C])
    text = 1 - flags[FLAG_LO]
    share = text.astype(F32)
    for k in range(4):
        at = slice(k * block, (k + 1) * block)
        shard = flags[FLAG_PLACE] ^ k
        there = pl.ds(pl.multiple_of(shard * block, block), block)
        boxes = own_ref[:, there] * mine + theirs_ref[:, there] * (1 - mine)
        index = lax.broadcasted_iota(jnp.int32, (1, block), 1) + shard * block
        column = (index & (GRID_W - 1)).astype(F32)
        line = (index >> (GRID_W.bit_length() - 1)).astype(F32)
        text_place = boxes[0:2, :].astype(F32) / NBIN
        coord_x = text_place[0:1, :] * share + (column + 0.5) / GRID_W * (1.0 - share)
        coord_y = text_place[1:2, :] * share + (line + 0.5) / (tokens // GRID_W) * (1.0 - share)
        count = boxes[2:3, :] * text + tokens * (1 - text)
        info[...] = jnp.zeros_like(info) if k == 0 else info[...]
        info[0:1, at] = coord_x
        info[1:2, at] = coord_y
        info[2:3, at] = jnp.where(index < count, 0.0, 1.0)
    turned = info[...].T
    delta_x = turned[:, 0:1] - info[0:1, :]
    delta_y = turned[:, 1:2] - info[1:2, :]
    distance = jnp.sqrt(delta_x * delta_x + delta_y * delta_y)
    far_ref[...] = jnp.where(turned[:, 2:3] > 0.5, FAR, distance)


def distances(flags, own, theirs, after=()):
    tokens = own.shape[1]
    scratch = [pltpu.VMEM((8, tokens), F32)]
    return kernel_call(
        distance_body, [shape(tokens, tokens, F32)], [flags, own, theirs], 1, scratch, after
    )[0]


def both(a, b):
    return (a.astype(F32) + b.astype(F32)).astype(BF16)


def near_body(own_ref, core_ref, out_ref):
    out_ref[...] = both(own_ref[...], core_ref[...])


def near_sum(own, core, after):
    return kernel_call(near_body, [shape(*own.shape, BF16)], [own, core], after=after)[0]


def far_body(cuts, flags, own_ref, core_ref, *pieces):
    rows = own_ref.shape[0] // 4
    for i in range(4):
        base = ((flags[FLAG_RING] + 3 - i) & 3) * rows
        for piece, low, high in zip(pieces, cuts, cuts[1:]):
            first, last = max(low, i * rows), min(high, (i + 1) * rows)
            if first < last:
                at = pl.ds(pl.multiple_of(base + first - i * rows, 16), last - first)
                piece[first - low : last - low, :] = both(own_ref[at, :], core_ref[at, :])


def far_sum(flags, own, core, cuts, after):
    outs = [shape(high - low, own.shape[1], BF16) for low, high in zip(cuts, cuts[1:])]
    body = functools.partial(far_body, cuts)
    return kernel_call(body, outs, [flags, own, core], 1, after=after)


class Span:
    def __init__(self, array, start, rows):
        self.array, self.start, self.rows = array, start, rows


def turn_body(plan, flags, *refs):
    ins, outs = refs[: plan["ins"]], refs[plan["ins"] :]

    def rows_of(span):
        index, start, rows = span
        return ins[index][start : start + rows, :]

    for step, near, skip, spans, places in plan["sums"]:
        rows = spans[0][2]
        base = ((flags[FLAG_RING] + 3 - step) & 3) * (ins[near].shape[0] // 4)
        at = pl.ds(pl.multiple_of(base + skip, 16), rows)
        total = ins[near][at, :].astype(F32)
        for span in spans:
            total = total + rows_of(span).astype(F32)
        total = total.astype(BF16)
        for out, start in places:
            outs[out][start : start + rows, :] = total
    for span, places in plan["moves"]:
        for out, start in places:
            outs[out][start : start + span[2], :] = rows_of(span)


def turn(flags, sums, moves, after):
    ins, index = [flags], {}

    def place_of(array):
        if id(array) not in index:
            index[id(array)] = len(ins) - 1
            ins.append(array)
        return index[id(array)]

    def static(span):
        return (place_of(span.array), span.start, span.rows)

    heights = {}

    def places_of(outs, rows):
        places = []
        for out in outs:
            places.append((out, heights.get(out, 0)))
            heights[out] = heights.get(out, 0) + rows
        return places

    plan = {"sums": [], "moves": []}
    for step, near, skip, spans, outs in sums:
        rows = spans[0].rows
        plan["sums"].append(
            (step, place_of(near), skip, [static(s) for s in spans], places_of(outs, rows))
        )
    for span, outs in moves:
        plan["moves"].append((static(span), places_of(outs, span.rows)))
    plan["ins"] = len(ins) - 1
    order = sorted(heights)
    number = {out: i for i, out in enumerate(order)}
    for kind in ("sums", "moves"):
        plan[kind] = [
            (*item[:-1], [(number[out], start) for out, start in item[-1]]) for item in plan[kind]
        ]
    cols = ins[1].shape[1]
    shapes = [shape(heights[out], cols, BF16) for out in order]
    body = functools.partial(turn_body, plan)
    made = kernel_call(body, shapes, ins, 1, after=after)
    places = [
        {order[out]: start for out, start in item[-1]} for kind in ("sums", "moves") for item in plan[kind]
    ]
    return dict(zip(order, made, strict=True)), places


def chunk_sum(flags, sums, after):
    made, places = turn(flags, sums, [], after)
    return made["z"]


def grad_body(left_ref, right_ref, out_ref):
    out_ref[...] = dot(left_ref[...], right_ref[...], ROWS).astype(BF16)


def grad_of(left, right, after, cost=LIGHT):
    outs = [shape(left.shape[1], right.shape[1], BF16)]
    return kernel_call(grad_body, outs, [left, right], after=after, cost=cost)[0]


def add_body(left_ref, right_ref, out_ref):
    out_ref[...] = left_ref[...] + right_ref[...]


def add(left, right, after):
    return kernel_call(add_body, [shape(*left.shape, left.dtype)], [left, right], after=after)[0]


def expand_output_body(normed_ref, hidden_ref, attended_ref, branch_ref, out_ref):
    rows = normed_ref.shape[1]
    out_ref[:rows, :] = dot(normed_ref[...], hidden_ref[...], ROWS).astype(BF16)
    out_ref[rows:, :] = dot(attended_ref[...], branch_ref[...], ROWS).astype(BF16)


def expand_output_grad(normed, hidden_grad, attended, branch_grad, after, cost=LIGHT):
    rows = normed.shape[1] + attended.shape[1]
    outs = [shape(rows, normed.shape[1], BF16)]
    ins = [normed, hidden_grad, attended, branch_grad]
    return kernel_call(expand_output_body, outs, ins, after=after, cost=cost)[0]


def join_body(heights, flags, first_ref, second_ref, out_ref):
    start = low = 0
    for height in heights:
        for ref, side in ((first_ref, flags[FLAG_HALF]), (second_ref, 1 - flags[FLAG_HALF])):
            at = pl.multiple_of(low + side * height, height)
            out_ref[pl.ds(at, height), :] = ref[start : start + height, :]
        start += height
        low += 2 * height
    rest = out_ref.shape[0] - low
    if rest:
        out_ref[low:, :] = first_ref[start : start + rest, :]


def join(flags, first, second, heights, after):
    rows = first.shape[0] + sum(heights)
    outs = [shape(rows, first.shape[1], BF16)]
    body = functools.partial(join_body, heights)
    return kernel_call(body, outs, [flags, first, second], 1, after=after)[0]


def join_ring_body(flags, *refs):
    pieces, out_ref = refs[:-1], refs[-1]
    rows = pieces[0].shape[0]
    for r, piece in enumerate(pieces):
        at = pl.multiple_of(((flags[FLAG_RING] + 4 - r) & 3) * rows, rows)
        out_ref[pl.ds(at, rows), :] = piece[...]


def join_ring(flags, pieces, after):
    rows, cols = pieces[0].shape
    outs = [shape(4 * rows, cols, BF16)]
    return kernel_call(join_ring_body, outs, [flags, *pieces], 1, after=after)[0]


def lay_body(groups, r, start, flags, *refs):
    size = len(groups)
    chunks, refs = refs[:2], refs[2:]
    outs, (held, sems) = refs[-2 * size - 2 : -2], refs[-2:]
    rows = held.shape[1]
    spot = (flags[FLAG_RING] + 4 - r) & 3
    waits = []
    for side in range(2):
        slot, sem = held.at[side], sems.at[side]
        slot[...] = chunks[side][start : start + rows, :].astype(F32)
        stream = flags[FLAG_LO] ^ side
        for p in range(4):
            for g, (low, high) in enumerate(groups):
                first, last = max(p * rows, low), min((p + 1) * rows, high)
                if first >= last:
                    continue
                piece = slot.at[pl.ds(first - p * rows, last - first)]
                place = pl.ds(first - low, last - first)
                for s in range(2):
                    copy = pltpu.make_async_copy(piece, outs[s * size + g].at[place], sem)
                    pl.when((spot == p) & (stream == s))(copy.start)
        waits.append(pltpu.make_async_copy(slot, outs[0].at[pl.ds(0, rows)], sem))
    for copy in waits:
        copy.wait()


def lay(flags, r, mine, theirs, start, rows, groups, laid, after, cost):
    cols = mine.shape[1]
    outs = [shape(high - low, cols, F32) for low, high in groups] * 2
    ins = [flags, mine, theirs]
    first = len(ins)
    body = functools.partial(lay_body, groups, r, start)
    laid = [] if laid is None else list(laid)

    def whole(*refs):
        body(*refs[:first], *refs[first + len(laid) + len(after) :])

    return pl.pallas_call(
        whole,
        out_shape=outs,
        in_specs=[IN_SMEM, IN_VMEM, IN_VMEM] + [IN_ANY] * (len(laid) + len(after)),
        out_specs=[IN_ANY] * len(outs),
        scratch_shapes=[pltpu.VMEM((2, rows, cols), F32), pltpu.SemaphoreType.DMA((2,))],
        input_output_aliases={first + i: i for i in range(len(laid))},
        compiler_params=pltpu.CompilerParams(vmem_limit_bytes=VMEM_LIMIT),
        cost_estimate=pl.CostEstimate(
            flops=int(FLOPS_US * cost), bytes_accessed=1000, transcendentals=0
        ),
    )(*ins, *laid, *after)


def sort_body(flags, *refs):
    parts, outs, sems = refs[:4], refs[4:8], refs[8]
    rows = outs[0].shape[1]
    copies = []
    for k in range(4):
        stream = flags[FLAG_C] ^ (k & 1)
        page = flags[FLAG_X] ^ (k >> 1)
        for n in range(2):
            piece = parts[k].at[pl.ds(n * rows, rows)]
            sem = sems.at[2 * k + n]

            def move(out, piece=piece, page=page, sem=sem):
                pltpu.make_async_copy(piece, out.at[page], sem).start()

            each(
                stream,
                functools.partial(move, outs[2 * n]),
                functools.partial(move, outs[2 * n + 1]),
            )
            copies.append(pltpu.make_async_copy(piece, outs[0].at[0], sem))
    for copy in copies:
        copy.wait()


def sort_rows(flags, parts, after=()):
    rows, cols = parts[0].shape
    outs = [jax.ShapeDtypeStruct((2, rows // 2, cols), BF16)] * 4
    scratch = [pltpu.SemaphoreType.DMA((8,))]
    return kernel_call(sort_body, outs, [flags, *parts], 1, scratch, after, far_ins=4, far_outs=4)


def slope_of(w_ref, wide, h):
    rows = [w_ref[4 * wide + i : 4 * wide + i + 1, h : h + 1].astype(F32) for i in range(3)]
    return rows[0] + rows[1] + rows[2]


def attention_ahead_body(heads, block, first, normed_ref, w_ref, far_ref, *refs):
    branch_ref, refs = (None, refs) if first else (refs[0], refs[1:])
    kept, (out_ref, *held, sems) = refs[:3], refs[3:]
    qkv_ref, attended_ref, log_ref = held
    keep = [pltpu.make_async_copy(held[i], kept[i], sems.at[i]) for i in range(3)]
    tokens = normed_ref.shape[0]
    wide = heads * HEAD_DIM
    qkv_ref[...] = dot(normed_ref[...], w_ref[: 3 * wide, :], COLS).astype(BF16)
    log_ref[...] = jnp.zeros_like(log_ref)
    keep[0].start()
    for h in range(heads):
        col = slice(h * HEAD_DIM, (h + 1) * HEAD_DIM)
        keys = qkv_ref[:, wide + col.start : wide + col.stop]
        values_t = qkv_ref[:, 2 * wide + col.start : 2 * wide + col.stop].T
        slope = slope_of(w_ref, wide, h)
        for b in range(tokens // block):
            rows = slice(b * block, (b + 1) * block)
            scores = dot(keys, qkv_ref[rows, col], COLS) * SCALE - slope * far_ref[:, rows]
            highest = jnp.max(scores, axis=0, keepdims=True)
            exponent = jnp.exp(scores - highest)
            totals = jnp.sum(exponent, axis=0, keepdims=True)
            soft_weights = (exponent * (1.0 / totals)).astype(BF16)
            log_ref[h : h + 1, rows] = highest + jnp.log(totals)
            attended_ref[rows, col] = dot(values_t, soft_weights).T.astype(BF16)
    keep[1].start()
    keep[2].start()
    part = dot(attended_ref[...], w_ref[3 * wide : 4 * wide, :])
    out_ref[...] = part if first else branch_ref[...] + part
    for copy in keep:
        copy.wait()


def attention_ahead(heads, normed, w, far, branch, after=(), cost=LIGHT):
    rows, cols = normed.shape
    wide = heads * HEAD_DIM
    ins = [normed, w, far] + ([] if branch is None else [branch])
    outs = [shape(rows, 3 * wide, BF16), shape(rows, wide, BF16), shape(8, rows, F32)]
    scratch = [pltpu.VMEM(out.shape, out.dtype) for out in outs] + [pltpu.SemaphoreType.DMA((3,))]
    outs.append(shape(rows, cols, F32))
    body = functools.partial(attention_ahead_body, heads, min(256, rows), branch is None)
    return kernel_call(body, outs, ins, 0, scratch, after, hbm_outs=3, cost=cost)


def attention_behind_body(
    heads, block, first, branch_ref, normed_ref, w_ref, qkv_ref, log_ref, far_ref, *refs
):
    grad_ref = None if first else refs[0]
    weight_grad, out_slope, out_ref, out_qkv, attended_grad, keys_sum, values_sum = (
        refs if first else refs[1:]
    )
    tokens = branch_ref.shape[0]
    wide = heads * HEAD_DIM
    attended_grad[...] = dot(branch_ref[...], w_ref[3 * wide : 4 * wide, :], COLS).astype(BF16)
    for h in range(heads):
        col = slice(h * HEAD_DIM, (h + 1) * HEAD_DIM)
        key_col = slice(wide + col.start, wide + col.stop)
        value_col = slice(2 * wide + col.start, 2 * wide + col.stop)
        keys = qkv_ref[:, key_col]
        values = qkv_ref[:, value_col]
        keys_t = keys.T
        slope = slope_of(w_ref, wide, h)
        for b in range(tokens // block):
            rows = slice(b * block, (b + 1) * block)
            queries = qkv_ref[rows, col]
            grad = attended_grad[rows, col]
            far = far_ref[:, rows]
            scores = dot(keys, queries, COLS) * SCALE - slope * far
            probs = jnp.exp(scores - log_ref[h : h + 1, rows])
            values_part = dot(probs.astype(BF16), grad)
            probs_grad = dot(values, grad, COLS)
            mean = jnp.sum(probs * probs_grad, axis=0, keepdims=True)
            scores_grad = probs * (probs_grad - mean)
            out_slope[h : h + 1, rows] = jnp.sum(scores_grad * far, axis=0, keepdims=True)
            scores_grad = scores_grad.astype(BF16)
            keys_part = dot(scores_grad, queries)
            if b == 0:
                keys_sum[...] = keys_part
                values_sum[...] = values_part
            else:
                keys_sum[...] += keys_part
                values_sum[...] += values_part
            queries_grad = dot(keys_t, scores_grad) * SCALE
            out_qkv[rows, col] = queries_grad.T.astype(BF16)
        out_qkv[:, key_col] = (keys_sum[...] * SCALE).astype(BF16)
        out_qkv[:, value_col] = values_sum[...].astype(BF16)
    part = dot(out_qkv[...], w_ref[: 3 * wide, :])
    weight_grad[...] = dot(out_qkv[...], normed_ref[...], ROWS).astype(BF16)
    out_ref[...] = part if first else grad_ref[...] + part


def attention_behind(heads, branch_grad, normed, w, kept, far, grad, after=(), cost=LIGHT):
    rows, cols = branch_grad.shape
    wide = heads * HEAD_DIM
    ins = [branch_grad, normed, w, *kept, far] + ([] if grad is None else [grad])
    outs = [shape(3 * wide, cols, BF16), shape(8, rows, F32), shape(rows, cols, F32)]
    scratch = [pltpu.VMEM((rows, 3 * wide), BF16), pltpu.VMEM((rows, wide), BF16)] + [pltpu.VMEM((rows, HEAD_DIM), F32)] * 2
    body = functools.partial(attention_behind_body, heads, min(256, rows), grad is None)
    return kernel_call(body, outs, ins, 0, scratch, after, cost=cost)


def gelu_both(values):
    square = values * values
    bend = jnp.tanh(GELU_A * values * (1.0 + GELU_B * square))
    half = 0.5 * (1.0 + bend)
    slope = half + 0.5 * values * (1.0 - bend * bend) * (
        GELU_A + (3.0 * GELU_A * GELU_B) * square
    )
    return values * half, slope


def hidden_ahead_body(count, blocks, starts, normed_ref, *refs):
    weights, refs = refs[:count], refs[count:]
    parts, outs, held = refs[:blocks], refs[blocks:-1], refs[-1]
    tokens, cols = normed_ref.shape
    for k in range(blocks):
        rows = tokens // blocks
        outs[2 * count][k * rows : (k + 1) * rows, :] = parts[k][parts[k].shape[0] - rows :, :]
    step = 32
    for j in range(count):
        held[...] = dot(normed_ref[...], weights[j][starts[j] : starts[j] + cols, :])
        for b in range(tokens // step):
            rows = slice(b * step, (b + 1) * step)
            active, back = gelu_both(held[rows, :])
            outs[2 * j][rows, :] = active.astype(BF16)
            outs[2 * j + 1][rows, :] = back.astype(BF16)


def hidden_ahead(normed, weights, parts=(), after=(), cost=LIGHT):
    rows, cols = normed.shape
    arrays, starts = zip(*weights, strict=True)
    count, wide = len(weights), arrays[0].shape[1]
    outs = [shape(rows, wide, BF16)] * (2 * count)
    if parts:
        outs.append(shape(rows, cols, BF16))
    body = functools.partial(hidden_ahead_body, count, len(parts), starts)
    scratch = [pltpu.VMEM((rows, wide), F32)]
    out = kernel_call(body, outs, [normed, *arrays, *parts], 0, scratch, after, cost=cost)
    return out[0 : 2 * count : 2], out[1 : 2 * count : 2], out[-1]


def hidden_behind_body(count, first, starts, cot_ref, *refs):
    active, back, shrink, expand = (refs[count * i : count * (i + 1)] for i in range(4))
    refs = refs[4 * count :]
    before, refs = ((), refs) if first else (refs[:2], refs[2:])
    grads, (added_ref, out_ref) = refs[:count], refs[count:]
    cols, wide = cot_ref.shape[1], active[0].shape[1]
    for j in range(count):
        down = slice(starts[0][j], starts[0][j] + wide)
        up = slice(starts[1][j], starts[1][j] + cols)
        part = dot(active[j][...], shrink[j][down, :])
        if j == 0:
            added_ref[...] = part if first else before[0][...] + part
        else:
            added_ref[...] += part
        active_grad = dot(cot_ref[...], shrink[j][down, :], COLS)
        grads[j][...] = (active_grad * back[j][...].astype(F32)).astype(BF16)
        part = dot(grads[j][...], expand[j][up, :], COLS)
        if j == 0:
            out_ref[...] = part if first else before[1][...] + part
        else:
            out_ref[...] += part


def hidden_behind(cotangent, active, back, shrink, expand, before=(), after=(), cost=LIGHT):
    rows, cols = cotangent.shape
    count, wide = len(active), active[0].shape[1]
    downs, ups = zip(*shrink, strict=True), zip(*expand, strict=True)
    (downs, down_starts), (ups, up_starts) = downs, ups
    outs = [shape(rows, wide, BF16)] * count + [shape(rows, cols, F32)] * 2
    body = functools.partial(hidden_behind_body, count, not before, (down_starts, up_starts))
    ins = [cotangent, *active, *back, *downs, *ups, *before]
    out = kernel_call(body, outs, ins, after=after, cost=cost)
    return out[:count], out[count:]


class Links:
    def __init__(self, pairs):
        self.pairs = pairs
        self.high = pairs // 2
        self.ring_size = 4

    def send(self, value, move):
        table = []
        for dp in range(self.pairs):
            for tensor in range(4):
                hi, lo, x, c = move(dp // 2, dp % 2, tensor // 2, tensor % 2)
                table.append((dp * 4 + tensor, (hi * 2 + lo) * 4 + x * 2 + c))
        return lax.ppermute(value, AXES, table)

    def core(self, value):
        return self.send(value, lambda hi, lo, x, c: (hi, lo, x, 1 - c))

    def across(self, value):
        return self.send(value, lambda hi, lo, x, c: (hi, lo, 1 - x, c))

    def stream(self, value):
        return self.send(value, lambda hi, lo, x, c: (hi, 1 - lo, x, c))

    def level(self, value, bit):
        return self.send(value, lambda hi, lo, x, c: (hi ^ bit, lo, x, c))

    def ring(self, value):
        after = (1, 3, 0, 2)
        return self.send(value, lambda hi, lo, x, c: (hi // 4 * 4 + after[hi % 4], lo, x, c))

    def out_to_page(self, value, k):
        return self.send(value, lambda hi, lo, x, c: (hi, c ^ (k & 1), x ^ (k >> 1), lo))

    def back_to_rows(self, value, k):
        return self.send(value, lambda hi, lo, x, c: (hi, c, x ^ (k >> 1), lo ^ (k & 1)))


def add_low(a, b):
    return (a.astype(F32) + b.astype(F32)).astype(BF16)


class Clock:
    def __init__(self, start):
        self.now = start

    def passed(self, *values):
        values, self.now = lax.optimization_barrier((list(values), self.now))
        return values[0] if len(values) == 1 else values


def shards(
    text_input,
    visual_input,
    text_boxes,
    text_count,
    text_prenorm,
    text_query,
    text_key,
    text_value,
    text_output,
    text_midnorm,
    text_expand,
    text_shrink,
    visual_prenorm,
    visual_query,
    visual_key,
    visual_value,
    visual_output,
    visual_midnorm,
    visual_expand,
    visual_shrink,
    slopes,
    text_cotangent,
    visual_cotangent,
):
    dp_index = lax.axis_index("dp")
    tensor_index = lax.axis_index("tensor")
    hi, lo = dp_index // 2, dp_index % 2
    x, c = tensor_index // 2, tensor_index % 2
    links = Links(lax.axis_size("dp"))
    heads_slot = slopes.shape[0]
    half = hi % 2
    n = links.ring_size
    spot = (hi % n) ^ ((hi % n) >> 1)
    flags = jnp.stack([lo, x, c, half, spot, 2 * x + lo, tensor_index]).astype(jnp.int32)
    gain_first, gain_second = (
        jnp.where(lo == 0, text, visual).astype(F32)[None]
        for text, visual in ((text_prenorm, visual_prenorm), (text_midnorm, visual_midnorm))
    )

    def half_rows(shard):
        return lax.dynamic_slice_in_dim(shard, half * (shard.shape[0] // 2), shard.shape[0] // 2)

    def page_blocks(text_rows, visual_rows):
        blocks = []
        for k in range(4):
            parts = [
                lax.dynamic_index_in_dim(rows, x ^ (k >> 1), 0, False)
                for rows in (text_rows, visual_rows)
            ]
            blocks.append(jnp.where((c ^ (k & 1)) == 0, *parts))
        return blocks

    def to_page(blocks, chosen=(3, 2, 1, 0)):
        return [links.out_to_page(blocks[k], k) for k in chosen][::-1]

    def low(value):
        return value.astype(BF16)

    def add_low(a, b):
        return low(a.astype(F32) + b.astype(F32))

    clock = Clock(slopes)
    passed = clock.passed

    text_attn = [text_query.T, text_key.T, text_value.T, text_output]
    visual_attn = [visual_query.T, visual_key.T, visual_value.T, visual_output]
    slope_parts = []
    rest = slopes
    for i in range(3):
        slope_parts.append(low(rest))
        rest = rest - slope_parts[i].astype(F32)
    wide, width = text_output.shape
    tail = jnp.zeros((16, width), BF16).at[:3, :heads_slot].set(jnp.stack(slope_parts))
    heights = [2 * wide]
    attn_own = jnp.concatenate(
        [
            jnp.where(
                lo == 0,
                jnp.concatenate([text_query.T, text_key.T, text_value.T, text_output]),
                jnp.concatenate([visual_query.T, visual_key.T, visual_value.T, visual_output]),
            ),
            tail,
        ]
    )

    attn_half = passed(jnp.concatenate([half_rows(attn_own[: 4 * wide]), tail]))
    attn_first = links.across(attn_half)
    text_rows, visual_rows = passed(text_input, visual_input)
    in_blocks = page_blocks(text_rows, visual_rows)
    cot_parts = page_blocks(text_cotangent, visual_cotangent)
    in_blocks = [
        jnp.concatenate([in_blocks[k], cot_parts[k]]) if k < 2 else in_blocks[k] for k in range(4)
    ]
    in_blocks = to_page(passed(in_blocks))
    info = passed(page_info(flags, text_count, text_boxes, [clock.now]))
    info_theirs = links.stream(info)
    expand_own = jnp.where(lo == 0, text_expand, visual_expand)
    shrink_own = jnp.where(lo == 0, text_shrink, visual_shrink)
    expand_half = half_rows(expand_own)
    info_theirs = passed(info_theirs)
    far = passed(distances(flags, info, info_theirs, [clock.now]))
    expand_half, cot_parts, gain_first, gain_second = passed(
        expand_half, cot_parts, gain_first, gain_second
    )
    attn_first = passed(attn_first)
    attn_second = links.level(attn_first, 1)
    in_blocks = passed(in_blocks)
    attn_own, expand_half, cot_parts = passed(attn_own, expand_half, cot_parts)
    attn_core = links.core(attn_own)
    expand_first = links.across(expand_half)
    expand_core = links.core(expand_own)
    source, first_normed = passed(*first_norm(gain_first, in_blocks, text_input.shape[1], [clock.now]))

    saved = [None] * 4

    def ahead(j, weights, branch, cost=LIGHT):
        qkv, attended, log_total, branch = attention_ahead(
            heads_slot, first_normed, weights, far, branch, [clock.now], cost
        )
        saved[j] = (qkv, log_total, attended)
        return passed(branch)

    branch = ahead(0, attn_own, None)
    attn_core = passed(attn_core)
    branch = ahead(1, attn_core, branch)
    quarter = shrink_own.shape[0] // 4
    shrink_part = passed(lax.dynamic_slice_in_dim(shrink_own, spot * quarter, quarter))
    attn_second = passed(attn_second)
    expand_first, expand_core = passed(expand_first, expand_core)
    attn_other = passed(join(flags, attn_first, attn_second, heights, [clock.now]))

    expand_second = links.level(expand_first, 1)
    attn_last = links.core(attn_other)
    cot_parts, shrink_part = passed(cot_parts, shrink_part)
    shrink_parts = [links.across(shrink_part)]
    cot_far = to_page(cot_parts, (3, 2))
    branch = ahead(2, attn_other, branch, HEAVY)
    attn_last = passed(attn_last)
    branch = ahead(3, attn_last, branch)
    attn_slots = [attn_own, attn_core, attn_other, attn_last]
    expand_second = passed(expand_second)
    shrink_parts[0] = passed(shrink_parts[0])
    cot_far = passed(cot_far)
    expand_other = passed(join(flags, expand_first, expand_second, [width // 2], [clock.now]))

    shrink_own = passed(shrink_own)
    expand_last = links.core(expand_other)
    shrink_parts.append(links.ring(shrink_parts[0]))
    shrink_core = links.core(shrink_own)
    middle, second_normed = second_norm(source, branch, gain_second, [clock.now])
    second_normed = passed(second_normed)
    active, back = [], []
    for j in range(4):
        weights = (expand_own, expand_core, expand_other, expand_last)[j]
        some, other, joined = hidden_ahead(
            second_normed,
            [(weights, 0)],
            [*in_blocks[:2], *cot_far] if j == 0 else [],
            [clock.now],
            HEAVY if j == 0 else LIGHT,
        )
        active += [passed(some[0])]
        back += other
        if j == 0:
            cotangent = passed(joined)
        if j == 1:
            expand_last = passed(expand_last)
    expand_slots = [(w, 0) for w in (expand_own, expand_core, expand_other, expand_last)]
    parts, parts_core = {}, {}
    for j in (3, 1):
        parts[j] = passed(grad_of(active[j], cotangent, [clock.now]))
    shrink_parts[1], shrink_core = passed(shrink_parts[1], shrink_core)
    for j in (3, 1):
        parts_core[j] = links.core(parts[j])
    shrink_parts.append(links.ring(shrink_parts[1]))
    shrink_slots = [(shrink_own, 0), (shrink_core, 0)]
    for j, cost in ((2, HEAVY), (0, LIGHT)):
        parts[j] = passed(grad_of(active[j], cotangent, [clock.now], cost))
    parts_core = passed(parts_core)

    class Wave:
        def __init__(self, rows, groups, cuts=None):
            self.rows, self.groups = rows, groups
            self.cuts = [i * rows for i in range(5)] if cuts is None else cuts
            self.added = self.came = 0
            self.moved, self.laid = None, None
            self.crossed, self.chunks = [], []

        def far(self, own, core):
            self.pieces = passed(list(far_sum(flags, own, core, self.cuts, [clock.now])))

        def near(self, own, core):
            self.kept = passed(near_sum(own, core, [clock.now]))

        def parts(self, step):
            found = []
            for k, (low, high) in enumerate(zip(self.cuts, self.cuts[1:])):
                first, last = max(low, step * self.rows), min(high, (step + 1) * self.rows)
                if first < last:
                    found.append((k, first, last))
            return found

        def sums(self, outs):
            step, found = self.added, []
            for k, first, last in self.parts(step):
                piece, skip = self.crossed[k], first - step * self.rows
                spans = [Span(piece.array, piece.start + first - self.cuts[k], last - first)]
                if self.moved is not None:
                    spans.append(Span(self.moved.array, self.moved.start + skip, last - first))
                found.append((step, self.kept, skip, spans, outs))
            return found

        def lay(self, *chunks, cost=LIGHT):
            for k in chunks:
                mine, theirs, start = self.chunks[k]
                self.laid = lay(
                    flags,
                    k,
                    mine,
                    theirs.array,
                    start,
                    self.rows,
                    self.groups,
                    self.laid,
                    [clock.now],
                    cost,
                )
                self.laid = passed(list(self.laid))

    tall = text_shrink.shape[0]
    shrink = Wave(tall // 4, [(0, tall)], [i * tall // 48 for i in (0, 12, 28, 42, 48)])
    expand = Wave((width + wide) // 4, [(0, width), (width, width + wide)])
    attn = Wave(3 * wide // 4, [(i * wide, (i + 1) * wide) for i in range(3)])
    groups = links.high // n

    def cross(*waves):
        for wave in waves:
            piece = wave.pieces[len(wave.crossed)]
            wave.crossed.append(Span(links.across(piece), 0, piece.shape[0]))

    def spin(*waves, crossing=()):
        sums, moves, users = [], [], []
        for wave in waves:
            step = wave.added
            if step < n:
                last = step == n - 1
                if last and groups > 1:
                    table = [
                        [(g * n + r) * 2 + l for g in range(groups)]
                        for r in range(n)
                        for l in range(2)
                    ]
                    total = chunk_sum(flags, wave.sums(["z"]), [clock.now])
                    total = passed(lax.psum(total, "dp", axis_index_groups=table))
                    moves.append((Span(total, 0, wave.rows), ["z", "y"]))
                    users.append(("move", wave, wave.rows))
                else:
                    found = wave.sums(["z", "y"] if last else ["z"])
                    sums += found
                    users += [("sum", wave if i == 0 else None, wave.rows) for i in range(len(found))]
                wave.added += 1
            else:
                outs = ["z", "y"] if len(wave.chunks) < n - 1 else ["y"]
                moves.append((wave.moved, outs))
                users.append(("move", wave, wave.rows))
        pending = {}
        for wave in crossing:
            k = len(wave.crossed) + pending.get(id(wave), 0)
            pending[id(wave)] = pending.get(id(wave), 0) + 1
            rows = wave.pieces[k].shape[0]
            moves.append((Span(wave.pieces[k], 0, rows), ["x"]))
            users.append(("move", wave, rows))
        users = [u for u in users if u[0] == "sum"] + [u for u in users if u[0] == "move"]
        made, places = turn(flags, sums, moves, [clock.now])
        names = sorted(made)
        made = dict(zip(names, passed([made[name] for name in names]), strict=True))
        sent = {}
        if "z" in made:
            sent["z"] = links.ring(made["z"])
        if "y" in made:
            sent["y"] = links.stream(made["y"])
        if "x" in made:
            sent["x"] = links.across(made["x"])
        for (kind, wave, rows), place in zip(users, places, strict=True):
            if wave is None:
                continue
            if "x" in place:
                wave.crossed.append(Span(sent["x"], place["x"], rows))
            if "z" in place:
                wave.moved = Span(sent["z"], place["z"], wave.rows)
            if "y" in place:
                wave.chunks.append(
                    [made["y"], Span(sent["y"], place["y"], wave.rows), place["y"]]
                )

    def settle(spans):
        arrays = {id(s.array): s.array for s in spans}
        keys = list(arrays)
        fresh = dict(zip(keys, passed([arrays[k] for k in keys], [])[0], strict=True))
        for s in {id(s): s for s in spans}.values():
            s.array = fresh[id(s.array)]

    def arrive(*waves):
        spans = []
        for wave in waves:
            if wave.added < n:
                spans += [wave.crossed[k] for k, first, last in wave.parts(wave.added)]
            spans += [] if wave.moved is None else [wave.moved]
        settle(spans)

    def landed(wave, *chunks):
        settle([wave.chunks[k][1] for k in chunks])
        wave.lay(*chunks)

    shrink.far(parts[2], parts_core[3])
    shrink.near(parts[0], parts_core[1])
    shrink_parts[2] = passed(shrink_parts[2])
    cross(shrink)
    shrink_parts.append(links.ring(shrink_parts[2]))
    grads, sums = hidden_behind(
        cotangent,
        active[:2],
        back[:2],
        shrink_slots,
        expand_slots[:2],
        after=[clock.now],
        cost=HEAVY,
    )
    grads, sums = passed(grads, list(sums))
    arrive(shrink)
    shrink_parts[3] = passed(shrink_parts[3])
    shrink_other = passed(join_ring(flags, shrink_parts, [clock.now]))
    shrink_last = links.core(shrink_other)
    spin(shrink, crossing=(shrink,))
    shrink_last = passed(shrink_last)
    shrink_slots += [(shrink_other, 0), (shrink_last, 0)]
    grads_far, (added, second_grad) = hidden_behind(
        cotangent,
        active[2:],
        back[2:],
        shrink_slots[2:],
        expand_slots[2:],
        sums,
        [clock.now],
        HEAVY,
    )
    hidden_grad = [*grads, *passed(grads_far)]
    middle_grad, branch_grad, midnorm_grad, result = second_back(
        middle, gain_second, second_grad, cotangent, added, [clock.now]
    )
    branch_grad = passed(branch_grad)

    def expand_part(j, cost=LIGHT):
        return passed(
            expand_output_grad(
                second_normed, hidden_grad[j], saved[j][2], branch_grad, [clock.now], cost
            )
        )

    parts = {j: expand_part(j) for j in (3, 2)}
    arrive(shrink)
    spin(shrink, crossing=(shrink,))
    parts_core = links.core(parts[3])
    parts.update({1: expand_part(1, HEAVY), 0: expand_part(0)})
    parts_core = passed(parts_core)
    arrive(shrink)
    expand.far(parts[2], parts_core)
    spin(shrink, crossing=(shrink, expand))

    def under_way(wave, *chunks):
        settle([wave.chunks[k][1] for k in chunks])

    slope_rows = [None] * 4
    first_grad = None
    for step, j in enumerate((3, 2, 1, 0)):
        if step == 0:
            parts_core = links.core(parts[1])
        elif step == 1:
            spin(shrink, expand, crossing=(expand,))
            part_core = links.core(part)
        elif step == 2:
            attn.far(part, part_core)
            spin(shrink, expand, crossing=(expand, attn))
        else:
            spin(shrink, expand, crossing=(expand, attn))
            part_core = links.core(part)
        part, slope_rows[j], first_grad = attention_behind(
            heads_slot,
            branch_grad,
            first_normed,
            attn_slots[j],
            saved[j][:2],
            far,
            first_grad,
            [clock.now],
            HEAVY,
        )
        first_grad, part = passed(first_grad, part)
        if step == 0:
            expand.near(parts[0], passed(parts_core))
        elif step == 1:
            part_core = passed(part_core)
        elif step == 3:
            rows_out, small = first_back(
                heads_slot,
                flags,
                source,
                gain_first,
                first_grad,
                middle_grad,
                midnorm_grad,
                result,
                slope_rows,
                [clock.now],
            )
            small, rows_out = passed(small, list(rows_out))
            attn.near(part, passed(part_core))
        arrive(*((shrink, expand) if step < 3 else (shrink, expand, attn)))
        if step == 2:
            under_way(shrink, 0)
        if step == 3:
            under_way(shrink, 1, 2)

    rows_back = [None] * 4

    def hop(value, moved):
        return passed(add(value, moved, [clock.now]))

    def send_back(k):
        rows_back[k] = links.back_to_rows(rows_out[k], k)

    def sent_back(k):
        rows_back[k] = passed(rows_back[k])

    spin(shrink, expand, attn, crossing=(attn, attn))
    small_moved = links.core(small)
    shrink.lay(0)
    shrink.lay(1)
    shrink.lay(2)
    arrive(expand, attn)
    small = hop(small, passed(small_moved))

    spin(expand, attn)
    small_moved = links.across(small)
    arrive(expand, attn)
    under_way(shrink, 3)
    under_way(expand, 1)
    small = hop(small, passed(small_moved))

    spin(expand, attn)
    small_moved = links.level(small, 1)
    send_back(0)
    send_back(2)
    shrink.lay(3)
    expand.lay(0)
    expand.lay(1)
    arrive(expand, attn)
    under_way(expand, 2)
    small = hop(small, passed(small_moved))
    bit = 4
    while bit < links.high:
        small = hop(small, passed(links.level(small, bit)))
        bit *= 2

    spin(expand, attn)
    small_moved = links.level(small, 2)
    expand.lay(2)
    arrive(attn)
    sent_back(0)
    sent_back(2)
    small = hop(small, passed(small_moved))

    spin(attn)
    small_other = links.stream(small)
    send_back(3)
    arrive(attn)
    small_other = passed(small_other)
    under_way(expand, 3)
    text_small = jnp.where(lo == 0, small, small_other)
    visual_small = jnp.where(lo == 0, small_other, small)
    slope_sum = lax.dynamic_slice(
        (text_small + visual_small)[2], (tensor_index * heads_slot,), (heads_slot,)
    )
    text_small, visual_small, slope_sum = passed(text_small, visual_small, slope_sum)

    spin(attn)
    send_back(1)
    expand.lay(3)
    attn.lay(0)
    arrive(attn)
    under_way(attn, 1)
    sent_back(3)

    spin(attn)
    attn.lay(1, cost=HEAVY)
    sent_back(1)
    text_result, visual_result, text_input_grad, visual_input_grad = passed(
        *sort_rows(flags, rows_back, [clock.now])
    )
    landed(attn, 2)
    landed(attn, 3)

    text_sh, visual_sh = shrink.laid
    text_ex, text_out, visual_ex, visual_out = expand.laid
    text_at, visual_at = attn.laid[:3], attn.laid[3:]
    return (
        text_result,
        visual_result,
        text_input_grad,
        visual_input_grad,
        text_small[0],
        *(grad.T for grad in text_at),
        text_out,
        text_small[1],
        text_ex,
        text_sh,
        visual_small[0],
        *(grad.T for grad in visual_at),
        visual_out,
        visual_small[1],
        visual_ex,
        visual_sh,
        slope_sum,
    )


def solution(mesh):
    rows = P("dp", "tensor", None)
    split_out = P(None, "tensor")
    split_in = P("tensor", None)
    weights = (P(), split_out, split_out, split_out, split_in, P(), split_out, split_in)
    return jax.shard_map(
        shards,
        mesh=mesh,
        in_specs=(
            rows,
            rows,
            P("dp", None, None),
            P("dp"),
            *weights,
            *weights,
            P("tensor"),
            rows,
            rows,
        ),
        out_specs=(rows, rows, rows, rows, *weights, *weights, P("tensor")),
        check_vma=False,
    )
```

```python
import functools

import jax
import jax.numpy as jnp
from jax import lax
from jax.experimental import pallas as pl
from jax.experimental.pallas import tpu as pltpu
from jax.sharding import PartitionSpec as P

HEAD_DIM = 64
GRID_W = 32
NBIN = 1000
EPSILON = 1e-05
AXES = ("dp", "tensor")
ROWS = (((0,), (0,)), ((), ()))
COLS = (((1,), (1,)), ((), ()))
F32 = jnp.float32
BF16 = jnp.bfloat16
FAR = 1e30
GELU_A = 0.7978845608028654
GELU_B = 0.044715
SCALE = HEAD_DIM ** (-0.5)
FLAG_LO, FLAG_X, FLAG_C, FLAG_HALF, FLAG_RING, FLAG_PLACE, FLAG_TENSOR = range(7)
FLOPS_US = 1_150_000_000
LIGHT, HEAVY = 0.001, 20
VMEM_LIMIT = 16 * 1024 * 1024
IN_VMEM = pl.BlockSpec(memory_space=pltpu.VMEM)
IN_SMEM = pl.BlockSpec(memory_space=pltpu.SMEM)
IN_ANY = pl.BlockSpec(memory_space=pl.ANY)
IN_HBM = pl.BlockSpec(memory_space=pltpu.HBM)


def dot(a, b, dims=None):
    if dims is None:
        return jnp.dot(a, b, preferred_element_type=F32)
    return lax.dot_general(a, b, dims, preferred_element_type=F32)


def kernel_call(body, outs, ins, scalars=0, scratch=(), after=(), far_ins=0, far_outs=0, hbm_outs=0, cost=LIGHT):
    count = len(ins)

    def whole(*refs):
        body(*refs[:count], *refs[count + len(after) :])

    near = [IN_SMEM] * scalars + [IN_VMEM] * (count - scalars - far_ins) + [IN_ANY] * far_ins
    return pl.pallas_call(
        whole,
        out_shape=outs,
        in_specs=near + [IN_ANY] * len(after),
        out_specs=[IN_HBM] * hbm_outs
        + [IN_VMEM] * (len(outs) - hbm_outs - far_outs)
        + [IN_ANY] * far_outs,
        scratch_shapes=list(scratch),
        compiler_params=pltpu.CompilerParams(vmem_limit_bytes=VMEM_LIMIT),
        cost_estimate=pl.CostEstimate(flops=int(FLOPS_US * cost), bytes_accessed=1000, transcendentals=0),
    )(*ins, *after)


def shape(rows, cols, dtype):
    return jax.ShapeDtypeStruct((rows, cols), dtype)


def norm_parts(values):
    center = values - jnp.mean(values, axis=-1, keepdims=True)
    spread = jnp.mean(center * center, axis=-1, keepdims=True)
    scale = lax.rsqrt(spread + EPSILON)
    return center * scale, scale


def norm_back(normed, scale, gain, grad):
    inner = grad * gain
    mean_inner = jnp.mean(inner, axis=-1, keepdims=True)
    mean_both = jnp.mean(inner * normed, axis=-1, keepdims=True)
    return scale * (inner - mean_inner - normed * mean_both)


def first_norm_body(gain_ref, *refs):
    blocks, (source_ref, out_ref) = refs[:-2], refs[-2:]
    rows = source_ref.shape[0] // len(blocks)
    for k, block in enumerate(blocks):
        at = slice(k * rows, (k + 1) * rows)
        values = block[:rows, :]
        source_ref[at, :] = values
        normed, unused = norm_parts(values.astype(F32))
        out_ref[at, :] = (normed * gain_ref[...]).astype(BF16)


def first_norm(gain, blocks, rows, after):
    outs = [shape(rows * len(blocks), blocks[0].shape[1], BF16)] * 2
    return kernel_call(first_norm_body, outs, [gain, *blocks], after=after, cost=HEAVY)


def second_norm_body(source_ref, branch_ref, gain_ref, middle_ref, out_ref):
    middle = source_ref[...].astype(F32) + branch_ref[...]
    middle_ref[...] = middle
    normed, unused = norm_parts(middle)
    out_ref[...] = (normed * gain_ref[...]).astype(BF16)


def second_norm(source, branch, gain, after):
    outs = [shape(*source.shape, F32), shape(*source.shape, BF16)]
    return kernel_call(second_norm_body, outs, [source, branch, gain], after=after)


def second_back_body(
    middle_ref, gain_ref, grad_ref, cot_ref, added_ref, mid_ref, branch_ref, gain_out, result_ref
):
    middle = middle_ref[...]
    normed, scale = norm_parts(middle)
    grad = grad_ref[...]
    total = cot_ref[...].astype(F32) + norm_back(normed, scale, gain_ref[...], grad)
    mid_ref[...] = total
    branch_ref[...] = total.astype(BF16)
    gain_out[...] = jnp.sum(grad * normed, axis=0, keepdims=True)
    result_ref[...] = (middle + added_ref[...]).astype(BF16)


def second_back(middle, gain, grad, cotangent, added, after):
    rows, cols = middle.shape
    outs = [shape(rows, cols, F32), shape(rows, cols, BF16), shape(1, cols, F32)]
    outs.append(shape(rows, cols, BF16))
    ins = [middle, gain, grad, cotangent, added]
    return kernel_call(second_back_body, outs, ins, after=after)


def first_back_body(
    heads, flags, source_ref, gain_ref, grad_ref, mid_ref, midnorm_ref, result_ref, *refs
):
    slopes, blocks, small_ref = refs[:4], refs[4:8], refs[8]
    normed, scale = norm_parts(source_ref[...].astype(F32))
    grad = grad_ref[...]
    out = (mid_ref[...] + norm_back(normed, scale, gain_ref[...], grad)).astype(BF16)
    rows = result_ref.shape[0] // 4
    for k in range(4):
        blocks[k][:rows, :] = result_ref[k * rows : (k + 1) * rows, :]
        blocks[k][rows:, :] = out[k * rows : (k + 1) * rows, :]
    small_ref[...] = jnp.zeros_like(small_ref)
    small_ref[0:1, :] = jnp.sum(grad * normed, axis=0, keepdims=True)
    small_ref[1:2, :] = midnorm_ref[...]
    lane = lax.broadcasted_iota(jnp.int32, midnorm_ref.shape, 1)
    row = jnp.zeros(midnorm_ref.shape, F32)
    for j in range(4):
        sums = -jnp.sum(slopes[j][...], axis=1, keepdims=True)
        for h in range(heads):
            spot = (flags[FLAG_TENSOR] ^ j) * heads + h
            row = row + jnp.where(lane == spot, sums[h : h + 1, :], 0.0)
    small_ref[2:3, :] = row


def first_back(heads, flags, source, gain, grad, middle_grad, midnorm_grad, result, slope_rows, after):
    rows, cols = source.shape
    outs = [shape(rows // 2, cols, BF16)] * 4 + [shape(8, cols, F32)]
    ins = [flags, source, gain, grad, middle_grad, midnorm_grad, result, *slope_rows]
    out = kernel_call(functools.partial(first_back_body, heads), outs, ins, 1, after=after)
    return out[:4], out[4]


def each(flag, one, other):
    pl.when(flag == 0)(one)
    pl.when(flag != 0)(other)


def info_body(flags, counts, boxes_ref, info_ref):
    info_ref[...] = jnp.zeros_like(info_ref)
    info_ref[0:2, :] = boxes_ref[flags[FLAG_X]]
    info_ref[2:3, :] = jnp.full((1, info_ref.shape[1]), counts[flags[FLAG_X]], jnp.int32)


def page_info(flags, counts, boxes, after):
    outs = [shape(8, boxes.shape[2], jnp.int32)]
    return kernel_call(info_body, outs, [flags, counts, boxes], 2, after=after)[0]


def distance_body(flags, own_ref, theirs_ref, far_ref, info):
    tokens = far_ref.shape[0]
    block = tokens // 4
    mine = 1 - (flags[FLAG_LO] ^ flags[FLAG_C])
    text = 1 - flags[FLAG_LO]
    share = text.astype(F32)
    for k in range(4):
        at = slice(k * block, (k + 1) * block)
        shard = flags[FLAG_PLACE] ^ k
        there = pl.ds(pl.multiple_of(shard * block, block), block)
        boxes = own_ref[:, there] * mine + theirs_ref[:, there] * (1 - mine)
        index = lax.broadcasted_iota(jnp.int32, (1, block), 1) + shard * block
        column = (index & (GRID_W - 1)).astype(F32)
        line = (index >> (GRID_W.bit_length() - 1)).astype(F32)
        text_place = boxes[0:2, :].astype(F32) / NBIN
        coord_x = text_place[0:1, :] * share + (column + 0.5) / GRID_W * (1.0 - share)
        coord_y = text_place[1:2, :] * share + (line + 0.5) / (tokens // GRID_W) * (1.0 - share)
        count = boxes[2:3, :] * text + tokens * (1 - text)
        info[...] = jnp.zeros_like(info) if k == 0 else info[...]
        info[0:1, at] = coord_x
        info[1:2, at] = coord_y
        info[2:3, at] = jnp.where(index < count, 0.0, 1.0)
    turned = info[...].T
    delta_x = turned[:, 0:1] - info[0:1, :]
    delta_y = turned[:, 1:2] - info[1:2, :]
    distance = jnp.sqrt(delta_x * delta_x + delta_y * delta_y)
    far_ref[...] = jnp.where(turned[:, 2:3] > 0.5, FAR, distance)


def distances(flags, own, theirs, after=()):
    tokens = own.shape[1]
    scratch = [pltpu.VMEM((8, tokens), F32)]
    return kernel_call(
        distance_body, [shape(tokens, tokens, F32)], [flags, own, theirs], 1, scratch, after
    )[0]


def both(a, b):
    return (a.astype(F32) + b.astype(F32)).astype(BF16)


def near_body(own_ref, core_ref, out_ref):
    out_ref[...] = both(own_ref[...], core_ref[...])


def near_sum(own, core, after):
    return kernel_call(near_body, [shape(*own.shape, BF16)], [own, core], after=after)[0]


def far_body(cuts, flags, own_ref, core_ref, *pieces):
    rows = own_ref.shape[0] // 4
    for i in range(4):
        base = ((flags[FLAG_RING] + 3 - i) & 3) * rows
        for piece, low, high in zip(pieces, cuts, cuts[1:]):
            first, last = max(low, i * rows), min(high, (i + 1) * rows)
            if first < last:
                at = pl.ds(pl.multiple_of(base + first - i * rows, 16), last - first)
                piece[first - low : last - low, :] = both(own_ref[at, :], core_ref[at, :])


def far_sum(flags, own, core, cuts, after):
    outs = [shape(high - low, own.shape[1], BF16) for low, high in zip(cuts, cuts[1:])]
    body = functools.partial(far_body, cuts)
    return kernel_call(body, outs, [flags, own, core], 1, after=after)


class Span:
    def __init__(self, array, start, rows):
        self.array, self.start, self.rows = array, start, rows


def turn_body(plan, flags, *refs):
    ins, outs = refs[: plan["ins"]], refs[plan["ins"] :]

    def rows_of(span):
        index, start, rows = span
        return ins[index][start : start + rows, :]

    for step, near, skip, spans, places in plan["sums"]:
        rows = spans[0][2]
        base = ((flags[FLAG_RING] + 3 - step) & 3) * (ins[near].shape[0] // 4)
        at = pl.ds(pl.multiple_of(base + skip, 16), rows)
        total = ins[near][at, :].astype(F32)
        for span in spans:
            total = total + rows_of(span).astype(F32)
        total = total.astype(BF16)
        for out, start in places:
            outs[out][start : start + rows, :] = total
    for span, places in plan["moves"]:
        for out, start in places:
            outs[out][start : start + span[2], :] = rows_of(span)


def turn(flags, sums, moves, after):
    ins, index = [flags], {}

    def place_of(array):
        if id(array) not in index:
            index[id(array)] = len(ins) - 1
            ins.append(array)
        return index[id(array)]

    def static(span):
        return (place_of(span.array), span.start, span.rows)

    heights = {}

    def places_of(outs, rows):
        places = []
        for out in outs:
            places.append((out, heights.get(out, 0)))
            heights[out] = heights.get(out, 0) + rows
        return places

    plan = {"sums": [], "moves": []}
    for step, near, skip, spans, outs in sums:
        rows = spans[0].rows
        plan["sums"].append(
            (step, place_of(near), skip, [static(s) for s in spans], places_of(outs, rows))
        )
    for span, outs in moves:
        plan["moves"].append((static(span), places_of(outs, span.rows)))
    plan["ins"] = len(ins) - 1
    order = sorted(heights)
    number = {out: i for i, out in enumerate(order)}
    for kind in ("sums", "moves"):
        plan[kind] = [
            (*item[:-1], [(number[out], start) for out, start in item[-1]]) for item in plan[kind]
        ]
    cols = ins[1].shape[1]
    shapes = [shape(heights[out], cols, BF16) for out in order]
    body = functools.partial(turn_body, plan)
    made = kernel_call(body, shapes, ins, 1, after=after)
    places = [
        {order[out]: start for out, start in item[-1]} for kind in ("sums", "moves") for item in plan[kind]
    ]
    return dict(zip(order, made, strict=True)), places


def chunk_sum(flags, sums, after):
    made, places = turn(flags, sums, [], after)
    return made["z"]


def grad_body(left_ref, right_ref, out_ref):
    out_ref[...] = dot(left_ref[...], right_ref[...], ROWS).astype(BF16)


def grad_of(left, right, after, cost=LIGHT):
    outs = [shape(left.shape[1], right.shape[1], BF16)]
    return kernel_call(grad_body, outs, [left, right], after=after, cost=cost)[0]


def add_body(left_ref, right_ref, out_ref):
    out_ref[...] = left_ref[...] + right_ref[...]


def add(left, right, after):
    return kernel_call(add_body, [shape(*left.shape, left.dtype)], [left, right], after=after)[0]


def expand_output_body(normed_ref, hidden_ref, attended_ref, branch_ref, out_ref):
    rows = normed_ref.shape[1]
    out_ref[:rows, :] = dot(normed_ref[...], hidden_ref[...], ROWS).astype(BF16)
    out_ref[rows:, :] = dot(attended_ref[...], branch_ref[...], ROWS).astype(BF16)


def expand_output_grad(normed, hidden_grad, attended, branch_grad, after, cost=LIGHT):
    rows = normed.shape[1] + attended.shape[1]
    outs = [shape(rows, normed.shape[1], BF16)]
    ins = [normed, hidden_grad, attended, branch_grad]
    return kernel_call(expand_output_body, outs, ins, after=after, cost=cost)[0]


def join_body(heights, flags, first_ref, second_ref, out_ref):
    start = low = 0
    for height in heights:
        for ref, side in ((first_ref, flags[FLAG_HALF]), (second_ref, 1 - flags[FLAG_HALF])):
            at = pl.multiple_of(low + side * height, height)
            out_ref[pl.ds(at, height), :] = ref[start : start + height, :]
        start += height
        low += 2 * height
    rest = out_ref.shape[0] - low
    if rest:
        out_ref[low:, :] = first_ref[start : start + rest, :]


def join(flags, first, second, heights, after):
    rows = first.shape[0] + sum(heights)
    outs = [shape(rows, first.shape[1], BF16)]
    body = functools.partial(join_body, heights)
    return kernel_call(body, outs, [flags, first, second], 1, after=after)[0]


def join_ring_body(flags, *refs):
    pieces, out_ref = refs[:-1], refs[-1]
    rows = pieces[0].shape[0]
    for r, piece in enumerate(pieces):
        at = pl.multiple_of(((flags[FLAG_RING] + 4 - r) & 3) * rows, rows)
        out_ref[pl.ds(at, rows), :] = piece[...]


def join_ring(flags, pieces, after):
    rows, cols = pieces[0].shape
    outs = [shape(4 * rows, cols, BF16)]
    return kernel_call(join_ring_body, outs, [flags, *pieces], 1, after=after)[0]


def lay_body(groups, r, start, flags, *refs):
    size = len(groups)
    chunks, refs = refs[:2], refs[2:]
    outs, (held, sems) = refs[-2 * size - 2 : -2], refs[-2:]
    rows = held.shape[1]
    spot = (flags[FLAG_RING] + 4 - r) & 3
    waits = []
    for side in range(2):
        slot, sem = held.at[side], sems.at[side]
        slot[...] = chunks[side][start : start + rows, :].astype(F32)
        stream = flags[FLAG_LO] ^ side
        for p in range(4):
            for g, (low, high) in enumerate(groups):
                first, last = max(p * rows, low), min((p + 1) * rows, high)
                if first >= last:
                    continue
                piece = slot.at[pl.ds(first - p * rows, last - first)]
                place = pl.ds(first - low, last - first)
                for s in range(2):
                    copy = pltpu.make_async_copy(piece, outs[s * size + g].at[place], sem)
                    pl.when((spot == p) & (stream == s))(copy.start)
        waits.append(pltpu.make_async_copy(slot, outs[0].at[pl.ds(0, rows)], sem))
    for copy in waits:
        copy.wait()


def lay(flags, r, mine, theirs, start, rows, groups, laid, after, cost):
    cols = mine.shape[1]
    outs = [shape(high - low, cols, F32) for low, high in groups] * 2
    ins = [flags, mine, theirs]
    first = len(ins)
    body = functools.partial(lay_body, groups, r, start)
    laid = [] if laid is None else list(laid)

    def whole(*refs):
        body(*refs[:first], *refs[first + len(laid) + len(after) :])

    return pl.pallas_call(
        whole,
        out_shape=outs,
        in_specs=[IN_SMEM, IN_VMEM, IN_VMEM] + [IN_ANY] * (len(laid) + len(after)),
        out_specs=[IN_ANY] * len(outs),
        scratch_shapes=[pltpu.VMEM((2, rows, cols), F32), pltpu.SemaphoreType.DMA((2,))],
        input_output_aliases={first + i: i for i in range(len(laid))},
        compiler_params=pltpu.CompilerParams(vmem_limit_bytes=VMEM_LIMIT),
        cost_estimate=pl.CostEstimate(
            flops=int(FLOPS_US * cost), bytes_accessed=1000, transcendentals=0
        ),
    )(*ins, *laid, *after)


def sort_body(flags, *refs):
    parts, outs, sems = refs[:4], refs[4:8], refs[8]
    rows = outs[0].shape[1]
    copies = []
    for k in range(4):
        stream = flags[FLAG_C] ^ (k & 1)
        page = flags[FLAG_X] ^ (k >> 1)
        for n in range(2):
            piece = parts[k].at[pl.ds(n * rows, rows)]
            sem = sems.at[2 * k + n]

            def move(out, piece=piece, page=page, sem=sem):
                pltpu.make_async_copy(piece, out.at[page], sem).start()

            each(
                stream,
                functools.partial(move, outs[2 * n]),
                functools.partial(move, outs[2 * n + 1]),
            )
            copies.append(pltpu.make_async_copy(piece, outs[0].at[0], sem))
    for copy in copies:
        copy.wait()


def sort_rows(flags, parts, after=()):
    rows, cols = parts[0].shape
    outs = [jax.ShapeDtypeStruct((2, rows // 2, cols), BF16)] * 4
    scratch = [pltpu.SemaphoreType.DMA((8,))]
    return kernel_call(sort_body, outs, [flags, *parts], 1, scratch, after, far_ins=4, far_outs=4)


def slope_of(w_ref, wide, h):
    rows = [w_ref[4 * wide + i : 4 * wide + i + 1, h : h + 1].astype(F32) for i in range(3)]
    return rows[0] + rows[1] + rows[2]


def attention_ahead_body(heads, block, first, normed_ref, w_ref, far_ref, *refs):
    branch_ref, refs = (None, refs) if first else (refs[0], refs[1:])
    kept, (out_ref, *held, sems) = refs[:3], refs[3:]
    qkv_ref, attended_ref, log_ref = held
    keep = [pltpu.make_async_copy(held[i], kept[i], sems.at[i]) for i in range(3)]
    tokens = normed_ref.shape[0]
    wide = heads * HEAD_DIM
    qkv_ref[...] = dot(normed_ref[...], w_ref[: 3 * wide, :], COLS).astype(BF16)
    log_ref[...] = jnp.zeros_like(log_ref)
    keep[0].start()
    for h in range(heads):
        col = slice(h * HEAD_DIM, (h + 1) * HEAD_DIM)
        keys = qkv_ref[:, wide + col.start : wide + col.stop]
        values_t = qkv_ref[:, 2 * wide + col.start : 2 * wide + col.stop].T
        slope = slope_of(w_ref, wide, h)
        for b in range(tokens // block):
            rows = slice(b * block, (b + 1) * block)
            scores = dot(keys, qkv_ref[rows, col], COLS) * SCALE - slope * far_ref[:, rows]
            highest = jnp.max(scores, axis=0, keepdims=True)
            exponent = jnp.exp(scores - highest)
            totals = jnp.sum(exponent, axis=0, keepdims=True)
            soft_weights = (exponent * (1.0 / totals)).astype(BF16)
            log_ref[h : h + 1, rows] = highest + jnp.log(totals)
            attended_ref[rows, col] = dot(values_t, soft_weights).T.astype(BF16)
    keep[1].start()
    keep[2].start()
    part = dot(attended_ref[...], w_ref[3 * wide : 4 * wide, :])
    out_ref[...] = part if first else branch_ref[...] + part
    for copy in keep:
        copy.wait()


def attention_ahead(heads, normed, w, far, branch, after=(), cost=LIGHT):
    rows, cols = normed.shape
    wide = heads * HEAD_DIM
    ins = [normed, w, far] + ([] if branch is None else [branch])
    outs = [shape(rows, 3 * wide, BF16), shape(rows, wide, BF16), shape(8, rows, F32)]
    scratch = [pltpu.VMEM(out.shape, out.dtype) for out in outs] + [pltpu.SemaphoreType.DMA((3,))]
    outs.append(shape(rows, cols, F32))
    body = functools.partial(attention_ahead_body, heads, min(256, rows), branch is None)
    return kernel_call(body, outs, ins, 0, scratch, after, hbm_outs=3, cost=cost)


def attention_behind_body(
    heads, block, first, branch_ref, normed_ref, w_ref, qkv_ref, log_ref, far_ref, *refs
):
    grad_ref = None if first else refs[0]
    weight_grad, out_slope, out_ref, out_qkv, attended_grad, keys_sum, values_sum = (
        refs if first else refs[1:]
    )
    tokens = branch_ref.shape[0]
    wide = heads * HEAD_DIM
    attended_grad[...] = dot(branch_ref[...], w_ref[3 * wide : 4 * wide, :], COLS).astype(BF16)
    for h in range(heads):
        col = slice(h * HEAD_DIM, (h + 1) * HEAD_DIM)
        key_col = slice(wide + col.start, wide + col.stop)
        value_col = slice(2 * wide + col.start, 2 * wide + col.stop)
        keys = qkv_ref[:, key_col]
        values = qkv_ref[:, value_col]
        keys_t = keys.T
        slope = slope_of(w_ref, wide, h)
        for b in range(tokens // block):
            rows = slice(b * block, (b + 1) * block)
            queries = qkv_ref[rows, col]
            grad = attended_grad[rows, col]
            far = far_ref[:, rows]
            scores = dot(keys, queries, COLS) * SCALE - slope * far
            probs = jnp.exp(scores - log_ref[h : h + 1, rows])
            values_part = dot(probs.astype(BF16), grad)
            probs_grad = dot(values, grad, COLS)
            mean = jnp.sum(probs * probs_grad, axis=0, keepdims=True)
            scores_grad = probs * (probs_grad - mean)
            out_slope[h : h + 1, rows] = jnp.sum(scores_grad * far, axis=0, keepdims=True)
            scores_grad = scores_grad.astype(BF16)
            keys_part = dot(scores_grad, queries)
            if b == 0:
                keys_sum[...] = keys_part
                values_sum[...] = values_part
            else:
                keys_sum[...] += keys_part
                values_sum[...] += values_part
            queries_grad = dot(keys_t, scores_grad) * SCALE
            out_qkv[rows, col] = queries_grad.T.astype(BF16)
        out_qkv[:, key_col] = (keys_sum[...] * SCALE).astype(BF16)
        out_qkv[:, value_col] = values_sum[...].astype(BF16)
    part = dot(out_qkv[...], w_ref[: 3 * wide, :])
    weight_grad[...] = dot(out_qkv[...], normed_ref[...], ROWS).astype(BF16)
    out_ref[...] = part if first else grad_ref[...] + part


def attention_behind(heads, branch_grad, normed, w, kept, far, grad, after=(), cost=LIGHT):
    rows, cols = branch_grad.shape
    wide = heads * HEAD_DIM
    ins = [branch_grad, normed, w, *kept, far] + ([] if grad is None else [grad])
    outs = [shape(3 * wide, cols, BF16), shape(8, rows, F32), shape(rows, cols, F32)]
    scratch = [pltpu.VMEM((rows, 3 * wide), BF16), pltpu.VMEM((rows, wide), BF16)] + [pltpu.VMEM((rows, HEAD_DIM), F32)] * 2
    body = functools.partial(attention_behind_body, heads, min(256, rows), grad is None)
    return kernel_call(body, outs, ins, 0, scratch, after, cost=cost)


def gelu_both(values):
    square = values * values
    bend = jnp.tanh(GELU_A * values * (1.0 + GELU_B * square))
    half = 0.5 * (1.0 + bend)
    slope = half + 0.5 * values * (1.0 - bend * bend) * (
        GELU_A + (3.0 * GELU_A * GELU_B) * square
    )
    return values * half, slope


def hidden_ahead_body(count, blocks, starts, normed_ref, *refs):
    weights, refs = refs[:count], refs[count:]
    parts, outs, held = refs[:blocks], refs[blocks:-1], refs[-1]
    tokens, cols = normed_ref.shape
    for k in range(blocks):
        rows = tokens // blocks
        outs[2 * count][k * rows : (k + 1) * rows, :] = parts[k][parts[k].shape[0] - rows :, :]
    step = 32
    for j in range(count):
        held[...] = dot(normed_ref[...], weights[j][starts[j] : starts[j] + cols, :])
        for b in range(tokens // step):
            rows = slice(b * step, (b + 1) * step)
            active, back = gelu_both(held[rows, :])
            outs[2 * j][rows, :] = active.astype(BF16)
            outs[2 * j + 1][rows, :] = back.astype(BF16)


def hidden_ahead(normed, weights, parts=(), after=(), cost=LIGHT):
    rows, cols = normed.shape
    arrays, starts = zip(*weights, strict=True)
    count, wide = len(weights), arrays[0].shape[1]
    outs = [shape(rows, wide, BF16)] * (2 * count)
    if parts:
        outs.append(shape(rows, cols, BF16))
    body = functools.partial(hidden_ahead_body, count, len(parts), starts)
    scratch = [pltpu.VMEM((rows, wide), F32)]
    out = kernel_call(body, outs, [normed, *arrays, *parts], 0, scratch, after, cost=cost)
    return out[0 : 2 * count : 2], out[1 : 2 * count : 2], out[-1]


def hidden_behind_body(count, first, starts, cot_ref, *refs):
    active, back, shrink, expand = (refs[count * i : count * (i + 1)] for i in range(4))
    refs = refs[4 * count :]
    before, refs = ((), refs) if first else (refs[:2], refs[2:])
    grads, (added_ref, out_ref) = refs[:count], refs[count:]
    cols, wide = cot_ref.shape[1], active[0].shape[1]
    for j in range(count):
        down = slice(starts[0][j], starts[0][j] + wide)
        up = slice(starts[1][j], starts[1][j] + cols)
        part = dot(active[j][...], shrink[j][down, :])
        if j == 0:
            added_ref[...] = part if first else before[0][...] + part
        else:
            added_ref[...] += part
        active_grad = dot(cot_ref[...], shrink[j][down, :], COLS)
        grads[j][...] = (active_grad * back[j][...].astype(F32)).astype(BF16)
        part = dot(grads[j][...], expand[j][up, :], COLS)
        if j == 0:
            out_ref[...] = part if first else before[1][...] + part
        else:
            out_ref[...] += part


def hidden_behind(cotangent, active, back, shrink, expand, before=(), after=(), cost=LIGHT):
    rows, cols = cotangent.shape
    count, wide = len(active), active[0].shape[1]
    downs, ups = zip(*shrink, strict=True), zip(*expand, strict=True)
    (downs, down_starts), (ups, up_starts) = downs, ups
    outs = [shape(rows, wide, BF16)] * count + [shape(rows, cols, F32)] * 2
    body = functools.partial(hidden_behind_body, count, not before, (down_starts, up_starts))
    ins = [cotangent, *active, *back, *downs, *ups, *before]
    out = kernel_call(body, outs, ins, after=after, cost=cost)
    return out[:count], out[count:]


class Links:
    def __init__(self, pairs):
        self.pairs = pairs
        self.high = pairs // 2
        self.ring_size = 4

    def send(self, value, move):
        table = []
        for dp in range(self.pairs):
            for tensor in range(4):
                hi, lo, x, c = move(dp // 2, dp % 2, tensor // 2, tensor % 2)
                table.append((dp * 4 + tensor, (hi * 2 + lo) * 4 + x * 2 + c))
        return lax.ppermute(value, AXES, table)

    def core(self, value):
        return self.send(value, lambda hi, lo, x, c: (hi, lo, x, 1 - c))

    def across(self, value):
        return self.send(value, lambda hi, lo, x, c: (hi, lo, 1 - x, c))

    def stream(self, value):
        return self.send(value, lambda hi, lo, x, c: (hi, 1 - lo, x, c))

    def level(self, value, bit):
        return self.send(value, lambda hi, lo, x, c: (hi ^ bit, lo, x, c))

    def ring(self, value):
        after = (1, 3, 0, 2)
        return self.send(value, lambda hi, lo, x, c: (hi // 4 * 4 + after[hi % 4], lo, x, c))

    def out_to_page(self, value, k):
        return self.send(value, lambda hi, lo, x, c: (hi, c ^ (k & 1), x ^ (k >> 1), lo))

    def back_to_rows(self, value, k):
        return self.send(value, lambda hi, lo, x, c: (hi, c, x ^ (k >> 1), lo ^ (k & 1)))


def add_low(a, b):
    return (a.astype(F32) + b.astype(F32)).astype(BF16)


class Clock:
    def __init__(self, start):
        self.now = start

    def passed(self, *values):
        values, self.now = lax.optimization_barrier((list(values), self.now))
        return values[0] if len(values) == 1 else values


def shards(
    text_input,
    visual_input,
    text_boxes,
    text_count,
    text_prenorm,
    text_query,
    text_key,
    text_value,
    text_output,
    text_midnorm,
    text_expand,
    text_shrink,
    visual_prenorm,
    visual_query,
    visual_key,
    visual_value,
    visual_output,
    visual_midnorm,
    visual_expand,
    visual_shrink,
    slopes,
    text_cotangent,
    visual_cotangent,
):
    dp_index = lax.axis_index("dp")
    tensor_index = lax.axis_index("tensor")
    hi, lo = dp_index // 2, dp_index % 2
    x, c = tensor_index // 2, tensor_index % 2
    links = Links(lax.axis_size("dp"))
    heads_slot = slopes.shape[0]
    half = hi % 2
    n = links.ring_size
    spot = (hi % n) ^ ((hi % n) >> 1)
    flags = jnp.stack([lo, x, c, half, spot, 2 * x + lo, tensor_index]).astype(jnp.int32)
    gain_first, gain_second = (
        jnp.where(lo == 0, text, visual).astype(F32)[None]
        for text, visual in ((text_prenorm, visual_prenorm), (text_midnorm, visual_midnorm))
    )

    def half_rows(shard):
        return lax.dynamic_slice_in_dim(shard, half * (shard.shape[0] // 2), shard.shape[0] // 2)

    def page_blocks(text_rows, visual_rows):
        blocks = []
        for k in range(4):
            parts = [
                lax.dynamic_index_in_dim(rows, x ^ (k >> 1), 0, False)
                for rows in (text_rows, visual_rows)
            ]
            blocks.append(jnp.where((c ^ (k & 1)) == 0, *parts))
        return blocks

    def to_page(blocks, chosen=(3, 2, 1, 0)):
        return [links.out_to_page(blocks[k], k) for k in chosen][::-1]

    def low(value):
        return value.astype(BF16)

    def add_low(a, b):
        return low(a.astype(F32) + b.astype(F32))

    clock = Clock(slopes)
    passed = clock.passed

    text_attn = [text_query.T, text_key.T, text_value.T, text_output]
    visual_attn = [visual_query.T, visual_key.T, visual_value.T, visual_output]
    slope_parts = []
    rest = slopes
    for i in range(3):
        slope_parts.append(low(rest))
        rest = rest - slope_parts[i].astype(F32)
    wide, width = text_output.shape
    tail = jnp.zeros((16, width), BF16).at[:3, :heads_slot].set(jnp.stack(slope_parts))
    heights = [2 * wide]
    attn_own = jnp.concatenate(
        [
            jnp.where(
                lo == 0,
                jnp.concatenate([text_query.T, text_key.T, text_value.T, text_output]),
                jnp.concatenate([visual_query.T, visual_key.T, visual_value.T, visual_output]),
            ),
            tail,
        ]
    )

    attn_half = passed(jnp.concatenate([half_rows(attn_own[: 4 * wide]), tail]))
    attn_first = links.across(attn_half)
    text_rows, visual_rows = passed(text_input, visual_input)
    in_blocks = page_blocks(text_rows, visual_rows)
    cot_parts = page_blocks(text_cotangent, visual_cotangent)
    in_blocks = [
        jnp.concatenate([in_blocks[k], cot_parts[k]]) if k < 2 else in_blocks[k] for k in range(4)
    ]
    in_blocks = to_page(passed(in_blocks))
    info = passed(page_info(flags, text_count, text_boxes, [clock.now]))
    info_theirs = links.stream(info)
    expand_own = jnp.where(lo == 0, text_expand, visual_expand)
    shrink_own = jnp.where(lo == 0, text_shrink, visual_shrink)
    expand_half = half_rows(expand_own)
    info_theirs = passed(info_theirs)
    far = passed(distances(flags, info, info_theirs, [clock.now]))
    expand_half, cot_parts, gain_first, gain_second = passed(
        expand_half, cot_parts, gain_first, gain_second
    )
    attn_first = passed(attn_first)
    attn_second = links.level(attn_first, 1)
    in_blocks = passed(in_blocks)
    attn_own, expand_half, cot_parts = passed(attn_own, expand_half, cot_parts)
    attn_core = links.core(attn_own)
    expand_first = links.across(expand_half)
    expand_core = links.core(expand_own)
    source, first_normed = passed(*first_norm(gain_first, in_blocks, text_input.shape[1], [clock.now]))

    saved = [None] * 4

    def ahead(j, weights, branch, cost=LIGHT):
        qkv, attended, log_total, branch = attention_ahead(
            heads_slot, first_normed, weights, far, branch, [clock.now], cost
        )
        saved[j] = (qkv, log_total, attended)
        return passed(branch)

    branch = ahead(0, attn_own, None)
    attn_core = passed(attn_core)
    branch = ahead(1, attn_core, branch)
    quarter = shrink_own.shape[0] // 4
    shrink_part = passed(lax.dynamic_slice_in_dim(shrink_own, spot * quarter, quarter))
    attn_second = passed(attn_second)
    expand_first, expand_core = passed(expand_first, expand_core)
    attn_other = passed(join(flags, attn_first, attn_second, heights, [clock.now]))

    expand_second = links.level(expand_first, 1)
    attn_last = links.core(attn_other)
    cot_parts, shrink_part = passed(cot_parts, shrink_part)
    shrink_parts = [links.across(shrink_part)]
    cot_far = to_page(cot_parts, (3, 2))
    branch = ahead(2, attn_other, branch, HEAVY)
    attn_last = passed(attn_last)
    branch = ahead(3, attn_last, branch)
    attn_slots = [attn_own, attn_core, attn_other, attn_last]
    expand_second = passed(expand_second)
    shrink_parts[0] = passed(shrink_parts[0])
    cot_far = passed(cot_far)
    expand_other = passed(join(flags, expand_first, expand_second, [width // 2], [clock.now]))

    shrink_own = passed(shrink_own)
    expand_last = links.core(expand_other)
    shrink_parts.append(links.ring(shrink_parts[0]))
    shrink_core = links.core(shrink_own)
    middle, second_normed = second_norm(source, branch, gain_second, [clock.now])
    second_normed = passed(second_normed)
    active, back = [], []
    for j in range(4):
        weights = (expand_own, expand_core, expand_other, expand_last)[j]
        some, other, joined = hidden_ahead(
            second_normed,
            [(weights, 0)],
            [*in_blocks[:2], *cot_far] if j == 0 else [],
            [clock.now],
            HEAVY if j == 0 else LIGHT,
        )
        active += [passed(some[0])]
        back += other
        if j == 0:
            cotangent = passed(joined)
        if j == 1:
            expand_last = passed(expand_last)
    expand_slots = [(w, 0) for w in (expand_own, expand_core, expand_other, expand_last)]
    parts, parts_core = {}, {}
    for j in (3, 1):
        parts[j] = passed(grad_of(active[j], cotangent, [clock.now]))
    shrink_parts[1], shrink_core = passed(shrink_parts[1], shrink_core)
    for j in (3, 1):
        parts_core[j] = links.core(parts[j])
    shrink_parts.append(links.ring(shrink_parts[1]))
    shrink_slots = [(shrink_own, 0), (shrink_core, 0)]
    for j, cost in ((2, HEAVY), (0, LIGHT)):
        parts[j] = passed(grad_of(active[j], cotangent, [clock.now], cost))
    parts_core = passed(parts_core)

    class Wave:
        def __init__(self, rows, groups, cuts=None):
            self.rows, self.groups = rows, groups
            self.cuts = [i * rows for i in range(5)] if cuts is None else cuts
            self.added = self.came = 0
            self.moved, self.laid = None, None
            self.crossed, self.chunks = [], []

        def far(self, own, core):
            self.pieces = passed(list(far_sum(flags, own, core, self.cuts, [clock.now])))

        def near(self, own, core):
            self.kept = passed(near_sum(own, core, [clock.now]))

        def parts(self, step):
            found = []
            for k, (low, high) in enumerate(zip(self.cuts, self.cuts[1:])):
                first, last = max(low, step * self.rows), min(high, (step + 1) * self.rows)
                if first < last:
                    found.append((k, first, last))
            return found

        def sums(self, outs):
            step, found = self.added, []
            for k, first, last in self.parts(step):
                piece, skip = self.crossed[k], first - step * self.rows
                spans = [Span(piece.array, piece.start + first - self.cuts[k], last - first)]
                if self.moved is not None:
                    spans.append(Span(self.moved.array, self.moved.start + skip, last - first))
                found.append((step, self.kept, skip, spans, outs))
            return found

        def lay(self, *chunks, cost=LIGHT):
            for k in chunks:
                mine, theirs, start = self.chunks[k]
                self.laid = lay(
                    flags,
                    k,
                    mine,
                    theirs.array,
                    start,
                    self.rows,
                    self.groups,
                    self.laid,
                    [clock.now],
                    cost,
                )
                self.laid = passed(list(self.laid))

    tall = text_shrink.shape[0]
    shrink = Wave(tall // 4, [(0, tall)], [i * tall // 48 for i in (0, 12, 28, 42, 48)])
    expand = Wave((width + wide) // 4, [(0, width), (width, width + wide)])
    attn = Wave(3 * wide // 4, [(i * wide, (i + 1) * wide) for i in range(3)])
    groups = links.high // n

    def cross(*waves):
        for wave in waves:
            piece = wave.pieces[len(wave.crossed)]
            wave.crossed.append(Span(links.across(piece), 0, piece.shape[0]))

    def spin(*waves, crossing=()):
        sums, moves, users = [], [], []
        for wave in waves:
            step = wave.added
            if step < n:
                last = step == n - 1
                if last and groups > 1:
                    table = [
                        [(g * n + r) * 2 + l for g in range(groups)]
                        for r in range(n)
                        for l in range(2)
                    ]
                    total = chunk_sum(flags, wave.sums(["z"]), [clock.now])
                    total = passed(lax.psum(total, "dp", axis_index_groups=table))
                    moves.append((Span(total, 0, wave.rows), ["z", "y"]))
                    users.append(("move", wave, wave.rows))
                else:
                    found = wave.sums(["z", "y"] if last else ["z"])
                    sums += found
                    users += [("sum", wave if i == 0 else None, wave.rows) for i in range(len(found))]
                wave.added += 1
            else:
                outs = ["z", "y"] if len(wave.chunks) < n - 1 else ["y"]
                moves.append((wave.moved, outs))
                users.append(("move", wave, wave.rows))
        pending = {}
        for wave in crossing:
            k = len(wave.crossed) + pending.get(id(wave), 0)
            pending[id(wave)] = pending.get(id(wave), 0) + 1
            rows = wave.pieces[k].shape[0]
            moves.append((Span(wave.pieces[k], 0, rows), ["x"]))
            users.append(("move", wave, rows))
        users = [u for u in users if u[0] == "sum"] + [u for u in users if u[0] == "move"]
        made, places = turn(flags, sums, moves, [clock.now])
        names = sorted(made)
        made = dict(zip(names, passed([made[name] for name in names]), strict=True))
        sent = {}
        if "z" in made:
            sent["z"] = links.ring(made["z"])
        if "y" in made:
            sent["y"] = links.stream(made["y"])
        if "x" in made:
            sent["x"] = links.across(made["x"])
        for (kind, wave, rows), place in zip(users, places, strict=True):
            if wave is None:
                continue
            if "x" in place:
                wave.crossed.append(Span(sent["x"], place["x"], rows))
            if "z" in place:
                wave.moved = Span(sent["z"], place["z"], wave.rows)
            if "y" in place:
                wave.chunks.append(
                    [made["y"], Span(sent["y"], place["y"], wave.rows), place["y"]]
                )

    def settle(spans):
        arrays = {id(s.array): s.array for s in spans}
        keys = list(arrays)
        fresh = dict(zip(keys, passed([arrays[k] for k in keys], [])[0], strict=True))
        for s in {id(s): s for s in spans}.values():
            s.array = fresh[id(s.array)]

    def arrive(*waves):
        spans = []
        for wave in waves:
            if wave.added < n:
                spans += [wave.crossed[k] for k, first, last in wave.parts(wave.added)]
            spans += [] if wave.moved is None else [wave.moved]
        settle(spans)

    def landed(wave, *chunks):
        settle([wave.chunks[k][1] for k in chunks])
        wave.lay(*chunks)

    shrink.far(parts[2], parts_core[3])
    shrink.near(parts[0], parts_core[1])
    shrink_parts[2] = passed(shrink_parts[2])
    cross(shrink)
    shrink_parts.append(links.ring(shrink_parts[2]))
    grads, sums = hidden_behind(
        cotangent,
        active[:2],
        back[:2],
        shrink_slots,
        expand_slots[:2],
        after=[clock.now],
        cost=HEAVY,
    )
    grads, sums = passed(grads, list(sums))
    arrive(shrink)
    shrink_parts[3] = passed(shrink_parts[3])
    shrink_other = passed(join_ring(flags, shrink_parts, [clock.now]))
    shrink_last = links.core(shrink_other)
    spin(shrink, crossing=(shrink,))
    shrink_last = passed(shrink_last)
    shrink_slots += [(shrink_other, 0), (shrink_last, 0)]
    grads_far, (added, second_grad) = hidden_behind(
        cotangent,
        active[2:],
        back[2:],
        shrink_slots[2:],
        expand_slots[2:],
        sums,
        [clock.now],
        HEAVY,
    )
    hidden_grad = [*grads, *passed(grads_far)]
    middle_grad, branch_grad, midnorm_grad, result = second_back(
        middle, gain_second, second_grad, cotangent, added, [clock.now]
    )
    branch_grad = passed(branch_grad)

    def expand_part(j, cost=LIGHT):
        return passed(
            expand_output_grad(
                second_normed, hidden_grad[j], saved[j][2], branch_grad, [clock.now], cost
            )
        )

    parts = {j: expand_part(j) for j in (3, 2)}
    arrive(shrink)
    spin(shrink, crossing=(shrink,))
    parts_core = links.core(parts[3])
    parts.update({1: expand_part(1, HEAVY), 0: expand_part(0)})
    parts_core = passed(parts_core)
    arrive(shrink)
    expand.far(parts[2], parts_core)
    spin(shrink, crossing=(shrink, expand))

    def under_way(wave, *chunks):
        settle([wave.chunks[k][1] for k in chunks])

    slope_rows = [None] * 4
    first_grad = None
    for step, j in enumerate((3, 2, 1, 0)):
        if step == 0:
            parts_core = links.core(parts[1])
        elif step == 1:
            spin(shrink, expand, crossing=(expand,))
            part_core = links.core(part)
        elif step == 2:
            attn.far(part, part_core)
            spin(shrink, expand, crossing=(expand, attn))
        else:
            spin(shrink, expand, crossing=(expand, attn))
            part_core = links.core(part)
        part, slope_rows[j], first_grad = attention_behind(
            heads_slot,
            branch_grad,
            first_normed,
            attn_slots[j],
            saved[j][:2],
            far,
            first_grad,
            [clock.now],
            HEAVY,
        )
        first_grad, part = passed(first_grad, part)
        if step == 0:
            expand.near(parts[0], passed(parts_core))
        elif step == 1:
            part_core = passed(part_core)
        elif step == 3:
            rows_out, small = first_back(
                heads_slot,
                flags,
                source,
                gain_first,
                first_grad,
                middle_grad,
                midnorm_grad,
                result,
                slope_rows,
                [clock.now],
            )
            small, rows_out = passed(small, list(rows_out))
            attn.near(part, passed(part_core))
        arrive(*((shrink, expand) if step < 3 else (shrink, expand, attn)))
        if step == 2:
            under_way(shrink, 0)
        if step == 3:
            under_way(shrink, 1, 2)

    rows_back = [None] * 4

    def hop(value, moved):
        return passed(add(value, moved, [clock.now]))

    def send_back(k):
        rows_back[k] = links.back_to_rows(rows_out[k], k)

    def sent_back(k):
        rows_back[k] = passed(rows_back[k])

    spin(shrink, expand, attn, crossing=(attn, attn))
    small_moved = links.core(small)
    shrink.lay(0)
    shrink.lay(1)
    shrink.lay(2)
    arrive(expand, attn)
    small = hop(small, passed(small_moved))

    spin(expand, attn)
    small_moved = links.across(small)
    arrive(expand, attn)
    under_way(shrink, 3)
    under_way(expand, 1)
    small = hop(small, passed(small_moved))

    spin(expand, attn)
    small_moved = links.level(small, 1)
    send_back(0)
    send_back(2)
    shrink.lay(3)
    expand.lay(0)
    expand.lay(1)
    arrive(expand, attn)
    under_way(expand, 2)
    small = hop(small, passed(small_moved))
    bit = 4
    while bit < links.high:
        small = hop(small, passed(links.level(small, bit)))
        bit *= 2

    spin(expand, attn)
    small_moved = links.level(small, 2)
    expand.lay(2)
    arrive(attn)
    sent_back(0)
    sent_back(2)
    small = hop(small, passed(small_moved))

    spin(attn)
    small_other = links.stream(small)
    send_back(3)
    arrive(attn)
    under_way(expand, 3)

    spin(attn)
    send_back(1)
    expand.lay(3)
    attn.lay(0)
    small_other = passed(small_other)
    text_small = jnp.where(lo == 0, small, small_other)
    visual_small = jnp.where(lo == 0, small_other, small)
    slope_sum = lax.dynamic_slice(
        (text_small + visual_small)[2], (tensor_index * heads_slot,), (heads_slot,)
    )
    text_small, visual_small, slope_sum = passed(text_small, visual_small, slope_sum)
    arrive(attn)
    sent_back(3)

    spin(attn)
    under_way(attn, 1)
    attn.lay(1, cost=HEAVY)
    sent_back(1)
    text_result, visual_result, text_input_grad, visual_input_grad = passed(
        *sort_rows(flags, rows_back, [clock.now])
    )
    landed(attn, 2)
    landed(attn, 3)

    text_sh, visual_sh = shrink.laid
    text_ex, text_out, visual_ex, visual_out = expand.laid
    text_at, visual_at = attn.laid[:3], attn.laid[3:]
    return (
        text_result,
        visual_result,
        text_input_grad,
        visual_input_grad,
        text_small[0],
        *(grad.T for grad in text_at),
        text_out,
        text_small[1],
        text_ex,
        text_sh,
        visual_small[0],
        *(grad.T for grad in visual_at),
        visual_out,
        visual_small[1],
        visual_ex,
        visual_sh,
        slope_sum,
    )


def solution(mesh):
    rows = P("dp", "tensor", None)
    split_out = P(None, "tensor")
    split_in = P("tensor", None)
    weights = (P(), split_out, split_out, split_out, split_in, P(), split_out, split_in)
    return jax.shard_map(
        shards,
        mesh=mesh,
        in_specs=(
            rows,
            rows,
            P("dp", None, None),
            P("dp"),
            *weights,
            *weights,
            P("tensor"),
            rows,
            rows,
        ),
        out_specs=(rows, rows, rows, rows, *weights, *weights, P("tensor")),
        check_vma=False,
    )
```
